128 devices in a mesh: patch: 32 (over y, x, z_hi), tp: 4 (over z_lo, core).
Axes of the slice: x: 4, y: 4, z: 4 (z_hi: 2, z_lo: 2; z = z_hi * 2 + z_lo), core: 2. Of those that a mesh axis runs over, the one named last changes fastest.
Arguments:
- hidden: bfloat16 [2, 4608, 5120], P(None, 'patch', 'tp'), may hold values from -6 to 6
- mod_shift: float32 [2, 5120], replicated, may hold values from -3 to 3
- mod_scale: float32 [2, 5120], replicated, may hold values from -3 to 3
- w_query: bfloat16 [5120, 2560], P(None, 'tp'), may hold values from -4 to 4
- w_key: bfloat16 [5120, 2560], P(None, 'tp'), may hold values from -4 to 4
- w_value: bfloat16 [5120, 2560], P(None, 'tp'), may hold values from -0.078125 to 0.078125
- q_gain: float32 [2560], P('tp'), may hold values from 1 to 4
- k_gain: float32 [2560], P('tp'), may hold values from 0.5 to 1.5
- token_place: int32 [4608], P('patch'), may hold values from 0 to 4607, each once
- stale_keys: bfloat16 [2, 4608, 2560], P(None, 'patch', 'tp'), may hold values from -160 to 160
- stale_values: bfloat16 [2, 4608, 2560], P(None, 'patch', 'tp'), may hold values from -6 to 6
Outputs:
- attended: bfloat16 [2, 4608, 2560], P(None, 'patch', 'tp')
- fresh_keys: bfloat16 [2, 4608, 2560], P(None, 'patch', 'tp')
- fresh_values: bfloat16 [2, 4608, 2560], P(None, 'patch', 'tp')
The draws below stay inside these ranges and needn't reach their ends.
Inputs may be any that keep to these rules, and one draw needn't show every extreme that they name: `token_place`: each slot holds a different grid token.
All inputs are finite; a program needn't handle non-finite values.
Results may differ from the reference program's by a relative error of at most 0.015.
The reference program's roundings to bfloat16 on the way count: a program that leaves them out, or rounds other values in their place, can miss the bound.
Values may be sent and summed in bfloat16 or wider, within the bound.
No kernel may reach another device: no remote copies, remote signals or barrier semaphores. Data moves between devices by JAX's collectives and lax.ppermute only.
A program may use at most 192 MiB of HBM per device.

```python
import math
import jax
import jax.numpy as jnp
from jax import lax

B = 2
TOK_DEV = 144
D = 5120
HEADS = 20
HD = 128
FRAMES = 3
GRID_W = 48
TOKENS = 4608
N_PATCH = 32


def rise_columns(entries, col_key, top_spread):
    cols = entries.shape[1]
    spread = jnp.exp(jax.random.uniform(col_key, (cols,), jnp.float32) * jnp.log(top_spread))
    trend = jnp.exp(jnp.arange(cols, dtype=jnp.float32) * (jnp.log(3.0) / max(cols - 1, 1)))
    return (entries * (spread * trend / 6.0)[None, :] * D ** (-0.5)).astype(jnp.bfloat16)


def draw_w_query(key, part):
    key = jax.random.fold_in(key, 11)
    entry_key, col_key = jax.random.split(key)
    entries = jax.random.truncated_normal(entry_key, -4.0, 4.0, (D, HEADS * HD), jnp.float32)
    return rise_columns(entries, col_key, 10.0)


def draw_w_key(key, part):
    key = jax.random.fold_in(key, 17)
    entry_key, col_key = jax.random.split(key)
    entries = jax.random.truncated_normal(entry_key, -4.0, 4.0, (D, HEADS * HD), jnp.float32)
    return rise_columns(entries, col_key, 10.0)


def draw_stale_keys(key, part):
    key = jax.random.fold_in(key, 23)
    entry_key = jax.random.fold_in(key, 0)
    entries = jax.random.truncated_normal(entry_key, -4.0, 4.0, (B, TOKENS, HEADS, HD), jnp.float32)
    return entries.reshape(B, TOKENS, HEADS * HD).astype(jnp.bfloat16)


def block_scale(rng, extent, cuts, least, high):
    def one(dim, blocks):
        heights = jax.random.uniform(jax.random.fold_in(jax.random.fold_in(rng, 6), dim), (blocks,), jnp.float32, least / len(cuts), high / len(cuts))
        return jnp.repeat(jnp.exp(heights), extent[dim] // blocks).reshape((-1,) + (1,) * (len(extent) - dim - 1))

    level = one(*cuts[0])
    for cut in cuts[1:]:
        level = level * one(*cut)
    return level


def noise(own_key, shape, scale, bound, cuts=(), held_as=jnp.bfloat16):
    result = scale * jax.random.normal(own_key, shape, jnp.float32)
    if cuts:
        result = result * block_scale(own_key, shape, cuts, -0.22, 0.18)
    return jnp.clip(result, -bound, bound).astype(held_as)


def setup_inputs(seed: int = 0) -> dict:
    splits = jax.random.split(jax.random.key(seed), 12)
    return {
        "hidden": noise(splits[0], (B, TOKENS, D), 1.0, 6.0, ((1, 32), (2, 4))),
        "mod_shift": noise(splits[1], (2, D), 0.5, 3.0, (), jnp.float32),
        "mod_scale": noise(splits[2], (2, D), 0.25, 3.0, (), jnp.float32),
        "w_query": draw_w_query(jax.random.fold_in(splits[11], 71), 0),
        "w_key": draw_w_key(jax.random.fold_in(splits[11], 71), 0),
        "w_value": noise(splits[5], (D, HEADS * HD), D ** -0.5, 0.078125, ((1, 4),)),
        "q_gain": jnp.clip(jnp.exp(math.log(4.0) - 1.3862944 * jax.random.uniform(splits[6], (HEADS * HD,), jnp.float32) ** block_scale(splits[6], (HEADS * HD,), ((0, 4),), -0.2, 0.2)), 1.0, 4.0),
        "k_gain": jnp.clip(1.0 + 0.1 * jax.random.normal(splits[7], (HEADS * HD,), jnp.float32), 0.5, 1.5),
        "token_place": jax.random.permutation(splits[8], TOKENS).astype(jnp.int32),
        "stale_keys": draw_stale_keys(jax.random.fold_in(splits[11], 71), 0),
        "stale_values": noise(splits[10], (B, TOKENS, HEADS * HD), 1.0, 6.0, ((1, 32), (2, 4))),
    }


masked_score = -1e+30
epsilon = 1e-06

def pair_angles(place, frame_tok, head_dim):
    half_dim = head_dim // 2
    third_dim = half_dim // 3
    frame_pairs = half_dim - 2 * third_dim
    frame_id = (place // frame_tok).astype(jnp.float32)
    within = place % frame_tok
    grid_row = (within // GRID_W).astype(jnp.float32)
    grid_col = (within % GRID_W).astype(jnp.float32)
    pair_idx = jnp.arange(half_dim)
    in_frame = pair_idx < frame_pairs
    in_row = (pair_idx >= frame_pairs) & (pair_idx < frame_pairs + third_dim)
    offset_pair = jnp.where(in_frame, pair_idx, jnp.where(in_row, pair_idx - frame_pairs, pair_idx - frame_pairs - third_dim)).astype(jnp.float32)
    part_width = jnp.where(in_frame, 2 * frame_pairs, 2 * third_dim).astype(jnp.float32)
    frequency = jnp.exp(-math.log(10000.0) * 2.0 * offset_pair / part_width)
    position = jnp.where(in_frame[None, :], frame_id[:, None], jnp.where(in_row[None, :], grid_row[:, None], grid_col[:, None]))
    return position * frequency[None, :]

def rope_tables(place, frame_tok, heads_count):
    angles = pair_angles(place, frame_tok, HD)
    cos_full = jnp.tile(jnp.repeat(jnp.cos(angles), 2, axis=1), (1, heads_count))
    sin_full = jnp.tile(jnp.repeat(jnp.sin(angles), 2, axis=1), (1, heads_count))
    return (cos_full, sin_full)

def rope_rotate(values, cos_full, sin_full):
    cols = values.shape[-1]
    even_slot = jnp.arange(cols) % 2 == 0
    next_entry = jnp.roll(values, -1, axis=-1)
    prev_entry = jnp.roll(values, 1, axis=-1)
    swapped = jnp.where(even_slot, -next_entry, prev_entry)
    return values * cos_full + swapped * sin_full

def reference(hidden, mod_shift, mod_scale, w_query, w_key, w_value, q_gain, k_gain, token_place, stale_keys, stale_values):
    frame_tok = TOKENS // FRAMES
    frame_id = token_place // frame_tok
    clean_rows = (frame_id == 0) | (frame_id == FRAMES - 1)
    whole = hidden.astype(jnp.float32)
    row_mean = lax.optimization_barrier(jnp.mean(whole, axis=-1, keepdims=True))
    centered = whole - row_mean
    variance = lax.optimization_barrier(jnp.mean(centered * centered, axis=-1, keepdims=True))
    normed = centered * lax.rsqrt(variance + epsilon)
    bias_rows = jnp.where(clean_rows[:, None], mod_shift[1][None, :], mod_shift[0][None, :])
    gain_rows = jnp.where(clean_rows[:, None], mod_scale[1][None, :], mod_scale[0][None, :])
    modded = (normed * (1.0 + gain_rows) + bias_rows).astype(jnp.bfloat16)
    flat_rows = modded.reshape(B * TOKENS, D)
    queries = jnp.dot(flat_rows, w_query, preferred_element_type=jnp.float32)
    keys_new = jnp.dot(flat_rows, w_key, preferred_element_type=jnp.float32)
    values_new = jnp.dot(flat_rows, w_value, preferred_element_type=jnp.float32).astype(jnp.bfloat16)
    queries = queries * lax.rsqrt(lax.optimization_barrier(jnp.mean(queries * queries, axis=-1, keepdims=True)) + epsilon) * q_gain[None, :]
    keys_new = keys_new * lax.rsqrt(lax.optimization_barrier(jnp.mean(keys_new * keys_new, axis=-1, keepdims=True)) + epsilon) * k_gain[None, :]
    cos_full, sin_full = rope_tables(token_place, frame_tok, HEADS)
    queries = rope_rotate(queries.reshape(B, TOKENS, HEADS * HD), cos_full, sin_full).astype(jnp.bfloat16)
    keys_new = rope_rotate(keys_new.reshape(B, TOKENS, HEADS * HD), cos_full, sin_full).astype(jnp.bfloat16)
    values_new = values_new.reshape(B, TOKENS, HEADS * HD)
    inverse_sqrt_scale = 1.0 / math.sqrt(HD)
    owner_rows = jnp.arange(TOKENS) // TOK_DEV
    same_patch = owner_rows[None, :] == jnp.arange(N_PATCH)[:, None]

    def split_heads(array):
        return array.reshape(B, TOKENS, HEADS, HD).transpose(2, 0, 1, 3)

    def one_head(operands):
        head_q, head_k, head_v, earlier_key_rows, earlier_value_rows = operands
        query_block_rows = head_q.astype(jnp.float32).reshape(B, N_PATCH, TOK_DEV, HD)
        block_k = head_k.astype(jnp.float32).reshape(B, N_PATCH, TOK_DEV, HD)
        block_v = head_v.astype(jnp.float32).reshape(B, N_PATCH, TOK_DEV, HD)
        fresh_scores = jnp.einsum('bpqd,bpkd->bpqk', query_block_rows, block_k) * inverse_sqrt_scale
        outdated_score_matrix = jnp.einsum('wlxh,wch->wlxc', query_block_rows, earlier_key_rows.astype(jnp.float32)) * inverse_sqrt_scale
        outdated_score_matrix = jnp.where(same_patch[None, :, None, :], masked_score, outdated_score_matrix)
        row_top = jnp.maximum(lax.optimization_barrier(jnp.max(fresh_scores, axis=-1)), lax.optimization_barrier(jnp.max(outdated_score_matrix, axis=-1)))
        fresh_probs = jnp.exp(fresh_scores - row_top[..., None])
        stale_probs = jnp.exp(outdated_score_matrix - row_top[..., None])
        row_sum = lax.optimization_barrier(jnp.sum(fresh_probs, axis=-1)) + lax.optimization_barrier(jnp.sum(stale_probs, axis=-1))
        fresh_low = lax.optimization_barrier(fresh_probs.astype(jnp.bfloat16))
        outdated_lower_bound = lax.optimization_barrier(stale_probs.astype(jnp.bfloat16))
        output_total = jnp.einsum('bpqk,bpkd->bpqd', fresh_low.astype(jnp.float32), block_v)
        output_total = output_total + jnp.einsum('alci,aio->alco', outdated_lower_bound.astype(jnp.float32), earlier_value_rows.astype(jnp.float32))
        return (output_total / row_sum[..., None]).reshape(B, TOKENS, HD)
    per_head = lax.map(one_head, (split_heads(queries), split_heads(keys_new), split_heads(values_new), split_heads(stale_keys), split_heads(stale_values)))
    attended = per_head.transpose(1, 2, 0, 3).reshape(B, TOKENS, HEADS * HD).astype(jnp.bfloat16)
    return (attended, keys_new, values_new)
```

```python
import functools
import math

import jax
import jax.numpy as jnp
import numpy as np
from jax import lax
from jax.experimental import pallas as pl
from jax.experimental.pallas import tpu as pltpu
from jax.sharding import PartitionSpec as P

D = 5120
HEADS = 20
HD = 128
FRAMES = 3
GRID_W = 48
EPS = 1e-06
MASKED = -1e30
NY, NX, NZ = 4, 4, 2
TP = 4
N_PATCH = NY * NX * NZ
TOK = 144
B = 2
ROWS = B * TOK
LOCAL_HEADS = 5
WIDTH = LOCAL_HEADS * HD
CHUNK = D // TP
STAT_LANES = 384
PIECE = 5 * TOK
MSG_ROWS = 2 * TOK + 16
SCORE_SCALE = math.log2(math.e) / math.sqrt(HD)
F32 = jnp.float32
BF16 = jnp.bfloat16
AXES = ("patch", "tp")


def params(mib):
    return pltpu.CompilerParams(vmem_limit_bytes=mib * 1024 * 1024)


def vmem():
    return pl.BlockSpec(memory_space=pltpu.VMEM)


def smem():
    return pl.BlockSpec(memory_space=pltpu.SMEM)


def linear(u, v, z_hi, z_lo, core):
    y, x = (u, v) if core == 0 else (v, u)
    return ((y * NX + x) * NZ + z_hi) * TP + z_lo * 2 + core


def places():
    return [
        (u, v, h, l, c)
        for u in range(4)
        for v in range(4)
        for h in range(2)
        for l in range(2)
        for c in range(2)
    ]


def permute(value, move):
    return lax.ppermute(value, AXES, [(linear(*p), linear(*move(*p))) for p in places()])


def swap_pair(value):
    return permute(value, lambda u, v, h, l, c: (u, v ^ 1, h, l, c))


def swap_v(value):
    return permute(value, lambda u, v, h, l, c: (u, v ^ 3, h, l, c))


def swap_z_hi(value):
    return permute(value, lambda u, v, h, l, c: (u, v, 1 - h, l, c))


def swap_tp(value, z, core):
    return permute(value, lambda u, v, h, l, c: (u, v, h, l ^ z, c) if not core else swapped(u, v, h, l ^ z, c))


def swapped(u, v, h, l, c):
    return v, u, h, l, 1 - c


def exchange(value):
    groups = []
    for c in range(2):
        for l in range(2):
            for h in range(2):
                for pair in ((0, 1), (3, 2)):
                    groups.append([linear(u, v, h, l, c) for v in pair for u in range(4)])
    return lax.all_to_all(value, AXES, 0, 0, axis_index_groups=groups)


def frequencies():
    half_dim = HD // 2
    third_dim = half_dim // 3
    frame_pairs = half_dim - 2 * third_dim
    pair = np.arange(HD) // 2
    offset = np.where(
        pair < frame_pairs,
        pair,
        np.where(pair < frame_pairs + third_dim, pair - frame_pairs, pair - frame_pairs - third_dim),
    )
    width = np.where(pair < frame_pairs, 2 * frame_pairs, 2 * third_dim)
    return np.exp(-math.log(10000.0) * 2.0 * offset / width).astype(np.float32).reshape(1, HD)


def columns_to_rows(first, second):
    lane = lax.broadcasted_iota(jnp.int32, (ROWS, 128), 1)
    both = jnp.where(lane == 0, first, jnp.where(lane == 1, second, 0.0))
    padded = jnp.concatenate([both, jnp.zeros((STAT_LANES - ROWS, 128), F32)], axis=0)
    return padded.T[0:8]


def row_to_column(row):
    return jnp.broadcast_to(row, (128, STAT_LANES)).T[0:ROWS]


def stats_kernel(hidden_ref, out_ref):
    part = hidden_ref[...].astype(F32)
    mean = jnp.sum(part, axis=1, keepdims=True) * (1.0 / CHUNK)
    centered = part - mean
    deviation = jnp.sum(centered * centered, axis=1, keepdims=True)
    out_ref[...] = columns_to_rows(mean, deviation)


def row_stats(hidden_rows):
    return pl.pallas_call(
        stats_kernel,
        out_shape=jax.ShapeDtypeStruct((8, STAT_LANES), F32),
        in_specs=[vmem()],
        out_specs=vmem(),
        compiler_params=params(16),
        cost_estimate=pl.CostEstimate(
            flops=4 * ROWS * CHUNK, bytes_accessed=2 * ROWS * CHUNK, transcendentals=0
        ),
        name="row_stats",
    )(hidden_rows)


def prepare_kernel(s_ref, place_hbm, freq, key_hbm, value_hbm, *refs):
    refs = refs[3:]
    send, last_own, last_send, cond, cos, sin, places_s, place_ref, key_ref, value_ref, sems = refs
    copies = [
        pltpu.make_async_copy(source, target, sems.at[n])
        for n, (source, target) in enumerate(
            ((key_hbm, key_ref), (value_hbm, value_ref), (place_hbm, place_ref))
        )
    ]
    for copy in copies:
        copy.start()
    copies[2].wait()
    for row in range(TOK):
        places_s[row : row + 1] = jnp.full((1, HD), place_ref[row], jnp.int32)
    place = places_s[...]
    frame_tok = TOK * N_PATCH // FRAMES
    frame = jnp.where(place >= frame_tok, 1, 0) + jnp.where(place >= 2 * frame_tok, 1, 0)
    within = place - frame * frame_tok
    grid_row = ((within.astype(F32) + 0.5) * (1.0 / GRID_W)).astype(jnp.int32)
    grid_col = within - grid_row * GRID_W
    lane = lax.broadcasted_iota(jnp.int32, (TOK, HD), 1)
    third = 2 * (HD // 6)
    frame_lanes = HD - 2 * third
    position = jnp.where(
        lane < frame_lanes, frame, jnp.where(lane < frame_lanes + third, grid_row, grid_col)
    )
    angles = position.astype(F32) * freq[...]
    cos[...] = jnp.cos(angles)
    sine = jnp.sin(angles)
    sin[...] = jnp.where(lane % 2 == 0, -sine, sine)
    flag = jnp.where((frame == 0) | (frame == FRAMES - 1), 1.0, 0.0)
    cond[0:TOK] = flag
    cond[TOK:ROWS] = flag
    own = s_ref[0]
    for n, ref in enumerate((key_ref, value_ref)):
        copies[n].wait()
        for s in range(B):
            for head in range(4):
                send[s * 4 + head, n] = ref[s, :, head * HD : (head + 1) * HD]
        last_own[n] = ref[own, :, 4 * HD :]
        last_send[n] = ref[1 - own, :, 4 * HD :]


def prepare(s, token_place, stale_keys, stale_values, after):
    table = jax.ShapeDtypeStruct((TOK, HD), F32)
    last = jax.ShapeDtypeStruct((2, TOK, HD), BF16)
    hbm = pl.BlockSpec(memory_space=pltpu.HBM)
    return pl.pallas_call(
        prepare_kernel,
        out_shape=[
            jax.ShapeDtypeStruct((8, 2, TOK, HD), BF16),
            last,
            last,
            jax.ShapeDtypeStruct((ROWS, HD), F32),
            table,
            table,
        ],
        in_specs=[smem(), hbm, vmem(), hbm, hbm] + [pl.BlockSpec(memory_space=pl.ANY)] * 3,
        out_specs=[vmem()] * 6,
        scratch_shapes=[
            pltpu.VMEM((TOK, HD), jnp.int32),
            pltpu.SMEM((TOK,), jnp.int32),
            pltpu.VMEM((B, TOK, WIDTH), BF16),
            pltpu.VMEM((B, TOK, WIDTH), BF16),
            pltpu.SemaphoreType.DMA((3,)),
        ],
        compiler_params=params(58),
        cost_estimate=pl.CostEstimate(
            flops=100 * TOK * HD, bytes_accessed=8 * ROWS * WIDTH, transcendentals=0
        ),
        name="prepare",
    )(s, token_place, jnp.asarray(frequencies()), stale_keys, stale_values, *after)


def assemble_kernel(s_ref, arrived, last_own, last_other, first, second):
    own = s_ref[0]
    for n in range(2):
        for u in range(4):
            first[n, u * TOK : (u + 1) * TOK] = arrived[u, n]
            second[n, u * TOK : (u + 1) * TOK] = arrived[4 + u, n]
        mine, other = last_own[n], last_other[n]
        first[n, 4 * TOK :] = jnp.where(own == 0, mine, other)
        second[n, 4 * TOK :] = jnp.where(own == 0, other, mine)


def assemble(s, arrived, last_own, last_other):
    shape = jax.ShapeDtypeStruct((2, PIECE, HD), BF16)
    return pl.pallas_call(
        assemble_kernel,
        out_shape=[shape, shape],
        in_specs=[smem()] + [vmem()] * 3,
        out_specs=[vmem()] * 2,
        compiler_params=params(32),
        cost_estimate=pl.CostEstimate(
            flops=0, bytes_accessed=16 * PIECE * HD, transcendentals=0
        ),
        name="assemble",
    )(s, arrived, last_own, last_other)


def merged_stats(refs):
    means = [ref[0:1] for ref in refs]
    mean = (means[0] + means[1] + means[2] + means[3]) * 0.25
    total = jnp.zeros_like(mean)
    for ref, one in zip(refs, means):
        total = total + (ref[1:2] + CHUNK * (one - mean) * (one - mean))
    return mean, lax.rsqrt(total * (1.0 / D) + EPS)


def project_kernel(count, first, last, *refs):
    t_ref = refs[0]
    chunks = refs[1 : 1 + count]
    cond, shift, scale, w_q, w_k, w_v, s0, s1, s2, s3 = refs[1 + count : 11 + count]
    rest = list(refs[11 + count :])
    acc_in = None if first else rest.pop(0)
    if last:
        q_out, k_out, v_out, sq_out, buffer, sems = rest
    else:
        acc, buffer, sems = rest
    copies = {}
    for c in range(count):
        row = pl.multiple_of(t_ref[c] * CHUNK, CHUNK)
        for n, weight in enumerate((w_q, w_k, w_v)):
            copies[c, n] = pltpu.make_async_copy(
                weight.at[pl.ds(row, CHUNK)], buffer.at[c, n], sems.at[c, n]
            )
            copies[c, n].start()
    mean, rstd = merged_stats((s0, s1, s2, s3))
    mean = row_to_column(mean)[:, 0:1]
    rstd = row_to_column(rstd)[:, 0:1]
    conditioned = cond[:, 0:1] > 0.5
    totals = [None] * 3
    for c in range(count):
        cols = pl.ds(pl.multiple_of(t_ref[c] * CHUNK, CHUNK), CHUNK)
        part = chunks[c][...].astype(F32)
        gain = jnp.where(conditioned, scale[1:2, cols], scale[0:1, cols])
        bias = jnp.where(conditioned, shift[1:2, cols], shift[0:1, cols])
        modded = ((part - mean) * rstd * (1.0 + gain) + bias).astype(BF16)
        for n in range(3):
            columns = slice(n * WIDTH, (n + 1) * WIDTH)
            copies[c, n].wait()
            product = jnp.dot(modded, buffer[c, n], preferred_element_type=F32)
            if c == 0 and not first:
                product = product + acc_in[:, columns]
            if last:
                totals[n] = product
            elif c == 0:
                acc[:, columns] = product
            else:
                acc[:, columns] += product
    if last:
        query, key, value = totals
        q_out[...] = query
        k_out[...] = key
        v_out[...] = value.astype(BF16)
        sq_out[...] = columns_to_rows(
            jnp.sum(query * query, axis=1, keepdims=True),
            jnp.sum(key * key, axis=1, keepdims=True),
        )


def project(name, blocks, chunks, cond, shift, scale, weights, stats, acc=None, last=False):
    count = len(chunks)
    hbm = pl.BlockSpec(memory_space=pltpu.HBM)
    in_specs = [smem()] + [vmem()] * (count + 3) + [hbm] * 3 + [vmem()] * 4
    args = [blocks, *chunks, cond, shift, scale, *weights, *stats]
    if acc is not None:
        in_specs.append(vmem())
        args.append(acc)
    if last:
        out_shape = [
            jax.ShapeDtypeStruct((ROWS, WIDTH), F32),
            jax.ShapeDtypeStruct((ROWS, WIDTH), F32),
            jax.ShapeDtypeStruct((ROWS, WIDTH), BF16),
            jax.ShapeDtypeStruct((8, STAT_LANES), F32),
        ]
        out_specs = [vmem()] * 4
    else:
        out_shape = jax.ShapeDtypeStruct((ROWS, 3 * WIDTH), F32)
        out_specs = vmem()
    return pl.pallas_call(
        functools.partial(project_kernel, count, acc is None, last),
        out_shape=out_shape,
        in_specs=in_specs,
        out_specs=out_specs,
        scratch_shapes=[
            pltpu.VMEM((count, 3, CHUNK, WIDTH), BF16),
            pltpu.SemaphoreType.DMA((count, 3)),
        ],
        compiler_params=params(58),
        cost_estimate=pl.CostEstimate(
            flops=2 * ROWS * count * CHUNK * 3 * WIDTH,
            bytes_accessed=2 * count * CHUNK * 3 * WIDTH,
            transcendentals=0,
        ),
        name=name,
    )(*args)


def rope_kernel(q_ref, k_ref, squares, qg, kg, cos, sin, q_all, k_all, send):
    total = squares[0] + squares[1] + squares[2] + squares[3]
    inverse = lax.rsqrt(total * (1.0 / (HEADS * HD)) + EPS)
    even = lax.broadcasted_iota(jnp.int32, (ROWS, HD), 1) % 2 == 0
    cos_rows = jnp.concatenate([cos[...], cos[...]], axis=0)
    sin_rows = jnp.concatenate([sin[...], sin[...]], axis=0)

    def rotate(ref, column, gain, cols):
        part = ref[:, cols] * column * gain[cols].reshape(1, HD)
        swap = jnp.where(even, pltpu.roll(part, HD - 1, 1), pltpu.roll(part, 1, 1))
        return (part * cos_rows + swap * sin_rows).astype(BF16)

    q_column = row_to_column(inverse[0:1])
    k_column = row_to_column(inverse[1:2])
    for head in range(LOCAL_HEADS):
        cols = slice(head * HD, (head + 1) * HD)
        query = rotate(q_ref, q_column, qg, cols)
        q_all[:, cols] = query
        for s in range(B):
            rows = query[s * TOK : (s + 1) * TOK]
            if head < 4:
                send[s * 4 + head, 0] = rows
            else:
                for u in range(4):
                    send[s * 4 + u, 1] = rows
        k_all[:, cols] = rotate(k_ref, k_column, kg, cols)


def norm_rope(query, key, squares, q_gain, k_gain, cos, sin):
    flat = jax.ShapeDtypeStruct((ROWS, WIDTH), BF16)
    return pl.pallas_call(
        rope_kernel,
        out_shape=[flat, flat, jax.ShapeDtypeStruct((8, 2, TOK, HD), BF16)],
        in_specs=[vmem()] * 7,
        out_specs=[vmem()] * 3,
        compiler_params=params(32),
        cost_estimate=pl.CostEstimate(
            flops=20 * ROWS * WIDTH, bytes_accessed=16 * ROWS * WIDTH, transcendentals=0
        ),
        name="norm_rope",
    )(query, key, squares, q_gain, k_gain, cos, sin)


def scores_of(query, keys):
    return lax.dot_general(query, keys, (((1,), (1,)), ((), ())), preferred_element_type=F32)


def fresh_kernel(q_ref, k_ref, v_ref, out_ref, lse_ref):
    for s in range(B):
        rows = slice(s * TOK, (s + 1) * TOK)
        for head in range(LOCAL_HEADS):
            cols = slice(head * HD, (head + 1) * HD)
            scores = scores_of(q_ref[rows, cols], k_ref[rows, cols])
            top = jnp.max(scores, axis=1, keepdims=True)
            probs = jnp.exp2((scores - top) * SCORE_SCALE)
            total = jnp.sum(probs, axis=1, keepdims=True)
            out = jnp.dot(probs.astype(BF16), v_ref[rows, cols], preferred_element_type=F32)
            out_ref[head, s] = out / total
            lse_ref[head, s] = jnp.broadcast_to(top * SCORE_SCALE + jnp.log2(total), (TOK, HD))


def fresh_attention(query, key, value):
    shape = jax.ShapeDtypeStruct((LOCAL_HEADS, B, TOK, HD), F32)
    return pl.pallas_call(
        fresh_kernel,
        out_shape=[shape, shape],
        in_specs=[vmem()] * 3,
        out_specs=[vmem()] * 2,
        compiler_params=params(32),
        cost_estimate=pl.CostEstimate(
            flops=4 * ROWS * TOK * WIDTH,
            bytes_accessed=14 * ROWS * WIDTH,
            transcendentals=ROWS * TOK * LOCAL_HEADS,
        ),
        name="fresh_attention",
    )(query, key, value)


TILE = 2 * TOK
GROUP = 16
PER_PIECE = 4 * TOK
KEYS = 4 * PER_PIECE
KEYS_LAST = 4 * TOK


def stale_kernel(far, u_ref, queries, *refs):
    pieces = refs[0:4]
    if far:
        near_out, near_lse, _, msg_ref = refs[4:8]
    else:
        out_ref, lse_ref = refs[4:6]
    lse_s, k_main, v_main, k_last, v_last, scores_s, probs_s, sems = refs[-8:]
    copies = []
    for n, piece in enumerate(pieces):
        main, last = pl.ds(n * PER_PIECE, PER_PIECE), pl.ds(n * TOK, TOK)
        head, tail = pl.ds(0, PER_PIECE), pl.ds(PER_PIECE, TOK)
        for kind, part, target, rows in (
            (0, head, k_main, main),
            (1, head, v_main, main),
            (0, tail, k_last, last),
            (1, tail, v_last, last),
        ):
            copy = pltpu.make_async_copy(
                piece.at[kind, part], target.at[rows], sems.at[len(copies)]
            )
            copy.start()
            copies.append(copy)
    for copy in copies:
        copy.wait()

    jobs = [(tile, e) for tile in range(4) for e in range(2)]

    def score(i):
        tile, e = jobs[i]
        count = KEYS_LAST if e else KEYS
        query = jnp.concatenate([queries[2 * tile, e], queries[2 * tile + 1, e]], axis=0)
        out = scores_s.at[i % 2]
        out[:, 0:count] = scores_of(query, k_last[...] if e else k_main[...])
        if far:
            return
        for n in range(2):
            block = 2 * tile + n
            rows = slice(n * TOK, (n + 1) * TOK)
            if not e:
                out[rows, block * TOK : (block + 1) * TOK] = jnp.full((TOK, TOK), MASKED, F32)
            else:
                lane = lax.broadcasted_iota(jnp.int32, (TOK, 384), 1)
                low = block // 4 * TOK
                own = (lane >= low) & (lane < low + TOK) & (u_ref[0] == block % 4)
                out[rows, 0:384] = jnp.where(own, MASKED, out[rows, 0:384])

    def softmax(i):
        count = KEYS_LAST if jobs[i][1] else KEYS
        tops, totals = [], []
        for row in range(0, TILE, GROUP):
            rows = slice(row, row + GROUP)
            part = scores_s[i % 2, rows, 0:count]
            top = jnp.max(part, axis=1, keepdims=True)
            probs = jnp.exp2((part - top) * SCORE_SCALE)
            totals.append(jnp.sum(probs, axis=1, keepdims=True))
            tops.append(top)
            probs_s[i % 2, rows, 0:count] = probs.astype(BF16)
        return jnp.concatenate(tops, axis=0), jnp.concatenate(totals, axis=0)

    def finish(i, top, total):
        tile, e = jobs[i]
        count = KEYS_LAST if e else KEYS
        values = v_last[...] if e else v_main[...]
        out = jnp.dot(probs_s[i % 2, :, 0:count], values, preferred_element_type=F32) / total
        lse = top * SCORE_SCALE + jnp.log2(total)
        rows = slice(tile * TILE, (tile + 1) * TILE)
        if not far:
            out_ref[e, rows] = out
            lse_ref[e, rows] = jnp.broadcast_to(lse, (TILE, HD))
            return
        lse_near = near_lse[e, rows][:, 0:1]
        high = jnp.maximum(lse, lse_near)
        weight, weight_near = jnp.exp2(lse - high), jnp.exp2(lse_near - high)
        both = weight + weight_near
        out = (out * weight + near_out[e, rows] * weight_near) / both
        lse_s[e, rows] = jnp.broadcast_to(high + jnp.log2(both), (TILE, HD))
        for n in range(2):
            msg_ref[2 * tile + n, e * TOK : (e + 1) * TOK] = out[n * TOK : (n + 1) * TOK].astype(BF16)

    score(0)
    for i in range(len(jobs)):
        if i + 1 < len(jobs):
            score(i + 1)
        finish(i, *softmax(i))
    if far:
        lane = lax.broadcasted_iota(jnp.int32, (HD, HD), 1)
        table = jnp.zeros((HD, HD), F32)
        rest_rows = jnp.zeros((2 * HD - TOK, HD), F32)
        for block in range(8):
            for e in range(2):
                at = block * TOK
                first = lse_s[e, at : at + HD]
                rest = jnp.concatenate([lse_s[e, at + HD : at + TOK], rest_rows], axis=0)
                table = jnp.where(lane == block * 4 + e * 2, first, table)
                table = jnp.where(lane == block * 4 + e * 2 + 1, rest, table)
        flat = table.T
        for block in range(8):
            part = flat[block * 4 : block * 4 + 4]
            high = part.astype(BF16).astype(F32)
            middle = (part - high).astype(BF16).astype(F32)
            low = part - high - middle
            stack = jnp.concatenate([high, middle, low, jnp.zeros((4, HD), F32)], axis=0)
            msg_ref[block, 2 * TOK : MSG_ROWS] = stack.astype(BF16)


def stale_attention(u, queries, pieces, near=None, after=None):
    far = near is not None
    args = [u, queries, *pieces]
    hbm = pl.BlockSpec(memory_space=pltpu.HBM)
    in_specs = [smem(), vmem()] + [hbm] * 4
    state = jax.ShapeDtypeStruct((2, 8 * TOK, HD), F32)
    if far:
        args += [*near, after]
        in_specs += [vmem()] * 2 + [pl.BlockSpec(memory_space=pl.ANY)]
        out_shape = jax.ShapeDtypeStruct((8, MSG_ROWS, HD), BF16)
        out_specs = vmem()
    else:
        out_shape = [state, state]
        out_specs = [vmem()] * 2
    work = 8 * TOK * (KEYS + KEYS_LAST)
    return pl.pallas_call(
        functools.partial(stale_kernel, far),
        out_shape=out_shape,
        in_specs=in_specs,
        out_specs=out_specs,
        scratch_shapes=[
            pltpu.VMEM((2, 8 * TOK, HD), F32),
            pltpu.VMEM((KEYS, HD), BF16),
            pltpu.VMEM((KEYS, HD), BF16),
            pltpu.VMEM((KEYS_LAST, HD), BF16),
            pltpu.VMEM((KEYS_LAST, HD), BF16),
            pltpu.VMEM((2, TILE, KEYS), F32),
            pltpu.VMEM((2, TILE, KEYS), BF16),
            pltpu.SemaphoreType.DMA((16,)),
        ],
        compiler_params=params(40),
        cost_estimate=pl.CostEstimate(
            flops=4 * work * HD, bytes_accessed=4 * (KEYS + KEYS_LAST) * HD, transcendentals=work
        ),
        name="far_attention" if far else "near_attention",
    )(*args)


def merge_kernel(fresh_out, fresh_lse, msgs, out_ref):
    rows = []
    for block in range(8):
        stack = msgs[block, 2 * TOK : MSG_ROWS].astype(F32)
        rows.append(stack[0:4] + stack[4:8] + stack[8:12])
    table = jnp.concatenate(rows + [jnp.zeros((HD - 32, HD), F32)], axis=0).T

    def message(block, e):
        at = block * 4 + e * 2
        lse = jnp.concatenate([table[:, at : at + 1], table[0 : TOK - HD, at + 1 : at + 2]], axis=0)
        return msgs[block, e * TOK : (e + 1) * TOK].astype(F32), lse

    def combine(parts):
        top = parts[0][1]
        for _, lse in parts[1:]:
            top = jnp.maximum(top, lse)
        total = out = None
        for value, lse in parts:
            weight = jnp.exp2(lse - top)
            term = value * weight
            total = weight if total is None else total + weight
            out = term if out is None else out + term
        return (out / total).astype(BF16)

    for s in range(B):
        for head in range(LOCAL_HEADS):
            parts = [(fresh_out[head, s], fresh_lse[head, s][:, 0:1])]
            if head < 4:
                parts.append(message(s * 4 + head, 0))
            else:
                parts += [message(s * 4 + u, 1) for u in range(4)]
            out_ref[s, :, head * HD : (head + 1) * HD] = combine(parts)


def merge(fresh_out, fresh_lse, msgs):
    return pl.pallas_call(
        merge_kernel,
        out_shape=jax.ShapeDtypeStruct((B, TOK, WIDTH), BF16),
        in_specs=[vmem()] * 3,
        out_specs=vmem(),
        compiler_params=params(32),
        cost_estimate=pl.CostEstimate(
            flops=10 * ROWS * WIDTH, bytes_accessed=14 * ROWS * WIDTH, transcendentals=0
        ),
        name="merge",
    )(fresh_out, fresh_lse, msgs)


def shards(
    hidden,
    mod_shift,
    mod_scale,
    w_query,
    w_key,
    w_value,
    q_gain,
    k_gain,
    token_place,
    stale_keys,
    stale_values,
):
    patch = lax.axis_index("patch")
    tp = lax.axis_index("tp")
    y = patch // (NX * NZ)
    x = (patch // NZ) % NX
    u = jnp.where(tp % 2 == 0, y, x).astype(jnp.int32).reshape(1)
    v = jnp.where(tp % 2 == 0, x, y).astype(jnp.int32).reshape(1)
    s = (v ^ (v >> 1)) & 1

    own_rows = hidden.reshape(ROWS, CHUNK)
    z_rows = swap_tp(own_rows, 1, 0)
    core_rows = swap_tp(own_rows, 0, 1)

    own_stats = row_stats(own_rows)
    stats = [own_stats] + [swap_tp(own_stats, z, c) for z, c in ((0, 1), (1, 0), (1, 1))]

    send, last_own, last_send, cond, cos, sin = prepare(
        s, token_place, stale_keys, stale_values, stats[1:]
    )
    near = assemble(s, exchange(send), last_own, swap_pair(last_send))
    near_all = [*near, *[swap_v(piece) for piece in near]]

    weights = (w_query, w_key, w_value)
    block = lambda flip: (tp ^ flip).astype(jnp.int32).reshape(1)
    blocks = jnp.concatenate([block(0), block(1)])
    same = (cond, mod_shift, mod_scale, weights, stats)
    acc = project("project_chip", blocks, [own_rows, core_rows], *same)

    *near, z_rows = lax.optimization_barrier((*near, z_rows))
    cross_rows = swap_tp(z_rows, 0, 1)
    far = [swap_z_hi(piece) for piece in near]
    far_all = [*far, *[swap_v(piece) for piece in far]]
    acc = project("project_z", block(2), [z_rows], *same, acc=acc)
    query, key, fresh_values, own_sq = project(
        "project_cross", block(3), [cross_rows], *same, acc=acc, last=True
    )

    squares = lax.all_to_all(jnp.broadcast_to(own_sq, (TP, 8, STAT_LANES)), "tp", 0, 0)
    q_all, fresh_keys, send = norm_rope(query, key, squares, q_gain, k_gain, cos, sin)
    queries = exchange(send)
    fresh_out, fresh_lse = fresh_attention(q_all, fresh_keys, fresh_values)

    partial = stale_attention(u, queries, near_all)
    msgs = exchange(stale_attention(u, queries, far_all, near=partial, after=fresh_lse))
    attended = merge(fresh_out, fresh_lse, msgs)
    return (
        attended,
        fresh_keys.reshape(B, TOK, WIDTH),
        fresh_values.reshape(B, TOK, WIDTH),
    )


def solution(mesh):
    in_specs = (
        P(None, "patch", "tp"),
        P(),
        P(),
        P(None, "tp"),
        P(None, "tp"),
        P(None, "tp"),
        P("tp"),
        P("tp"),
        P("patch"),
        P(None, "patch", "tp"),
        P(None, "patch", "tp"),
    )
    out_specs = (P(None, "patch", "tp"), P(None, "patch", "tp"), P(None, "patch", "tp"))
    return jax.shard_map(shards, mesh=mesh, in_specs=in_specs, out_specs=out_specs, check_vma=False)
```

```python
import functools
import math

import jax
import jax.numpy as jnp
import numpy as np
from jax import lax
from jax.experimental import pallas as pl
from jax.experimental.pallas import tpu as pltpu
from jax.sharding import PartitionSpec as P

D = 5120
HEADS = 20
HD = 128
FRAMES = 3
GRID_W = 48
EPS = 1e-06
MASKED = -1e30
NY, NX, NZ = 4, 4, 2
TP = 4
N_PATCH = NY * NX * NZ
TOK = 144
B = 2
ROWS = B * TOK
LOCAL_HEADS = 5
WIDTH = LOCAL_HEADS * HD
CHUNK = D // TP
STAT_LANES = 384
PIECE = 5 * TOK
MSG_ROWS = 2 * TOK + 16
SCORE_SCALE = math.log2(math.e) / math.sqrt(HD)
F32 = jnp.float32
BF16 = jnp.bfloat16
AXES = ("patch", "tp")
VMEM_MIB = 40


def params(mib):
    return pltpu.CompilerParams(vmem_limit_bytes=mib * 1024 * 1024)


def vmem():
    return pl.BlockSpec(memory_space=pltpu.VMEM)


def smem():
    return pl.BlockSpec(memory_space=pltpu.SMEM)


def linear(u, v, z_hi, z_lo, core):
    y, x = (u, v) if core == 0 else (v, u)
    return ((y * NX + x) * NZ + z_hi) * TP + z_lo * 2 + core


def places():
    return [
        (u, v, h, l, c)
        for u in range(4)
        for v in range(4)
        for h in range(2)
        for l in range(2)
        for c in range(2)
    ]


def permute(value, move):
    return lax.ppermute(value, AXES, [(linear(*p), linear(*move(*p))) for p in places()])


def to_peer(value, p, k):
    return permute(value, lambda u, v, h, l, c: ((u + k) % 4, v ^ p, h, l, c))


def swap_v(value):
    return permute(value, lambda u, v, h, l, c: (u, v ^ 3, h, l, c))


def swap_z_hi(value):
    return permute(value, lambda u, v, h, l, c: (u, v, 1 - h, l, c))


def swap_tp(value, z, core):
    if core:
        return permute(value, lambda u, v, h, l, c: (v, u, h, l ^ z, 1 - c))
    return permute(value, lambda u, v, h, l, c: (u, v, h, l ^ z, c))


def frequencies():
    half_dim = HD // 2
    third_dim = half_dim // 3
    frame_pairs = half_dim - 2 * third_dim
    pair = np.arange(HD) // 2
    offset = np.where(
        pair < frame_pairs,
        pair,
        np.where(pair < frame_pairs + third_dim, pair - frame_pairs, pair - frame_pairs - third_dim),
    )
    width = np.where(pair < frame_pairs, 2 * frame_pairs, 2 * third_dim)
    return np.exp(-math.log(10000.0) * 2.0 * offset / width).astype(np.float32).reshape(1, HD)


def columns_to_rows(first, second):
    lane = lax.broadcasted_iota(jnp.int32, (ROWS, 128), 1)
    both = jnp.where(lane == 0, first, jnp.where(lane == 1, second, 0.0))
    padded = jnp.concatenate([both, jnp.zeros((STAT_LANES - ROWS, 128), F32)], axis=0)
    return padded.T[0:8]


def row_to_column(row):
    return jnp.broadcast_to(row, (128, STAT_LANES)).T[0:ROWS]


def stats_kernel(hidden_hbm, out_ref, hidden_ref, sem):
    copy = pltpu.make_async_copy(hidden_hbm, hidden_ref, sem.at[0])
    copy.start()
    copy.wait()
    part = hidden_ref[...].astype(F32)
    mean = jnp.sum(part, axis=1, keepdims=True) * (1.0 / CHUNK)
    centered = part - mean
    deviation = jnp.sum(centered * centered, axis=1, keepdims=True)
    out_ref[...] = columns_to_rows(mean, deviation)


def row_stats(hidden_rows):
    return pl.pallas_call(
        stats_kernel,
        out_shape=jax.ShapeDtypeStruct((8, STAT_LANES), F32),
        in_specs=[pl.BlockSpec(memory_space=pltpu.HBM)],
        out_specs=vmem(),
        scratch_shapes=[pltpu.VMEM((ROWS, CHUNK), BF16), pltpu.SemaphoreType.DMA((1,))],
        compiler_params=params(VMEM_MIB),
        cost_estimate=pl.CostEstimate(
            flops=4 * ROWS * CHUNK, bytes_accessed=2 * ROWS * CHUNK, transcendentals=0
        ),
        name="row_stats",
    )(hidden_rows)


def pack_kernel(u_ref, key_hbm, value_hbm, *refs):
    outs, sems = refs[0:5], refs[5]
    copies = []
    for k in range(5):
        head = lax.rem(u_ref[0] + k, 4) if k < 4 else 4
        cols = pl.ds(pl.multiple_of(head * HD, HD), HD)
        for n, source in enumerate((key_hbm, value_hbm)):
            for s in range(B):
                copy = pltpu.make_async_copy(
                    source.at[s, :, cols], outs[k].at[s, n], sems.at[len(copies)]
                )
                copy.start()
                copies.append(copy)
    for copy in copies:
        copy.wait()


def pack_stale(u, stale_keys, stale_values):
    hbm = pl.BlockSpec(memory_space=pltpu.HBM)
    return pl.pallas_call(
        pack_kernel,
        out_shape=[jax.ShapeDtypeStruct((B, 2, TOK, HD), BF16)] * 5,
        in_specs=[smem(), hbm, hbm],
        out_specs=[vmem()] * 5,
        scratch_shapes=[pltpu.SemaphoreType.DMA((20,))],
        compiler_params=params(VMEM_MIB),
        cost_estimate=pl.CostEstimate(
            flops=0, bytes_accessed=8 * ROWS * WIDTH, transcendentals=0
        ),
        name="pack_stale",
    )(u, stale_keys, stale_values)


def tables_kernel(place_hbm, freq, after, cond, cos, sin, places_s, place_ref, sem):
    copy = pltpu.make_async_copy(place_hbm, place_ref, sem.at[0])
    copy.start()
    copy.wait()
    for row in range(TOK):
        places_s[row : row + 1] = jnp.full((1, HD), place_ref[row], jnp.int32)
    place = places_s[...]
    frame_tok = TOK * N_PATCH // FRAMES
    frame = jnp.where(place >= frame_tok, 1, 0) + jnp.where(place >= 2 * frame_tok, 1, 0)
    within = place - frame * frame_tok
    grid_row = ((within.astype(F32) + 0.5) * (1.0 / GRID_W)).astype(jnp.int32)
    grid_col = within - grid_row * GRID_W
    lane = lax.broadcasted_iota(jnp.int32, (TOK, HD), 1)
    third = 2 * (HD // 6)
    frame_lanes = HD - 2 * third
    position = jnp.where(
        lane < frame_lanes, frame, jnp.where(lane < frame_lanes + third, grid_row, grid_col)
    )
    angles = position.astype(F32) * freq[...]
    cos[...] = jnp.cos(angles)
    sine = jnp.sin(angles)
    sin[...] = jnp.where(lane % 2 == 0, -sine, sine)
    flag = jnp.where((frame == 0) | (frame == FRAMES - 1), 1.0, 0.0)
    cond[0:TOK] = flag
    cond[TOK:ROWS] = flag


def tables(token_place, after):
    table = jax.ShapeDtypeStruct((TOK, HD), F32)
    return pl.pallas_call(
        tables_kernel,
        out_shape=[jax.ShapeDtypeStruct((ROWS, HD), F32), table, table],
        in_specs=[
            pl.BlockSpec(memory_space=pltpu.HBM),
            vmem(),
            pl.BlockSpec(memory_space=pl.ANY),
        ],
        out_specs=[vmem()] * 3,
        scratch_shapes=[
            pltpu.VMEM((TOK, HD), jnp.int32),
            pltpu.SMEM((TOK,), jnp.int32),
            pltpu.SemaphoreType.DMA((1,)),
        ],
        compiler_params=params(VMEM_MIB),
        cost_estimate=pl.CostEstimate(
            flops=100 * TOK * HD, bytes_accessed=16 * TOK * HD, transcendentals=0
        ),
        name="tables",
    )(token_place, jnp.asarray(frequencies()), after)


def assemble_kernel(s_ref, *refs):
    parts, outs = refs[0:5], refs[5:7]
    for p in range(2):
        s = s_ref[0] if p == 0 else 1 - s_ref[0]
        for n in range(2):
            for r in range(5):
                outs[p][n, r * TOK : (r + 1) * TOK] = parts[r][s, n]


def assemble(s, parts):
    shape = jax.ShapeDtypeStruct((2, PIECE, HD), BF16)
    return pl.pallas_call(
        assemble_kernel,
        out_shape=[shape, shape],
        in_specs=[smem()] + [vmem()] * 5,
        out_specs=[vmem()] * 2,
        compiler_params=params(VMEM_MIB),
        cost_estimate=pl.CostEstimate(
            flops=0, bytes_accessed=16 * PIECE * HD, transcendentals=0
        ),
        name="assemble",
    )(s, *parts)


def merged_stats(refs):
    means = [ref[0:1] for ref in refs]
    mean = (means[0] + means[1] + means[2] + means[3]) * 0.25
    total = jnp.zeros_like(mean)
    for ref, one in zip(refs, means):
        total = total + (ref[1:2] + CHUNK * (one - mean) * (one - mean))
    return mean, lax.rsqrt(total * (1.0 / D) + EPS)


def project_kernel(count, unread, first, last, *refs):
    t_ref = refs[0]
    chunks = refs[1 : 1 + count]
    cond, shift, scale, w_q, w_k, w_v, s0, s1, s2, s3 = refs[1 + count : 11 + count]
    rest = list(refs[11 + count :])
    acc_in = None if first else rest.pop(0)
    rest = rest[unread:]
    if last:
        q_out, k_out, v_out, sq_out, buffer, sems = rest
    else:
        acc, buffer, sems = rest
    copies = {}
    for c in range(count):
        row = pl.multiple_of(t_ref[c] * CHUNK, CHUNK)
        for n, weight in enumerate((w_q, w_k, w_v)):
            copies[c, n] = pltpu.make_async_copy(
                weight.at[pl.ds(row, CHUNK)], buffer.at[c, n], sems.at[c, n]
            )
            copies[c, n].start()
    mean, rstd = merged_stats((s0, s1, s2, s3))
    mean = row_to_column(mean)[:, 0:1]
    rstd = row_to_column(rstd)[:, 0:1]
    conditioned = cond[:, 0:1] > 0.5
    totals = [None] * 3
    for c in range(count):
        cols = pl.ds(pl.multiple_of(t_ref[c] * CHUNK, CHUNK), CHUNK)
        part = chunks[c][...].astype(F32)
        gain = jnp.where(conditioned, scale[1:2, cols], scale[0:1, cols])
        bias = jnp.where(conditioned, shift[1:2, cols], shift[0:1, cols])
        modded = ((part - mean) * rstd * (1.0 + gain) + bias).astype(BF16)
        for n in range(3):
            columns = slice(n * WIDTH, (n + 1) * WIDTH)
            copies[c, n].wait()
            product = jnp.dot(modded, buffer[c, n], preferred_element_type=F32)
            if c == 0 and not first:
                product = product + acc_in[:, columns]
            if last:
                totals[n] = product
            elif c == 0:
                acc[:, columns] = product
            else:
                acc[:, columns] += product
    if last:
        query, key, value = totals
        q_out[...] = query
        k_out[...] = key
        v_out[...] = value.astype(BF16)
        sq_out[...] = columns_to_rows(
            jnp.sum(query * query, axis=1, keepdims=True),
            jnp.sum(key * key, axis=1, keepdims=True),
        )


def project(name, blocks, chunks, cond, shift, scale, weights, stats, acc=None, last=False, after=()):
    count = len(chunks)
    hbm = pl.BlockSpec(memory_space=pltpu.HBM)
    in_specs = [smem()] + [vmem()] * (count + 3) + [hbm] * 3 + [vmem()] * 4
    args = [blocks, *chunks, cond, shift, scale, *weights, *stats]
    if acc is not None:
        in_specs.append(vmem())
        args.append(acc)
    in_specs += [pl.BlockSpec(memory_space=pl.ANY)] * len(after)
    args += after
    if last:
        out_shape = [
            jax.ShapeDtypeStruct((ROWS, WIDTH), F32),
            jax.ShapeDtypeStruct((ROWS, WIDTH), F32),
            jax.ShapeDtypeStruct((ROWS, WIDTH), BF16),
            jax.ShapeDtypeStruct((8, STAT_LANES), F32),
        ]
        out_specs = [vmem()] * 4
    else:
        out_shape = jax.ShapeDtypeStruct((ROWS, 3 * WIDTH), F32)
        out_specs = vmem()
    return pl.pallas_call(
        functools.partial(project_kernel, count, len(after), acc is None, last),
        out_shape=out_shape,
        in_specs=in_specs,
        out_specs=out_specs,
        scratch_shapes=[
            pltpu.VMEM((count, 3, CHUNK, WIDTH), BF16),
            pltpu.SemaphoreType.DMA((count, 3)),
        ],
        compiler_params=params(VMEM_MIB),
        cost_estimate=pl.CostEstimate(
            flops=2 * ROWS * count * CHUNK * 3 * WIDTH,
            bytes_accessed=2 * count * CHUNK * 3 * WIDTH,
            transcendentals=0,
        ),
        name=name,
    )(*args)


def rope_kernel(u_ref, s_ref, q_ref, k_ref, s0, s1, s2, s3, qg, kg, cos, sin, k_all, *refs):
    sends, q_rot = refs[0:8], refs[8]
    total = s0[...] + s1[...] + s2[...] + s3[...]
    inverse = lax.rsqrt(total * (1.0 / (HEADS * HD)) + EPS)
    even = lax.broadcasted_iota(jnp.int32, (ROWS, HD), 1) % 2 == 0
    cos_rows = jnp.concatenate([cos[...], cos[...]], axis=0)
    sin_rows = jnp.concatenate([sin[...], sin[...]], axis=0)

    def rotate(ref, column, gain, cols):
        part = ref[:, cols] * column * gain[cols].reshape(1, HD)
        swap = jnp.where(even, pltpu.roll(part, HD - 1, 1), pltpu.roll(part, 1, 1))
        return (part * cos_rows + swap * sin_rows).astype(BF16)

    q_column = row_to_column(inverse[0:1])
    k_column = row_to_column(inverse[1:2])
    for head in range(LOCAL_HEADS):
        cols = slice(head * HD, (head + 1) * HD)
        query = rotate(q_ref, q_column, qg, cols)
        for s in range(B):
            q_rot[head, s] = query[s * TOK : (s + 1) * TOK]
        k_all[:, cols] = rotate(k_ref, k_column, kg, cols)
    for p in range(2):
        s = s_ref[0] if p == 0 else 1 - s_ref[0]
        for k in range(4):
            sends[4 * p + k][0] = q_rot[lax.rem(u_ref[0] + k, 4), s]
            sends[4 * p + k][1] = q_rot[4, s]


def norm_rope(u, s, query, key, squares, q_gain, k_gain, cos, sin):
    send = jax.ShapeDtypeStruct((2, TOK, HD), BF16)
    return pl.pallas_call(
        rope_kernel,
        out_shape=[jax.ShapeDtypeStruct((ROWS, WIDTH), BF16)] + [send] * 8,
        in_specs=[smem()] * 2 + [vmem()] * 10,
        out_specs=[vmem()] * 9,
        scratch_shapes=[pltpu.VMEM((LOCAL_HEADS, B, TOK, HD), BF16)],
        compiler_params=params(VMEM_MIB),
        cost_estimate=pl.CostEstimate(
            flops=20 * ROWS * WIDTH, bytes_accessed=16 * ROWS * WIDTH, transcendentals=0
        ),
        name="norm_rope",
    )(u, s, query, key, *squares, q_gain, k_gain, cos, sin)


def scores_of(query, keys):
    return lax.dot_general(query, keys, (((1,), (1,)), ((), ())), preferred_element_type=F32)


def to_rows(blocks):
    lane = lax.broadcasted_iota(jnp.int32, (HD, HD), 1)
    table = jnp.zeros((HD, HD), F32)
    empty = jnp.zeros((2 * HD - TOK, HD), F32)
    for n, block in enumerate(blocks):
        rest = jnp.concatenate([block[HD:TOK], empty], axis=0)
        table = jnp.where(lane == 2 * n, block[0:HD], table)
        table = jnp.where(lane == 2 * n + 1, rest, table)
    return table.T


FRESH_ROWS = 24


def fresh_kernel(u_ref, s_ref, k_ref, v_ref, *refs):
    queries, (out_ref, rows_ref) = refs[0:8], refs[8:10]
    lses = []
    for p in range(2):
        s = s_ref[0] if p == 0 else 1 - s_ref[0]
        rows = pl.ds(pl.multiple_of(s * TOK, TOK), TOK)
        for k in range(LOCAL_HEADS):
            head = lax.rem(u_ref[0] + k, 4) if k < 4 else 4
            cols = pl.ds(pl.multiple_of(head * HD, HD), HD)
            query = queries[4 * p + k][0] if k < 4 else queries[4 * p][1]
            scores = scores_of(query, k_ref[rows, cols])
            top = jnp.max(scores, axis=1, keepdims=True)
            probs = jnp.exp2((scores - top) * SCORE_SCALE)
            total = jnp.sum(probs, axis=1, keepdims=True)
            out = jnp.dot(probs.astype(BF16), v_ref[rows, cols], preferred_element_type=F32)
            out_ref[p, k] = out / total
            lses.append(jnp.broadcast_to(top * SCORE_SCALE + jnp.log2(total), (TOK, HD)))
    rows_ref[...] = to_rows(lses)[0:FRESH_ROWS]


def fresh_attention(u, s, key, value, queries):
    return pl.pallas_call(
        fresh_kernel,
        out_shape=[
            jax.ShapeDtypeStruct((B, LOCAL_HEADS, TOK, HD), F32),
            jax.ShapeDtypeStruct((FRESH_ROWS, HD), F32),
        ],
        in_specs=[smem()] * 2 + [vmem()] * 10,
        out_specs=[vmem()] * 2,
        compiler_params=params(VMEM_MIB),
        cost_estimate=pl.CostEstimate(
            flops=4 * ROWS * TOK * WIDTH,
            bytes_accessed=14 * ROWS * WIDTH,
            transcendentals=ROWS * TOK * LOCAL_HEADS,
        ),
        name="fresh_attention",
    )(u, s, key, value, *queries)


TILE = 2 * TOK
GROUP = 16
PER_PIECE = 4 * TOK
KEYS = 4 * PER_PIECE
KEYS_LAST = 4 * TOK
SPLIT = 768


def stale_kernel(far, count, *refs):
    queries, pieces = refs[0:count], refs[count : count + 4]
    rest = refs[count + 4 :]
    if far:
        near_out, near_lse = rest[0:2]
        msgs = rest[3 : 3 + count]
    else:
        out_ref, lse_ref = rest[0:2]
    lse_s, acc_s, k_main, v_main, k_last, v_last, scores_s, probs_s, sems = rest[-9:]
    copies = []
    for n, piece in enumerate(pieces):
        main, last = pl.ds(n * PER_PIECE, PER_PIECE), pl.ds(n * TOK, TOK)
        head, tail = pl.ds(0, PER_PIECE), pl.ds(PER_PIECE, TOK)
        for kind, part, target, rows in (
            (0, head, k_main, main),
            (0, tail, k_last, last),
            (1, head, v_main, main),
            (1, tail, v_last, last),
        ):
            copy = pltpu.make_async_copy(
                piece.at[kind, part], target.at[rows], sems.at[len(copies)]
            )
            copy.start()
            copies.append(copy)
    for copy in copies:
        copy.wait()

    jobs = [(tile, e) for e in range(2) for tile in range(count // 2)]

    def size(i):
        return KEYS_LAST if jobs[i][1] else KEYS

    def score_steps(i):
        tile, e = jobs[i]
        keys = k_last if e else k_main
        out = scores_s.at[i % 2]

        def step(at, end):
            query = jnp.concatenate([queries[2 * tile][e], queries[2 * tile + 1][e]], axis=0)
            out[:, at:end] = scores_of(query, keys[at:end])

        def hide():
            for n in range(2):
                block = 2 * tile + n
                rows = slice(n * TOK, (n + 1) * TOK)
                p, r = block // 4, block % 4
                if not e:
                    at = (p * 4 + r) * TOK
                elif r == 0:
                    at = p * TOK
                else:
                    continue
                out[rows, at : at + TOK] = jnp.full((TOK, TOK), MASKED, F32)

        steps = []
        for at in range(0, size(i), SPLIT):
            steps.append(functools.partial(step, at, min(at + SPLIT, size(i))))
        return steps if far else steps + [hide]

    def softmax_steps(i, tops, totals):
        def step(row):
            rows = slice(row, row + GROUP)
            part = scores_s[i % 2, rows, 0 : size(i)]
            top = jnp.max(part, axis=1, keepdims=True)
            probs = jnp.exp2((part - top) * SCORE_SCALE)
            totals.append(jnp.sum(probs, axis=1, keepdims=True))
            tops.append(top)
            probs_s[i % 2, rows, 0 : size(i)] = probs.astype(BF16)

        return [functools.partial(step, row) for row in range(0, TILE, GROUP)]

    def product_steps(i, tops, totals):
        tile, e = jobs[i]
        values = v_last if e else v_main

        def step(at, end):
            part = jnp.dot(probs_s[i % 2, :, at:end], values[at:end], preferred_element_type=F32)
            acc_s[...] = part if at == 0 else acc_s[...] + part

        def finish():
            top, total = jnp.concatenate(tops, axis=0), jnp.concatenate(totals, axis=0)
            out = acc_s[...] / total
            lse = top * SCORE_SCALE + jnp.log2(total)
            rows = slice(tile * TILE, (tile + 1) * TILE)
            if not far:
                for n in range(2):
                    block = 2 * tile + n
                    half = slice(n * TOK, (n + 1) * TOK)
                    out_ref[block // 4, block % 4, e] = out[half]
                    lse_ref[block // 4, block % 4, e] = jnp.broadcast_to(lse[half], (TOK, HD))
                return
            for n in range(2):
                block = 2 * tile + n
                half = slice(n * TOK, (n + 1) * TOK)
                lse_near = near_lse[block // 4, block % 4, e][:, 0:1]
                high = jnp.maximum(lse[half], lse_near)
                weight, weight_near = jnp.exp2(lse[half] - high), jnp.exp2(lse_near - high)
                both = weight + weight_near
                value = (out[half] * weight + near_out[block // 4, block % 4, e] * weight_near) / both
                lse_s[block, e] = jnp.broadcast_to(high + jnp.log2(both), (TOK, HD))
                msgs[block][e * TOK : (e + 1) * TOK] = value.astype(BF16)

        steps = []
        for at in range(0, size(i), SPLIT):
            steps.append(functools.partial(step, at, min(at + SPLIT, size(i))))
        return steps + [finish]

    def weave(*lists):
        order = []
        for steps in lists:
            order += [((n + 0.5) / len(steps), step) for n, step in enumerate(steps)]
        for _, step in sorted(order, key=lambda entry: entry[0]):
            step()

    weave(score_steps(0))
    pending = None
    for i in range(len(jobs)):
        tops, totals = [], []
        lists = [softmax_steps(i, tops, totals)]
        if i + 1 < len(jobs):
            lists.append(score_steps(i + 1))
        if pending is not None:
            lists.append(pending)
        weave(*lists)
        pending = product_steps(i, tops, totals)
    weave(pending)

    if far:
        flat = to_rows([lse_s[block, e] for block in range(count) for e in range(2)])
        for block in range(count):
            part = flat[block * 4 : block * 4 + 4]
            high = part.astype(BF16).astype(F32)
            middle = (part - high).astype(BF16).astype(F32)
            low = part - high - middle
            stack = jnp.concatenate([high, middle, low, jnp.zeros((4, HD), F32)], axis=0)
            msgs[block][2 * TOK : MSG_ROWS] = stack.astype(BF16)


def stale_attention(queries, pieces, near=None, after=None):
    far = near is not None
    count = len(queries)
    args = [*queries, *pieces]
    hbm = pl.BlockSpec(memory_space=pltpu.HBM)
    in_specs = [vmem()] * count + [hbm] * 4
    if far:
        args += [*near, after]
        in_specs += [vmem(), vmem(), pl.BlockSpec(memory_space=pl.ANY)]
        out_shape = [jax.ShapeDtypeStruct((MSG_ROWS, HD), BF16)] * count
    else:
        out_shape = [jax.ShapeDtypeStruct((B, 4, 2, TOK, HD), F32)] * 2
    work = count * TOK * (KEYS + KEYS_LAST)
    return pl.pallas_call(
        functools.partial(stale_kernel, far, count),
        out_shape=out_shape,
        in_specs=in_specs,
        out_specs=[vmem()] * len(out_shape),
        scratch_shapes=[
            pltpu.VMEM((8, 2, TOK, HD), F32),
            pltpu.VMEM((TILE, HD), F32),
            pltpu.VMEM((KEYS, HD), BF16),
            pltpu.VMEM((KEYS, HD), BF16),
            pltpu.VMEM((KEYS_LAST, HD), BF16),
            pltpu.VMEM((KEYS_LAST, HD), BF16),
            pltpu.VMEM((2, TILE, KEYS), F32),
            pltpu.VMEM((2, TILE, KEYS), BF16),
            pltpu.SemaphoreType.DMA((16,)),
        ],
        compiler_params=params(VMEM_MIB),
        cost_estimate=pl.CostEstimate(
            flops=4 * work * HD, bytes_accessed=4 * (KEYS + KEYS_LAST) * HD, transcendentals=work
        ),
        name="far_attention" if far else "near_attention",
    )(*args)


def merge_kernel(u_ref, s_ref, fresh_out, fresh_rows, *refs):
    msgs, out_ref = refs[0:8], refs[8]
    lses = []
    for msg in msgs:
        stack = msg[2 * TOK : MSG_ROWS].astype(F32)
        lses.append(stack[0:4] + stack[4:8] + stack[8:12])
    weights, jobs = [], []
    for p in range(2):
        for k in range(LOCAL_HEADS):
            at = (p * LOCAL_HEADS + k) * 2
            parts = [(None, fresh_rows[at : at + 2])]
            if k < 4:
                parts.append((4 * p + k, lses[4 * p + k][0:2]))
            else:
                parts += [(4 * p + n, lses[4 * p + n][2:4]) for n in range(4)]
            top = parts[0][1]
            for _, lse in parts[1:]:
                top = jnp.maximum(top, lse)
            raw = [jnp.exp2(lse - top) for _, lse in parts]
            total = sum(raw[1:], raw[0])
            jobs.append((p, k, [(source, len(weights) + n) for n, (source, _) in enumerate(parts)]))
            weights += [one / total for one in raw]
    filler = jnp.zeros((HD - 2 * len(weights), HD), F32)
    table = jnp.concatenate(weights + [filler], axis=0).T
    for p, k, parts in jobs:
        s = s_ref[0] if p == 0 else 1 - s_ref[0]
        head = lax.rem(u_ref[0] + k, 4) if k < 4 else 4
        out = [None, None]
        for source, n in parts:
            for half, rows in enumerate((slice(0, HD), slice(HD, TOK))):
                if source is None:
                    value = fresh_out[p, k, rows]
                else:
                    at = 0 if k < 4 else TOK
                    value = msgs[source][at + rows.start : at + rows.stop].astype(F32)
                column = table[0 : rows.stop - rows.start, 2 * n + half : 2 * n + half + 1]
                term = value * column
                out[half] = term if out[half] is None else out[half] + term
        cols = pl.ds(pl.multiple_of(head * HD, HD), HD)
        out_ref[s, :, cols] = jnp.concatenate(out, axis=0).astype(BF16)


def merge(u, s, fresh_out, fresh_rows, msgs):
    return pl.pallas_call(
        merge_kernel,
        out_shape=jax.ShapeDtypeStruct((B, TOK, WIDTH), BF16),
        in_specs=[smem()] * 2 + [vmem()] * 10,
        out_specs=vmem(),
        compiler_params=params(VMEM_MIB),
        cost_estimate=pl.CostEstimate(
            flops=10 * ROWS * WIDTH, bytes_accessed=14 * ROWS * WIDTH, transcendentals=0
        ),
        name="merge",
    )(u, s, fresh_out, fresh_rows, *msgs)


def shards(
    hidden,
    mod_shift,
    mod_scale,
    w_query,
    w_key,
    w_value,
    q_gain,
    k_gain,
    token_place,
    stale_keys,
    stale_values,
):
    patch = lax.axis_index("patch")
    tp = lax.axis_index("tp")
    y = patch // (NX * NZ)
    x = (patch // NZ) % NX
    u = jnp.where(tp % 2 == 0, y, x).astype(jnp.int32).reshape(1)
    v = jnp.where(tp % 2 == 0, x, y).astype(jnp.int32).reshape(1)
    s = (v ^ (v >> 1)) & 1

    own_rows = hidden.reshape(ROWS, CHUNK)
    own_stats = row_stats(own_rows)
    stats = [own_stats] + [swap_tp(own_stats, z, c) for z, c in ((1, 0), (1, 1), (0, 1))]
    own_rows, *stats = lax.optimization_barrier((own_rows, *stats))
    z_rows = swap_tp(own_rows, 1, 0)
    core_rows = swap_tp(own_rows, 0, 1)

    packed = pack_stale(u, stale_keys, stale_values)
    arrived = [packed[0]] + [to_peer(packed[4 - r], 0, 4 - r) for r in range(1, 4)]
    near, other = assemble(s, [*arrived, packed[4]])
    near = [near, to_peer(other, 1, 0)]
    near_all = [*near, *[swap_v(piece) for piece in near]]
    cond, cos, sin = tables(token_place, other)

    weights = (w_query, w_key, w_value)
    block = lambda flip: (tp ^ flip).astype(jnp.int32).reshape(1)
    blocks = jnp.concatenate([block(0), block(1)])
    same = (cond, mod_shift, mod_scale, weights, stats)
    acc = project("project_chip", blocks, [own_rows, core_rows], *same)

    *near, z_rows, acc = lax.optimization_barrier((*near, z_rows, acc))
    cross_rows = swap_tp(z_rows, 0, 1)
    far = [swap_z_hi(piece) for piece in near]
    acc = project("project_z", block(2), [z_rows], *same, acc=acc, after=near_all[2:])
    query, key, fresh_values, own_sq = project(
        "project_cross", block(3), [cross_rows], *same, acc=acc, last=True
    )

    squares = [own_sq] + [swap_tp(own_sq, z, c) for z, c in ((1, 0), (1, 1), (0, 1))]
    fresh_keys, *sends = norm_rope(u, s, query, key, squares, q_gain, k_gain, cos, sin)
    queries = [None] * 8
    queries[0] = sends[0]
    for p, r in ((0, 1), (0, 3), (1, 0), (0, 2), (1, 1), (1, 3), (1, 2)):
        k = (4 - r) % 4
        queries[4 * p + r] = to_peer(sends[4 * p + k], p, k)
    fresh_out, fresh_rows = fresh_attention(u, s, fresh_keys, fresh_values, sends)

    far_second, *queries = lax.optimization_barrier((far[1], *queries))
    far_all = [far[0], far_second, swap_v(far[0]), swap_v(far_second)]
    partial = stale_attention(queries, near_all)
    outs = stale_attention(queries, far_all, near=partial, after=fresh_rows)
    returned = [outs[0]] + [None] * 7
    for p, k in ((1, 0), (1, 1), (1, 3), (1, 2), (0, 1), (0, 3), (0, 2)):
        r = (4 - k) % 4
        returned[4 * p + k] = to_peer(outs[4 * p + r], p, r)
    attended = merge(u, s, fresh_out, fresh_rows, returned)
    return (
        attended,
        fresh_keys.reshape(B, TOK, WIDTH),
        fresh_values.reshape(B, TOK, WIDTH),
    )


def solution(mesh):
    in_specs = (
        P(None, "patch", "tp"),
        P(),
        P(),
        P(None, "tp"),
        P(None, "tp"),
        P(None, "tp"),
        P("tp"),
        P("tp"),
        P("patch"),
        P(None, "patch", "tp"),
        P(None, "patch", "tp"),
    )
    out_specs = (P(None, "patch", "tp"), P(None, "patch", "tp"), P(None, "patch", "tp"))
    return jax.shard_map(shards, mesh=mesh, in_specs=in_specs, out_specs=out_specs, check_vma=False)
```

```python
import functools
import math

import jax
import jax.numpy as jnp
import numpy as np
from jax import lax
from jax.experimental import pallas as pl
from jax.experimental.pallas import tpu as pltpu
from jax.sharding import PartitionSpec as P

D = 5120
HEADS = 20
HD = 128
FRAMES = 3
GRID_W = 48
EPS = 1e-06
MASKED = -1e30
NY, NX, NZ = 4, 4, 2
TP = 4
N_PATCH = NY * NX * NZ
TOK = 144
B = 2
ROWS = B * TOK
LOCAL_HEADS = 5
WIDTH = LOCAL_HEADS * HD
CHUNK = D // TP
STAT_LANES = 384
PIECE = 5 * TOK
MSG_ROWS = 2 * TOK + 16
SCORE_SCALE = math.log2(math.e) / math.sqrt(HD)
F32 = jnp.float32
BF16 = jnp.bfloat16
AXES = ("patch", "tp")
VMEM_MIB = 40


def params(mib):
    return pltpu.CompilerParams(vmem_limit_bytes=mib * 1024 * 1024)


def vmem():
    return pl.BlockSpec(memory_space=pltpu.VMEM)


def smem():
    return pl.BlockSpec(memory_space=pltpu.SMEM)


def linear(u, v, z_hi, z_lo, core):
    y, x = (u, v) if core == 0 else (v, u)
    return ((y * NX + x) * NZ + z_hi) * TP + z_lo * 2 + core


def places():
    return [
        (u, v, h, l, c)
        for u in range(4)
        for v in range(4)
        for h in range(2)
        for l in range(2)
        for c in range(2)
    ]


def permute(value, move):
    return lax.ppermute(value, AXES, [(linear(*p), linear(*move(*p))) for p in places()])


def shift_u(value, k):
    return permute(value, lambda u, v, h, l, c: ((u + k) % 4, v, h, l, c))


def shift_v(value, k):
    return permute(value, lambda u, v, h, l, c: (u, (v + k) % 4, h, l, c))


def swap_z_hi(value):
    return permute(value, lambda u, v, h, l, c: (u, v, 1 - h, l, c))


def swap_tp(value, z, core):
    if core:
        return permute(value, lambda u, v, h, l, c: (v, u, h, l ^ z, 1 - c))
    return permute(value, lambda u, v, h, l, c: (u, v, h, l ^ z, c))


def frequencies():
    half_dim = HD // 2
    third_dim = half_dim // 3
    frame_pairs = half_dim - 2 * third_dim
    pair = np.arange(HD) // 2
    offset = np.where(
        pair < frame_pairs,
        pair,
        np.where(pair < frame_pairs + third_dim, pair - frame_pairs, pair - frame_pairs - third_dim),
    )
    width = np.where(pair < frame_pairs, 2 * frame_pairs, 2 * third_dim)
    return np.exp(-math.log(10000.0) * 2.0 * offset / width).astype(np.float32).reshape(1, HD)


def columns_to_rows(first, second):
    lane = lax.broadcasted_iota(jnp.int32, (ROWS, 128), 1)
    both = jnp.where(lane == 0, first, jnp.where(lane == 1, second, 0.0))
    padded = jnp.concatenate([both, jnp.zeros((STAT_LANES - ROWS, 128), F32)], axis=0)
    return padded.T[0:8]


def row_to_column(row):
    return jnp.broadcast_to(row, (128, STAT_LANES)).T[0:ROWS]


def pack_kernel(u_ref, key_ref, value_ref, *outs):
    for k in range(5):
        head = lax.rem(u_ref[0] + k, 4) if k < 4 else 4
        cols = pl.ds(pl.multiple_of(head * HD, HD), HD)
        for n, source in enumerate((key_ref, value_ref)):
            for s in range(B):
                outs[k][s, n] = source[s, :, cols]


def pack_stale(u, stale_keys, stale_values):
    return pl.pallas_call(
        pack_kernel,
        out_shape=[jax.ShapeDtypeStruct((B, 2, TOK, HD), BF16)] * 5,
        in_specs=[smem(), vmem(), vmem()],
        out_specs=[vmem()] * 5,
        compiler_params=params(VMEM_MIB),
        cost_estimate=pl.CostEstimate(
            flops=0, bytes_accessed=8 * ROWS * WIDTH, transcendentals=0
        ),
        name="pack_stale",
    )(u, stale_keys, stale_values)


def tables_kernel(place_hbm, freq, after, cond, cos, sin, places_s, place_ref, sem):
    copy = pltpu.make_async_copy(place_hbm, place_ref, sem.at[0])
    copy.start()
    copy.wait()
    for row in range(TOK):
        places_s[row : row + 1] = jnp.full((1, HD), place_ref[row], jnp.int32)
    place = places_s[...]
    frame_tok = TOK * N_PATCH // FRAMES
    frame = jnp.where(place >= frame_tok, 1, 0) + jnp.where(place >= 2 * frame_tok, 1, 0)
    within = place - frame * frame_tok
    grid_row = ((within.astype(F32) + 0.5) * (1.0 / GRID_W)).astype(jnp.int32)
    grid_col = within - grid_row * GRID_W
    lane = lax.broadcasted_iota(jnp.int32, (TOK, HD), 1)
    third = 2 * (HD // 6)
    frame_lanes = HD - 2 * third
    position = jnp.where(
        lane < frame_lanes, frame, jnp.where(lane < frame_lanes + third, grid_row, grid_col)
    )
    angles = position.astype(F32) * freq[...]
    cos[...] = jnp.cos(angles)
    sine = jnp.sin(angles)
    sin[...] = jnp.where(lane % 2 == 0, -sine, sine)
    flag = jnp.where((frame == 0) | (frame == FRAMES - 1), 1.0, 0.0)
    cond[0:TOK] = flag
    cond[TOK:ROWS] = flag


def tables(token_place, after):
    table = jax.ShapeDtypeStruct((TOK, HD), F32)
    return pl.pallas_call(
        tables_kernel,
        out_shape=[jax.ShapeDtypeStruct((ROWS, HD), F32), table, table],
        in_specs=[
            pl.BlockSpec(memory_space=pltpu.HBM),
            vmem(),
            pl.BlockSpec(memory_space=pl.ANY),
        ],
        out_specs=[vmem()] * 3,
        scratch_shapes=[
            pltpu.VMEM((TOK, HD), jnp.int32),
            pltpu.SMEM((TOK,), jnp.int32),
            pltpu.SemaphoreType.DMA((1,)),
        ],
        compiler_params=params(VMEM_MIB),
        cost_estimate=pl.CostEstimate(
            flops=100 * TOK * HD, bytes_accessed=16 * TOK * HD, transcendentals=0
        ),
        name="tables",
    )(token_place, jnp.asarray(frequencies()), after)


def assemble_kernel(*refs):
    parts, out = refs[0:5], refs[5]
    for s in range(B):
        for n in range(2):
            for r in range(5):
                out[s, n, r * TOK : (r + 1) * TOK] = parts[r][s, n]


def assemble(parts):
    return pl.pallas_call(
        assemble_kernel,
        out_shape=jax.ShapeDtypeStruct((B, 2, PIECE, HD), BF16),
        in_specs=[vmem()] * 5,
        out_specs=vmem(),
        compiler_params=params(VMEM_MIB),
        cost_estimate=pl.CostEstimate(
            flops=0, bytes_accessed=16 * PIECE * HD, transcendentals=0
        ),
        name="assemble",
    )(*parts)


def modulate_kernel(t_ref, h0, h1, h2, h3, cond, shift, scale, out_ref):
    chunks = (h0, h1, h2, h3)
    total = jnp.zeros((ROWS, 1), F32)
    for chunk in chunks:
        total = total + jnp.sum(chunk[...].astype(F32), axis=1, keepdims=True)
    mean = total * (1.0 / D)
    deviation = jnp.zeros((ROWS, 1), F32)
    for chunk in chunks:
        centered = chunk[...].astype(F32) - mean
        deviation = deviation + jnp.sum(centered * centered, axis=1, keepdims=True)
    rstd = lax.rsqrt(deviation * (1.0 / D) + EPS)
    conditioned = cond[:, 0:1] > 0.5
    for c in range(TP):
        cols = pl.ds(pl.multiple_of(t_ref[c] * CHUNK, CHUNK), CHUNK)
        part = chunks[c][...].astype(F32)
        gain = jnp.where(conditioned, scale[1:2, cols], scale[0:1, cols])
        bias = jnp.where(conditioned, shift[1:2, cols], shift[0:1, cols])
        out_ref[:, cols] = ((part - mean) * rstd * (1.0 + gain) + bias).astype(BF16)


def modulate(blocks, chunks, cond, shift, scale):
    return pl.pallas_call(
        modulate_kernel,
        out_shape=jax.ShapeDtypeStruct((ROWS, D), BF16),
        in_specs=[smem()] + [vmem()] * 7,
        out_specs=vmem(),
        compiler_params=params(VMEM_MIB),
        cost_estimate=pl.CostEstimate(
            flops=12 * ROWS * D, bytes_accessed=4 * ROWS * D, transcendentals=0
        ),
        name="modulate",
    )(blocks, *chunks, cond, shift, scale)


def squares_kernel(q_ref, k_ref, out_ref):
    query, key = q_ref[...], k_ref[...]
    out_ref[...] = columns_to_rows(
        jnp.sum(query * query, axis=1, keepdims=True),
        jnp.sum(key * key, axis=1, keepdims=True),
    )


def sum_squares(query, key):
    return pl.pallas_call(
        squares_kernel,
        out_shape=jax.ShapeDtypeStruct((8, STAT_LANES), F32),
        in_specs=[vmem()] * 2,
        out_specs=vmem(),
        compiler_params=params(VMEM_MIB),
        cost_estimate=pl.CostEstimate(
            flops=4 * ROWS * WIDTH, bytes_accessed=8 * ROWS * WIDTH, transcendentals=0
        ),
        name="sum_squares",
    )(query, key)


def rope_kernel(u_ref, q_ref, k_ref, s0, s1, s2, s3, qg, kg, cos, sin, k_all, *refs):
    sends, q_rot = refs[0:4], refs[4]
    total = s0[...] + s1[...] + s2[...] + s3[...]
    inverse = lax.rsqrt(total * (1.0 / (HEADS * HD)) + EPS)
    even = lax.broadcasted_iota(jnp.int32, (ROWS, HD), 1) % 2 == 0
    cos_rows = jnp.concatenate([cos[...], cos[...]], axis=0)
    sin_rows = jnp.concatenate([sin[...], sin[...]], axis=0)

    def rotate(ref, column, gain, cols):
        part = ref[:, cols] * column * gain[cols].reshape(1, HD)
        swap = jnp.where(even, pltpu.roll(part, HD - 1, 1), pltpu.roll(part, 1, 1))
        return (part * cos_rows + swap * sin_rows).astype(BF16)

    q_column = row_to_column(inverse[0:1])
    k_column = row_to_column(inverse[1:2])
    for head in range(LOCAL_HEADS):
        cols = slice(head * HD, (head + 1) * HD)
        query = rotate(q_ref, q_column, qg, cols)
        for s in range(B):
            q_rot[head, s] = query[s * TOK : (s + 1) * TOK]
        k_all[:, cols] = rotate(k_ref, k_column, kg, cols)
    for k in range(4):
        for s in range(B):
            sends[k][s, 0] = q_rot[lax.rem(u_ref[0] + k, 4), s]
            sends[k][s, 1] = q_rot[4, s]


def norm_rope(u, query, key, squares, q_gain, k_gain, cos, sin):
    send = jax.ShapeDtypeStruct((B, 2, TOK, HD), BF16)
    flat = jax.ShapeDtypeStruct((ROWS, WIDTH), BF16)
    return pl.pallas_call(
        rope_kernel,
        out_shape=[flat] + [send] * 4,
        in_specs=[smem()] + [vmem()] * 10,
        out_specs=[vmem()] * 5,
        scratch_shapes=[pltpu.VMEM((LOCAL_HEADS, B, TOK, HD), BF16)],
        compiler_params=params(VMEM_MIB),
        cost_estimate=pl.CostEstimate(
            flops=20 * ROWS * WIDTH, bytes_accessed=16 * ROWS * WIDTH, transcendentals=0
        ),
        name="norm_rope",
    )(u, query, key, *squares, q_gain, k_gain, cos, sin)


def scores_of(query, keys):
    return lax.dot_general(query, keys, (((1,), (1,)), ((), ())), preferred_element_type=F32)


def to_rows(blocks):
    lane = lax.broadcasted_iota(jnp.int32, (HD, HD), 1)
    table = jnp.zeros((HD, HD), F32)
    empty = jnp.zeros((2 * HD - TOK, HD), F32)
    for n, block in enumerate(blocks):
        rest = jnp.concatenate([block[HD:TOK], empty], axis=0)
        table = jnp.where(lane == 2 * n, block[0:HD], table)
        table = jnp.where(lane == 2 * n + 1, rest, table)
    return table.T


FRESH_ROWS = 24


def fresh_kernel(u_ref, k_ref, v_ref, *refs):
    queries, (out_ref, rows_ref) = refs[0:4], refs[4:6]
    lses = []
    for s in range(B):
        rows = slice(s * TOK, (s + 1) * TOK)
        for k in range(LOCAL_HEADS):
            head = lax.rem(u_ref[0] + k, 4) if k < 4 else 4
            cols = pl.ds(pl.multiple_of(head * HD, HD), HD)
            query = queries[k][s, 0] if k < 4 else queries[0][s, 1]
            scores = scores_of(query, k_ref[rows, cols])
            top = jnp.max(scores, axis=1, keepdims=True)
            probs = jnp.exp2((scores - top) * SCORE_SCALE)
            total = jnp.sum(probs, axis=1, keepdims=True)
            out = jnp.dot(probs.astype(BF16), v_ref[rows, cols], preferred_element_type=F32)
            out_ref[s, k] = out / total
            lses.append(jnp.broadcast_to(top * SCORE_SCALE + jnp.log2(total), (TOK, HD)))
    rows_ref[...] = to_rows(lses)[0:FRESH_ROWS]


def fresh_attention(u, key, value, queries):
    return pl.pallas_call(
        fresh_kernel,
        out_shape=[
            jax.ShapeDtypeStruct((B, LOCAL_HEADS, TOK, HD), F32),
            jax.ShapeDtypeStruct((FRESH_ROWS, HD), F32),
        ],
        in_specs=[smem()] + [vmem()] * 6,
        out_specs=[vmem()] * 2,
        compiler_params=params(VMEM_MIB),
        cost_estimate=pl.CostEstimate(
            flops=4 * ROWS * TOK * WIDTH,
            bytes_accessed=14 * ROWS * WIDTH,
            transcendentals=ROWS * TOK * LOCAL_HEADS,
        ),
        name="fresh_attention",
    )(u, key, value, *queries)


TILE = 2 * TOK
GROUP = 16
PER_PIECE = 4 * TOK
KEYS = 4 * PER_PIECE
KEYS_LAST = 4 * TOK
SPLIT = 768


def stale_kernel(far, *refs):
    queries = refs[0:4]
    pieces, rest = refs[4:8], refs[8:]
    if far:
        near_out, near_lse = rest[0:2]
        msgs = rest[3:7]
    else:
        out_ref, lse_ref = rest[0:2]
    lse_s, acc_s, k_main, v_main, k_last, v_last, scores_s, probs_s, sems = rest[-9:]
    copies = ([], [])
    for s in range(B):
        for n in range(4):
            piece = pieces[n].at[s]
            main, last = pl.ds(n * PER_PIECE, PER_PIECE), pl.ds(n * TOK, TOK)
            head, tail = pl.ds(0, PER_PIECE), pl.ds(PER_PIECE, TOK)
            for kind, part, target, rows in (
                (0, head, k_main, main),
                (0, tail, k_last, last),
                (1, head, v_main, main),
                (1, tail, v_last, last),
            ):
                copy = pltpu.make_async_copy(
                    piece.at[kind, part], target.at[s, rows], sems.at[s, len(copies[s])]
                )
                copy.start()
                copies[s].append(copy)

    jobs = [(s, e, tile) for s in range(B) for e in range(2) for tile in range(2)]

    def size(i):
        return KEYS_LAST if jobs[i][1] else KEYS

    def score_steps(i):
        s, e, tile = jobs[i]
        keys = k_last if e else k_main
        out = scores_s.at[i % 2]

        def arrive():
            for copy in copies[s]:
                copy.wait()

        def step(at, end):
            query = jnp.concatenate([queries[2 * tile][s, e], queries[2 * tile + 1][s, e]], axis=0)
            out[:, at:end] = scores_of(query, keys[s, at:end])

        def hide():
            for n in range(2):
                r = 2 * tile + n
                rows = slice(n * TOK, (n + 1) * TOK)
                if e and r:
                    continue
                out[rows, r * TOK : (r + 1) * TOK] = jnp.full((TOK, TOK), MASKED, F32)

        steps = [] if i % 4 else [arrive]
        for at in range(0, size(i), SPLIT):
            steps.append(functools.partial(step, at, min(at + SPLIT, size(i))))
        return steps if far else steps + [hide]

    def softmax_steps(i, tops, totals):
        def step(row):
            rows = slice(row, row + GROUP)
            part = scores_s[i % 2, rows, 0 : size(i)]
            top = jnp.max(part, axis=1, keepdims=True)
            probs = jnp.exp2((part - top) * SCORE_SCALE)
            totals.append(jnp.sum(probs, axis=1, keepdims=True))
            tops.append(top)
            probs_s[i % 2, rows, 0 : size(i)] = probs.astype(BF16)

        return [functools.partial(step, row) for row in range(0, TILE, GROUP)]

    def product_steps(i, tops, totals):
        s, e, tile = jobs[i]
        values = v_last if e else v_main

        def step(at, end):
            part = jnp.dot(
                probs_s[i % 2, :, at:end], values[s, at:end], preferred_element_type=F32
            )
            acc_s[...] = part if at == 0 else acc_s[...] + part

        def finish():
            top, total = jnp.concatenate(tops, axis=0), jnp.concatenate(totals, axis=0)
            out = acc_s[...] / total
            lse = top * SCORE_SCALE + jnp.log2(total)
            for n in range(2):
                r = 2 * tile + n
                half = slice(n * TOK, (n + 1) * TOK)
                if not far:
                    out_ref[s, r, e] = out[half]
                    lse_ref[s, r, e] = jnp.broadcast_to(lse[half], (TOK, HD))
                    continue
                lse_near = near_lse[s, r, e][:, 0:1]
                high = jnp.maximum(lse[half], lse_near)
                weight, weight_near = jnp.exp2(lse[half] - high), jnp.exp2(lse_near - high)
                both = weight + weight_near
                value = (out[half] * weight + near_out[s, r, e] * weight_near) / both
                lse_s[s, r, e] = jnp.broadcast_to(high + jnp.log2(both), (TOK, HD))
                msgs[r][s, e * TOK : (e + 1) * TOK] = value.astype(BF16)

        steps = []
        for at in range(0, size(i), SPLIT):
            steps.append(functools.partial(step, at, min(at + SPLIT, size(i))))
        return steps + [finish]

    def weave(*lists):
        order = []
        for steps in lists:
            order += [((n + 0.5) / len(steps), step) for n, step in enumerate(steps)]
        for _, step in sorted(order, key=lambda entry: entry[0]):
            step()

    weave(score_steps(0))
    pending = None
    for i in range(len(jobs)):
        tops, totals = [], []
        lists = [softmax_steps(i, tops, totals)]
        if i + 1 < len(jobs):
            lists.append(score_steps(i + 1))
        if pending is not None:
            lists.append(pending)
        weave(*lists)
        pending = product_steps(i, tops, totals)
    weave(pending)

    if far:
        order = [(r, s) for r in range(4) for s in range(B)]
        flat = to_rows([lse_s[s, r, e] for r, s in order for e in range(2)])
        for n, (r, s) in enumerate(order):
            part = flat[n * 4 : n * 4 + 4]
            high = part.astype(BF16).astype(F32)
            middle = (part - high).astype(BF16).astype(F32)
            low = part - high - middle
            stack = jnp.concatenate([high, middle, low, jnp.zeros((4, HD), F32)], axis=0)
            msgs[r][s, 2 * TOK : MSG_ROWS] = stack.astype(BF16)


def stale_attention(queries, pieces, near=None, after=None):
    far = near is not None
    args = [*queries, *pieces]
    hbm = pl.BlockSpec(memory_space=pltpu.HBM)
    in_specs = [vmem()] * 4 + [hbm] * len(pieces)
    if far:
        args += [*near, after]
        in_specs += [vmem(), vmem(), pl.BlockSpec(memory_space=pl.ANY)]
        out_shape = [jax.ShapeDtypeStruct((B, MSG_ROWS, HD), BF16)] * 4
    else:
        out_shape = [jax.ShapeDtypeStruct((B, 4, 2, TOK, HD), F32)] * 2
    work = B * 4 * TOK * (KEYS + KEYS_LAST)
    return pl.pallas_call(
        functools.partial(stale_kernel, far),
        out_shape=out_shape,
        in_specs=in_specs,
        out_specs=[vmem()] * len(out_shape),
        scratch_shapes=[
            pltpu.VMEM((B, 4, 2, TOK, HD), F32),
            pltpu.VMEM((TILE, HD), F32),
            pltpu.VMEM((B, KEYS, HD), BF16),
            pltpu.VMEM((B, KEYS, HD), BF16),
            pltpu.VMEM((B, KEYS_LAST, HD), BF16),
            pltpu.VMEM((B, KEYS_LAST, HD), BF16),
            pltpu.VMEM((2, TILE, KEYS), F32),
            pltpu.VMEM((2, TILE, KEYS), BF16),
            pltpu.SemaphoreType.DMA((B, 16)),
        ],
        compiler_params=params(VMEM_MIB),
        cost_estimate=pl.CostEstimate(
            flops=4 * work * HD, bytes_accessed=8 * (KEYS + KEYS_LAST) * HD, transcendentals=work
        ),
        name="far_attention" if far else "near_attention",
    )(*args)


def merge_kernel(u_ref, fresh_out, fresh_rows, *refs):
    msgs, out_ref = refs[0:4], refs[4]
    lses = {}
    for k in range(4):
        for s in range(B):
            stack = msgs[k][s, 2 * TOK : MSG_ROWS].astype(F32)
            lses[s, k] = stack[0:4] + stack[4:8] + stack[8:12]
    weights, jobs = [], []
    for s in range(B):
        for k in range(LOCAL_HEADS):
            at = (s * LOCAL_HEADS + k) * 2
            parts = [(None, fresh_rows[at : at + 2])]
            if k < 4:
                parts.append((k, lses[s, k][0:2]))
            else:
                parts += [(n, lses[s, n][2:4]) for n in range(4)]
            top = parts[0][1]
            for _, lse in parts[1:]:
                top = jnp.maximum(top, lse)
            raw = [jnp.exp2(lse - top) for _, lse in parts]
            total = sum(raw[1:], raw[0])
            jobs.append((s, k, [(source, len(weights) + n) for n, (source, _) in enumerate(parts)]))
            weights += [one / total for one in raw]
    filler = jnp.zeros((HD - 2 * len(weights), HD), F32)
    table = jnp.concatenate(weights + [filler], axis=0).T
    for s, k, parts in jobs:
        head = lax.rem(u_ref[0] + k, 4) if k < 4 else 4
        out = [None, None]
        for source, n in parts:
            for half, rows in enumerate((slice(0, HD), slice(HD, TOK))):
                if source is None:
                    value = fresh_out[s, k, rows]
                else:
                    at = 0 if k < 4 else TOK
                    value = msgs[source][s, at + rows.start : at + rows.stop].astype(F32)
                column = table[0 : rows.stop - rows.start, 2 * n + half : 2 * n + half + 1]
                term = value * column
                out[half] = term if out[half] is None else out[half] + term
        cols = pl.ds(pl.multiple_of(head * HD, HD), HD)
        out_ref[s, :, cols] = jnp.concatenate(out, axis=0).astype(BF16)


def merge(u, fresh_out, fresh_rows, msgs):
    return pl.pallas_call(
        merge_kernel,
        out_shape=jax.ShapeDtypeStruct((B, TOK, WIDTH), BF16),
        in_specs=[smem()] + [vmem()] * 6,
        out_specs=vmem(),
        compiler_params=params(VMEM_MIB),
        cost_estimate=pl.CostEstimate(
            flops=10 * ROWS * WIDTH, bytes_accessed=14 * ROWS * WIDTH, transcendentals=0
        ),
        name="merge",
    )(u, fresh_out, fresh_rows, *msgs)


def gather_v(piece):
    return [piece, shift_v(piece, 3), shift_v(piece, 1), shift_v(piece, 2)]


def shards(
    hidden,
    mod_shift,
    mod_scale,
    w_query,
    w_key,
    w_value,
    q_gain,
    k_gain,
    token_place,
    stale_keys,
    stale_values,
):
    patch = lax.axis_index("patch")
    tp = lax.axis_index("tp")
    y = patch // (NX * NZ)
    x = (patch // NZ) % NX
    u = jnp.where(tp % 2 == 0, y, x).astype(jnp.int32).reshape(1)
    own_rows = hidden.reshape(ROWS, CHUNK)
    z_rows = swap_tp(own_rows, 1, 0)
    core_rows = swap_tp(own_rows, 0, 1)

    packed = pack_stale(u, stale_keys, stale_values)
    arrived = [packed[0]] + [shift_u(packed[4 - r], 4 - r) for r in range(1, 4)]
    near = assemble([*arrived, packed[4]])
    near_all = gather_v(near)
    far = swap_z_hi(near)
    cond, cos, sin = tables(token_place, near)

    z_rows, cond = lax.optimization_barrier((z_rows, cond))
    cross_rows = swap_tp(z_rows, 0, 1)
    blocks = jnp.stack([tp, tp ^ 1, tp ^ 2, tp ^ 3]).astype(jnp.int32)
    rows = [own_rows, core_rows, z_rows, cross_rows]
    modded = modulate(blocks, rows, cond, mod_shift, mod_scale)
    query = jnp.dot(modded, w_query, preferred_element_type=F32)
    key = jnp.dot(modded, w_key, preferred_element_type=F32)
    fresh_values = jnp.dot(modded, w_value, preferred_element_type=F32).astype(BF16)
    own_sq = sum_squares(query, key)
    own_sq, *near_all = lax.optimization_barrier((own_sq, *near_all))
    squares = [own_sq] + [swap_tp(own_sq, z, c) for z, c in ((1, 0), (1, 1), (0, 1))]
    fresh_keys, *sends = norm_rope(u, query, key, squares, q_gain, k_gain, cos, sin)
    queries = [sends[0]] + [shift_u(sends[4 - r], 4 - r) for r in (1, 3, 2)]
    queries = [queries[0], queries[1], queries[3], queries[2]]
    fresh_out, fresh_rows = fresh_attention(u, fresh_keys, fresh_values, sends)

    far, fresh_rows, *queries = lax.optimization_barrier((far, fresh_rows, *queries))
    far_all = gather_v(far)
    partial = stale_attention(queries, near_all)
    outs = stale_attention(queries, far_all, near=partial, after=fresh_rows)
    returned = [outs[0]] + [shift_u(outs[4 - k], 4 - k) for k in range(1, 4)]
    attended = merge(u, fresh_out, fresh_rows, returned)
    return (
        attended,
        fresh_keys.reshape(B, TOK, WIDTH),
        fresh_values.reshape(B, TOK, WIDTH),
    )


def solution(mesh):
    in_specs = (
        P(None, "patch", "tp"),
        P(),
        P(),
        P(None, "tp"),
        P(None, "tp"),
        P(None, "tp"),
        P("tp"),
        P("tp"),
        P("patch"),
        P(None, "patch", "tp"),
        P(None, "patch", "tp"),
    )
    out_specs = (P(None, "patch", "tp"), P(None, "patch", "tp"), P(None, "patch", "tp"))
    return jax.shard_map(shards, mesh=mesh, in_specs=in_specs, out_specs=out_specs, check_vma=False)
```

```python
import functools
import math

import jax
import jax.numpy as jnp
import numpy as np
from jax import lax
from jax.experimental import pallas as pl
from jax.experimental.pallas import tpu as pltpu
from jax.sharding import PartitionSpec as P

D = 5120
HEADS = 20
HD = 128
FRAMES = 3
GRID_W = 48
EPS = 1e-06
MASKED = -1e30
NY, NX, NZ = 4, 4, 2
TP = 4
N_PATCH = NY * NX * NZ
TOK = 144
B = 2
ROWS = B * TOK
LOCAL_HEADS = 5
WIDTH = LOCAL_HEADS * HD
CHUNK = D // TP
STAT_LANES = 384
PIECE = 5 * TOK
MSG_ROWS = 2 * TOK + 16
SCORE_SCALE = math.log2(math.e) / math.sqrt(HD)
F32 = jnp.float32
BF16 = jnp.bfloat16
AXES = ("patch", "tp")
GROUP = 16
VMEM_MIB = 24
ATTENTION_MIB = 34


def params(mib):
    return pltpu.CompilerParams(vmem_limit_bytes=mib * 1024 * 1024)


def vmem():
    return pl.BlockSpec(memory_space=pltpu.VMEM)


def smem():
    return pl.BlockSpec(memory_space=pltpu.SMEM)


def linear(u, v, z_hi, z_lo, core):
    y, x = (u, v) if core == 0 else (v, u)
    return ((y * NX + x) * NZ + z_hi) * TP + z_lo * 2 + core


def places():
    return [
        (u, v, h, l, c)
        for u in range(4)
        for v in range(4)
        for h in range(2)
        for l in range(2)
        for c in range(2)
    ]


def permute(value, move):
    return lax.ppermute(value, AXES, [(linear(*p), linear(*move(*p))) for p in places()])


def shift_u(value, k):
    return permute(value, lambda u, v, h, l, c: ((u + k) % 4, v, h, l, c))


def swap_v(value, mask):
    return permute(value, lambda u, v, h, l, c: (u, v ^ mask, h, l, c))


def exchange_u(values):
    came = {r: shift_u(values[4 - r], 4 - r) for r in (2, 1, 3)}
    return [values[0], came[1], came[2], came[3]]


def swap_z_hi(value):
    return permute(value, lambda u, v, h, l, c: (u, v, 1 - h, l, c))


def swap_tp(value, z, core):
    if core:
        return permute(value, lambda u, v, h, l, c: (v, u, h, l ^ z, 1 - c))
    return permute(value, lambda u, v, h, l, c: (u, v, h, l ^ z, c))


def frequencies():
    half_dim = HD // 2
    third_dim = half_dim // 3
    frame_pairs = half_dim - 2 * third_dim
    pair = np.arange(HD) // 2
    offset = np.where(
        pair < frame_pairs,
        pair,
        np.where(pair < frame_pairs + third_dim, pair - frame_pairs, pair - frame_pairs - third_dim),
    )
    width = np.where(pair < frame_pairs, 2 * frame_pairs, 2 * third_dim)
    return np.exp(-math.log(10000.0) * 2.0 * offset / width).astype(np.float32).reshape(1, HD)


def columns_to_rows(first, second):
    lane = lax.broadcasted_iota(jnp.int32, (ROWS, 128), 1)
    both = jnp.where(lane == 0, first, jnp.where(lane == 1, second, 0.0))
    padded = jnp.concatenate([both, jnp.zeros((STAT_LANES - ROWS, 128), F32)], axis=0)
    return padded.T[0:8]


def row_to_column(row):
    return jnp.broadcast_to(row, (128, STAT_LANES)).T[0:ROWS]


def pack_kernel(u_ref, key_ref, value_ref, *outs):
    for k in range(5):
        head = lax.rem(u_ref[0] + k, 4) if k < 4 else 4
        cols = pl.ds(pl.multiple_of(head * HD, HD), HD)
        for n, source in enumerate((key_ref, value_ref)):
            for s in range(B):
                outs[k][s, n] = source[s, :, cols]


def pack_stale(u, stale_keys, stale_values):
    return pl.pallas_call(
        pack_kernel,
        out_shape=[jax.ShapeDtypeStruct((B, 2, TOK, HD), BF16)] * 5,
        in_specs=[smem(), vmem(), vmem()],
        out_specs=[vmem()] * 5,
        compiler_params=params(VMEM_MIB),
        cost_estimate=pl.CostEstimate(
            flops=0, bytes_accessed=8 * ROWS * WIDTH, transcendentals=0
        ),
        name="pack_stale",
    )(u, stale_keys, stale_values)


def tables_kernel(place_hbm, freq, rows, shift, scale, after, *refs):
    cond, cos, sin, mod, rows_out, places_s, place_ref, sem = refs
    copy = pltpu.make_async_copy(place_hbm, place_ref, sem.at[0])
    copy.start()
    copy.wait()
    for row in range(TOK):
        places_s[row : row + 1] = jnp.full((1, HD), place_ref[row], jnp.int32)
    place = places_s[...]
    frame_tok = TOK * N_PATCH // FRAMES
    frame = jnp.where(place >= frame_tok, 1, 0) + jnp.where(place >= 2 * frame_tok, 1, 0)
    within = place - frame * frame_tok
    grid_row = ((within.astype(F32) + 0.5) * (1.0 / GRID_W)).astype(jnp.int32)
    grid_col = within - grid_row * GRID_W
    lane = lax.broadcasted_iota(jnp.int32, (TOK, HD), 1)
    third = 2 * (HD // 6)
    frame_lanes = HD - 2 * third
    position = jnp.where(
        lane < frame_lanes, frame, jnp.where(lane < frame_lanes + third, grid_row, grid_col)
    )
    angles = position.astype(F32) * freq[...]
    cos[...] = jnp.cos(angles)
    sine = jnp.sin(angles)
    sin[...] = jnp.where(lane % 2 == 0, -sine, sine)
    flag = jnp.where((frame == 0) | (frame == FRAMES - 1), 1.0, 0.0)
    cond[0:TOK] = flag
    cond[TOK:ROWS] = flag
    mod[0:2] = 1.0 + scale[...]
    mod[2:4] = shift[...]
    rows_out[...] = rows[...]


def tables(token_place, rows, shift, scale, after):
    table = jax.ShapeDtypeStruct((TOK, HD), F32)
    return pl.pallas_call(
        tables_kernel,
        out_shape=[
            jax.ShapeDtypeStruct((ROWS, HD), F32),
            table,
            table,
            jax.ShapeDtypeStruct((4, D), F32),
            jax.ShapeDtypeStruct((ROWS, CHUNK), BF16),
        ],
        in_specs=[pl.BlockSpec(memory_space=pltpu.HBM)]
        + [vmem()] * 4
        + [pl.BlockSpec(memory_space=pl.ANY)],
        out_specs=[vmem()] * 5,
        scratch_shapes=[
            pltpu.VMEM((TOK, HD), jnp.int32),
            pltpu.SMEM((TOK,), jnp.int32),
            pltpu.SemaphoreType.DMA((1,)),
        ],
        compiler_params=params(VMEM_MIB),
        cost_estimate=pl.CostEstimate(
            flops=100 * TOK * HD, bytes_accessed=40_000_000, transcendentals=0
        ),
        name="tables",
    )(token_place, jnp.asarray(frequencies()), rows, shift, scale, after)


def assemble_kernel(*refs):
    parts, out = refs[0:5], refs[5]
    for s in range(B):
        for n in range(2):
            for r in range(5):
                out[s, n, r * TOK : (r + 1) * TOK] = parts[r][s, n]


def assemble(parts):
    return pl.pallas_call(
        assemble_kernel,
        out_shape=jax.ShapeDtypeStruct((B, 2, PIECE, HD), BF16),
        in_specs=[vmem()] * 5,
        out_specs=vmem(),
        compiler_params=params(VMEM_MIB),
        cost_estimate=pl.CostEstimate(
            flops=0, bytes_accessed=16 * PIECE * HD, transcendentals=0
        ),
        name="assemble",
    )(*parts)


def modulate_kernel(t_ref, h0, h1, h2, h3, cond, mod, out_ref):
    chunks = (h0, h1, h2, h3)
    for row in range(0, ROWS, GROUP):
        rows = slice(row, row + GROUP)
        total = jnp.zeros((GROUP, 1), F32)
        for chunk in chunks:
            total = total + jnp.sum(chunk[rows].astype(F32), axis=1, keepdims=True)
        mean = total * (1.0 / D)
        deviation = jnp.zeros((GROUP, 1), F32)
        for chunk in chunks:
            centered = chunk[rows].astype(F32) - mean
            deviation = deviation + jnp.sum(centered * centered, axis=1, keepdims=True)
        rstd = lax.rsqrt(deviation * (1.0 / D) + EPS)
        conditioned = cond[rows, 0:1] > 0.5
        for c in range(TP):
            cols = pl.ds(pl.multiple_of(t_ref[c] * CHUNK, CHUNK), CHUNK)
            gain = jnp.where(conditioned, mod[1:2, cols], mod[0:1, cols])
            bias = jnp.where(conditioned, mod[3:4, cols], mod[2:3, cols])
            normed = (chunks[c][rows].astype(F32) - mean) * rstd
            out_ref[rows, cols] = (normed * gain + bias).astype(BF16)


def modulate(blocks, chunks, cond, mod):
    return pl.pallas_call(
        modulate_kernel,
        out_shape=jax.ShapeDtypeStruct((ROWS, D), BF16),
        in_specs=[smem()] + [vmem()] * 6,
        out_specs=vmem(),
        compiler_params=params(VMEM_MIB),
        cost_estimate=pl.CostEstimate(
            flops=12 * ROWS * D, bytes_accessed=20_000_000, transcendentals=0
        ),
        name="modulate",
    )(blocks, *chunks, cond, mod)


def squares_kernel(q_ref, k_ref, out_ref):
    query, key = q_ref[...], k_ref[...]
    out_ref[...] = columns_to_rows(
        jnp.sum(query * query, axis=1, keepdims=True),
        jnp.sum(key * key, axis=1, keepdims=True),
    )


def sum_squares(query, key):
    return pl.pallas_call(
        squares_kernel,
        out_shape=jax.ShapeDtypeStruct((8, STAT_LANES), F32),
        in_specs=[vmem()] * 2,
        out_specs=vmem(),
        compiler_params=params(VMEM_MIB),
        cost_estimate=pl.CostEstimate(
            flops=4 * ROWS * WIDTH, bytes_accessed=8 * ROWS * WIDTH, transcendentals=0
        ),
        name="sum_squares",
    )(query, key)


def rope_kernel(u_ref, q_ref, k_ref, s0, s1, s2, s3, qg, kg, cos, sin, k_all, *refs):
    sends, q_rot = refs[0:4], refs[4]
    total = s0[...] + s1[...] + s2[...] + s3[...]
    inverse = lax.rsqrt(total * (1.0 / (HEADS * HD)) + EPS)
    even = lax.broadcasted_iota(jnp.int32, (ROWS, HD), 1) % 2 == 0
    cos_rows = jnp.concatenate([cos[...], cos[...]], axis=0)
    sin_rows = jnp.concatenate([sin[...], sin[...]], axis=0)

    def rotate(ref, column, gain, cols):
        part = ref[:, cols] * column * gain[cols].reshape(1, HD)
        swap = jnp.where(even, pltpu.roll(part, HD - 1, 1), pltpu.roll(part, 1, 1))
        return (part * cos_rows + swap * sin_rows).astype(BF16)

    q_column = row_to_column(inverse[0:1])
    k_column = row_to_column(inverse[1:2])
    for head in range(LOCAL_HEADS):
        cols = slice(head * HD, (head + 1) * HD)
        query = rotate(q_ref, q_column, qg, cols)
        for s in range(B):
            q_rot[head, s] = query[s * TOK : (s + 1) * TOK]
        k_all[:, cols] = rotate(k_ref, k_column, kg, cols)
    for k in range(4):
        for s in range(B):
            sends[k][s, 0] = q_rot[lax.rem(u_ref[0] + k, 4), s]
            sends[k][s, 1] = q_rot[4, s]


def norm_rope(u, query, key, squares, q_gain, k_gain, cos, sin):
    send = jax.ShapeDtypeStruct((B, 2, TOK, HD), BF16)
    flat = jax.ShapeDtypeStruct((ROWS, WIDTH), BF16)
    return pl.pallas_call(
        rope_kernel,
        out_shape=[flat] + [send] * 4,
        in_specs=[smem()] + [vmem()] * 10,
        out_specs=[vmem()] * 5,
        scratch_shapes=[pltpu.VMEM((LOCAL_HEADS, B, TOK, HD), BF16)],
        compiler_params=params(VMEM_MIB),
        cost_estimate=pl.CostEstimate(
            flops=20 * ROWS * WIDTH, bytes_accessed=16 * ROWS * WIDTH, transcendentals=0
        ),
        name="norm_rope",
    )(u, query, key, *squares, q_gain, k_gain, cos, sin)


def scores_of(query, keys):
    return lax.dot_general(query, keys, (((1,), (1,)), ((), ())), preferred_element_type=F32)


def to_rows(blocks):
    lane = lax.broadcasted_iota(jnp.int32, (HD, HD), 1)
    table = jnp.zeros((HD, HD), F32)
    empty = jnp.zeros((2 * HD - TOK, HD), F32)
    for n, block in enumerate(blocks):
        rest = jnp.concatenate([block[HD:TOK], empty], axis=0)
        table = jnp.where(lane == 2 * n, block[0:HD], table)
        table = jnp.where(lane == 2 * n + 1, rest, table)
    return table.T


FRESH_ROWS = 24


def fresh_kernel(u_ref, k_ref, v_ref, *refs):
    queries, (out_ref, rows_ref) = refs[0:4], refs[4:6]
    lses = []
    for s in range(B):
        rows = slice(s * TOK, (s + 1) * TOK)
        for k in range(LOCAL_HEADS):
            head = lax.rem(u_ref[0] + k, 4) if k < 4 else 4
            cols = pl.ds(pl.multiple_of(head * HD, HD), HD)
            query = queries[k][s, 0] if k < 4 else queries[0][s, 1]
            scores = scores_of(query, k_ref[rows, cols])
            top = jnp.max(scores, axis=1, keepdims=True)
            probs = jnp.exp2((scores - top) * SCORE_SCALE)
            total = jnp.sum(probs, axis=1, keepdims=True)
            out = jnp.dot(probs.astype(BF16), v_ref[rows, cols], preferred_element_type=F32)
            out_ref[s, k] = out / total
            lses.append(jnp.broadcast_to(top * SCORE_SCALE + jnp.log2(total), (TOK, HD)))
    rows_ref[...] = to_rows(lses)[0:FRESH_ROWS]


def fresh_attention(u, key, value, queries):
    return pl.pallas_call(
        fresh_kernel,
        out_shape=[
            jax.ShapeDtypeStruct((B, LOCAL_HEADS, TOK, HD), F32),
            jax.ShapeDtypeStruct((FRESH_ROWS, HD), F32),
        ],
        in_specs=[smem()] + [vmem()] * 6,
        out_specs=[vmem()] * 2,
        compiler_params=params(VMEM_MIB),
        cost_estimate=pl.CostEstimate(
            flops=4 * ROWS * TOK * WIDTH,
            bytes_accessed=14 * ROWS * WIDTH,
            transcendentals=ROWS * TOK * LOCAL_HEADS,
        ),
        name="fresh_attention",
    )(u, key, value, *queries)


TILE = 2 * TOK
PER_PIECE = 4 * TOK
KEYS = 4 * PER_PIECE
KEYS_LAST = 4 * TOK
SPLIT = 768


def stale_kernel(far, *refs):
    queries = refs[0:4]
    pieces, rest = refs[4:8], refs[8:]
    if far:
        near_out, near_lse = rest[0:2]
        msgs = rest[3:7]
    else:
        out_ref, lse_ref = rest[0:2]
    lse_s, acc_s, k_main, v_main, k_last, v_last, scores_s, probs_s = rest[-8:]

    jobs = [(s, e, tile) for s in range(B) for e in range(2) for tile in range(2)]

    def size(i):
        return KEYS_LAST if jobs[i][1] else KEYS

    def score_steps(i):
        s, e, tile = jobs[i]
        keys = k_last if e else k_main
        out = scores_s.at[i % 2]

        def arrive():
            for n, piece in enumerate(pieces):
                main = slice(n * PER_PIECE, (n + 1) * PER_PIECE)
                last = slice(n * TOK, (n + 1) * TOK)
                k_main[s, main] = piece[s, 0, 0:PER_PIECE]
                k_last[s, last] = piece[s, 0, PER_PIECE:PIECE]
                v_main[s, main] = piece[s, 1, 0:PER_PIECE]
                v_last[s, last] = piece[s, 1, PER_PIECE:PIECE]

        def step(at, end):
            query = jnp.concatenate([queries[2 * tile][s, e], queries[2 * tile + 1][s, e]], axis=0)
            out[:, at:end] = scores_of(query, keys[s, at:end])

        def hide():
            for n in range(2):
                r = 2 * tile + n
                rows = slice(n * TOK, (n + 1) * TOK)
                if e and r:
                    continue
                out[rows, r * TOK : (r + 1) * TOK] = jnp.full((TOK, TOK), MASKED, F32)

        steps = [] if i % 4 else [arrive]
        for at in range(0, size(i), SPLIT):
            steps.append(functools.partial(step, at, min(at + SPLIT, size(i))))
        return steps if far else steps + [hide]

    def softmax_steps(i, tops, totals):
        def step(row):
            rows = slice(row, row + GROUP)
            part = scores_s[i % 2, rows, 0 : size(i)]
            top = jnp.max(part, axis=1, keepdims=True)
            probs = jnp.exp2((part - top) * SCORE_SCALE)
            totals.append(jnp.sum(probs, axis=1, keepdims=True))
            tops.append(top)
            probs_s[i % 2, rows, 0 : size(i)] = probs.astype(BF16)

        return [functools.partial(step, row) for row in range(0, TILE, GROUP)]

    def product_steps(i, tops, totals):
        s, e, tile = jobs[i]
        values = v_last if e else v_main

        def step(at, end):
            part = jnp.dot(
                probs_s[i % 2, :, at:end], values[s, at:end], preferred_element_type=F32
            )
            acc_s[...] = part if at == 0 else acc_s[...] + part

        def finish():
            top, total = jnp.concatenate(tops, axis=0), jnp.concatenate(totals, axis=0)
            out = acc_s[...] / total
            lse = top * SCORE_SCALE + jnp.log2(total)
            for n in range(2):
                r = 2 * tile + n
                half = slice(n * TOK, (n + 1) * TOK)
                if not far:
                    out_ref[s, r, e] = out[half]
                    lse_ref[s, r, e] = jnp.broadcast_to(lse[half], (TOK, HD))
                    continue
                lse_near = near_lse[s, r, e][:, 0:1]
                high = jnp.maximum(lse[half], lse_near)
                weight, weight_near = jnp.exp2(lse[half] - high), jnp.exp2(lse_near - high)
                both = weight + weight_near
                value = (out[half] * weight + near_out[s, r, e] * weight_near) / both
                lse_s[s, r, e] = jnp.broadcast_to(high + jnp.log2(both), (TOK, HD))
                msgs[r][s, e * TOK : (e + 1) * TOK] = value.astype(BF16)

        steps = []
        for at in range(0, size(i), SPLIT):
            steps.append(functools.partial(step, at, min(at + SPLIT, size(i))))
        return steps + [finish]

    def weave(*lists):
        order = []
        for steps in lists:
            order += [((n + 0.5) / len(steps), step) for n, step in enumerate(steps)]
        for _, step in sorted(order, key=lambda entry: entry[0]):
            step()

    weave(score_steps(0))
    pending = None
    for i in range(len(jobs)):
        tops, totals = [], []
        lists = [softmax_steps(i, tops, totals)]
        if i + 1 < len(jobs):
            lists.append(score_steps(i + 1))
        if pending is not None:
            lists.append(pending)
        weave(*lists)
        pending = product_steps(i, tops, totals)
    weave(pending)

    if far:
        order = [(r, s) for r in range(4) for s in range(B)]
        flat = to_rows([lse_s[s, r, e] for r, s in order for e in range(2)])
        for n, (r, s) in enumerate(order):
            part = flat[n * 4 : n * 4 + 4]
            high = part.astype(BF16).astype(F32)
            middle = (part - high).astype(BF16).astype(F32)
            low = part - high - middle
            stack = jnp.concatenate([high, middle, low, jnp.zeros((4, HD), F32)], axis=0)
            msgs[r][s, 2 * TOK : MSG_ROWS] = stack.astype(BF16)


def stale_attention(queries, pieces, near=None, after=None):
    far = near is not None
    args = [*queries, *pieces]
    in_specs = [vmem()] * 8
    if far:
        args += [*near, after]
        in_specs += [vmem(), vmem(), pl.BlockSpec(memory_space=pl.ANY)]
        out_shape = [jax.ShapeDtypeStruct((B, MSG_ROWS, HD), BF16)] * 4
    else:
        out_shape = [jax.ShapeDtypeStruct((B, 4, 2, TOK, HD), F32)] * 2
    work = B * 4 * TOK * (KEYS + KEYS_LAST)
    return pl.pallas_call(
        functools.partial(stale_kernel, far),
        out_shape=out_shape,
        in_specs=in_specs,
        out_specs=[vmem()] * len(out_shape),
        scratch_shapes=[
            pltpu.VMEM((B, 4, 2, TOK, HD), F32),
            pltpu.VMEM((TILE, HD), F32),
            pltpu.VMEM((B, KEYS, HD), BF16),
            pltpu.VMEM((B, KEYS, HD), BF16),
            pltpu.VMEM((B, KEYS_LAST, HD), BF16),
            pltpu.VMEM((B, KEYS_LAST, HD), BF16),
            pltpu.VMEM((2, TILE, KEYS), F32),
            pltpu.VMEM((2, TILE, KEYS), BF16),
        ],
        compiler_params=params(ATTENTION_MIB),
        cost_estimate=pl.CostEstimate(
            flops=4 * work * HD, bytes_accessed=8 * (KEYS + KEYS_LAST) * HD, transcendentals=work
        ),
        name="far_attention" if far else "near_attention",
    )(*args)


def merge_kernel(u_ref, fresh_out, fresh_rows, *refs):
    msgs, out_ref = refs[0:4], refs[4]
    lses = {}
    for k in range(4):
        for s in range(B):
            stack = msgs[k][s, 2 * TOK : MSG_ROWS].astype(F32)
            lses[s, k] = stack[0:4] + stack[4:8] + stack[8:12]
    weights, jobs = [], []
    for s in range(B):
        for k in range(LOCAL_HEADS):
            at = (s * LOCAL_HEADS + k) * 2
            parts = [(None, fresh_rows[at : at + 2])]
            if k < 4:
                parts.append((k, lses[s, k][0:2]))
            else:
                parts += [(n, lses[s, n][2:4]) for n in range(4)]
            top = parts[0][1]
            for _, lse in parts[1:]:
                top = jnp.maximum(top, lse)
            raw = [jnp.exp2(lse - top) for _, lse in parts]
            total = sum(raw[1:], raw[0])
            jobs.append((s, k, [(source, len(weights) + n) for n, (source, _) in enumerate(parts)]))
            weights += [one / total for one in raw]
    filler = jnp.zeros((HD - 2 * len(weights), HD), F32)
    table = jnp.concatenate(weights + [filler], axis=0).T
    for s, k, parts in jobs:
        head = lax.rem(u_ref[0] + k, 4) if k < 4 else 4
        out = [None, None]
        for source, n in parts:
            for half, rows in enumerate((slice(0, HD), slice(HD, TOK))):
                if source is None:
                    value = fresh_out[s, k, rows]
                else:
                    at = 0 if k < 4 else TOK
                    value = msgs[source][s, at + rows.start : at + rows.stop].astype(F32)
                column = table[0 : rows.stop - rows.start, 2 * n + half : 2 * n + half + 1]
                term = value * column
                out[half] = term if out[half] is None else out[half] + term
        cols = pl.ds(pl.multiple_of(head * HD, HD), HD)
        out_ref[s, :, cols] = jnp.concatenate(out, axis=0).astype(BF16)


def merge(u, fresh_out, fresh_rows, msgs):
    return pl.pallas_call(
        merge_kernel,
        out_shape=jax.ShapeDtypeStruct((B, TOK, WIDTH), BF16),
        in_specs=[smem()] + [vmem()] * 6,
        out_specs=vmem(),
        compiler_params=params(VMEM_MIB),
        cost_estimate=pl.CostEstimate(
            flops=10 * ROWS * WIDTH, bytes_accessed=14 * ROWS * WIDTH, transcendentals=0
        ),
        name="merge",
    )(u, fresh_out, fresh_rows, *msgs)


def shards(
    hidden,
    mod_shift,
    mod_scale,
    w_query,
    w_key,
    w_value,
    q_gain,
    k_gain,
    token_place,
    stale_keys,
    stale_values,
):
    patch = lax.axis_index("patch")
    tp = lax.axis_index("tp")
    y = patch // (NX * NZ)
    x = (patch // NZ) % NX
    u = jnp.where(tp % 2 == 0, y, x).astype(jnp.int32).reshape(1)
    own_rows = hidden.reshape(ROWS, CHUNK)
    z_rows = swap_tp(own_rows, 1, 0)
    core_rows = swap_tp(own_rows, 0, 1)

    packed = pack_stale(u, stale_keys, stale_values)
    arrived = exchange_u(packed)
    near = assemble([*arrived, packed[4]])
    near_one, near_three = swap_v(near, 1), swap_v(near, 3)
    far = swap_z_hi(near)
    cond, cos, sin, mod, own_rows = tables(token_place, own_rows, mod_shift, mod_scale, near)

    z_rows, cond = lax.optimization_barrier((z_rows, cond))
    cross_rows = swap_tp(z_rows, 0, 1)
    blocks = jnp.stack([tp, tp ^ 1, tp ^ 2, tp ^ 3]).astype(jnp.int32)
    modded = modulate(blocks, [own_rows, core_rows, z_rows, cross_rows], cond, mod)
    query = jnp.dot(modded, w_query, preferred_element_type=F32)
    key = jnp.dot(modded, w_key, preferred_element_type=F32)
    fresh_values = jnp.dot(modded, w_value, preferred_element_type=F32).astype(BF16)
    own_sq = sum_squares(query, key)
    own_sq, near_one, near_three = lax.optimization_barrier((own_sq, near_one, near_three))
    squares = [own_sq] + [swap_tp(own_sq, z, c) for z, c in ((1, 1), (1, 0), (0, 1))]
    near_two = swap_v(near_one, 3)
    fresh_keys, *sends = norm_rope(u, query, key, squares, q_gain, k_gain, cos, sin)
    far, near_two, *sends = lax.optimization_barrier((far, near_two, *sends))
    far_one, far_three = swap_v(far, 1), swap_v(far, 3)
    queries = exchange_u(sends)
    fresh_out, fresh_rows = fresh_attention(u, fresh_keys, fresh_values, sends)

    far_one, fresh_rows, *queries = lax.optimization_barrier((far_one, fresh_rows, *queries))
    far_two = swap_v(far_one, 3)
    partial = stale_attention(queries, [near, near_one, near_three, near_two])
    outs = stale_attention(
        queries, [far, far_one, far_three, far_two], near=partial, after=fresh_rows
    )
    returned = exchange_u(outs)
    attended = merge(u, fresh_out, fresh_rows, returned)
    return (
        attended,
        fresh_keys.reshape(B, TOK, WIDTH),
        fresh_values.reshape(B, TOK, WIDTH),
    )


def solution(mesh):
    in_specs = (
        P(None, "patch", "tp"),
        P(),
        P(),
        P(None, "tp"),
        P(None, "tp"),
        P(None, "tp"),
        P("tp"),
        P("tp"),
        P("patch"),
        P(None, "patch", "tp"),
        P(None, "patch", "tp"),
    )
    out_specs = (P(None, "patch", "tp"), P(None, "patch", "tp"), P(None, "patch", "tp"))
    return jax.shard_map(shards, mesh=mesh, in_specs=in_specs, out_specs=out_specs, check_vma=False)
```

```python
import functools
import math

import jax
import jax.numpy as jnp
import numpy as np
from jax import lax
from jax.experimental import pallas as pl
from jax.experimental.pallas import tpu as pltpu
from jax.sharding import PartitionSpec as P

D = 5120
HEADS = 20
HD = 128
FRAMES = 3
GRID_W = 48
EPS = 1e-06
MASKED = -1e30
NY, NX, NZ = 4, 4, 2
TP = 4
N_PATCH = NY * NX * NZ
TOK = 144
B = 2
ROWS = B * TOK
LOCAL_HEADS = 5
WIDTH = LOCAL_HEADS * HD
CHUNK = D // TP
STAT_LANES = 384
PIECE = 5 * TOK
MSG_ROWS = 2 * TOK + 16
SCORE_SCALE = math.log2(math.e) / math.sqrt(HD)
F32 = jnp.float32
BF16 = jnp.bfloat16
AXES = ("patch", "tp")
GROUP = 16
VMEM_MIB = 24
ATTENTION_MIB = 34


def params(mib):
    return pltpu.CompilerParams(vmem_limit_bytes=mib * 1024 * 1024)


def vmem():
    return pl.BlockSpec(memory_space=pltpu.VMEM)


def smem():
    return pl.BlockSpec(memory_space=pltpu.SMEM)


def linear(u, v, z_hi, z_lo, core):
    y, x = (u, v) if core == 0 else (v, u)
    return ((y * NX + x) * NZ + z_hi) * TP + z_lo * 2 + core


def places():
    return [
        (u, v, h, l, c)
        for u in range(4)
        for v in range(4)
        for h in range(2)
        for l in range(2)
        for c in range(2)
    ]


def permute(value, move):
    return lax.ppermute(value, AXES, [(linear(*p), linear(*move(*p))) for p in places()])


def shift_u(value, k):
    return permute(value, lambda u, v, h, l, c: ((u + k) % 4, v, h, l, c))


def swap_v(value, mask):
    return permute(value, lambda u, v, h, l, c: (u, v ^ mask, h, l, c))


def exchange_u(values):
    came = {r: shift_u(values[4 - r], 4 - r) for r in (2, 1, 3)}
    return [values[0], came[1], came[2], came[3]]


def swap_z_hi(value):
    return permute(value, lambda u, v, h, l, c: (u, v, 1 - h, l, c))


def swap_tp(value, z, core):
    if core:
        return permute(value, lambda u, v, h, l, c: (v, u, h, l ^ z, 1 - c))
    return permute(value, lambda u, v, h, l, c: (u, v, h, l ^ z, c))


def frequencies():
    half_dim = HD // 2
    third_dim = half_dim // 3
    frame_pairs = half_dim - 2 * third_dim
    pair = np.arange(HD) // 2
    offset = np.where(
        pair < frame_pairs,
        pair,
        np.where(pair < frame_pairs + third_dim, pair - frame_pairs, pair - frame_pairs - third_dim),
    )
    width = np.where(pair < frame_pairs, 2 * frame_pairs, 2 * third_dim)
    return np.exp(-math.log(10000.0) * 2.0 * offset / width).astype(np.float32).reshape(1, HD)


def columns_to_rows(first, second):
    lane = lax.broadcasted_iota(jnp.int32, (ROWS, 128), 1)
    both = jnp.where(lane == 0, first, jnp.where(lane == 1, second, 0.0))
    padded = jnp.concatenate([both, jnp.zeros((STAT_LANES - ROWS, 128), F32)], axis=0)
    return padded.T[0:8]


def row_to_column(row):
    return jnp.broadcast_to(row, (128, STAT_LANES)).T[0:ROWS]


def pack_kernel(u_ref, key_ref, value_ref, *outs):
    for k in range(5):
        head = lax.rem(u_ref[0] + k, 4) if k < 4 else 4
        cols = pl.ds(pl.multiple_of(head * HD, HD), HD)
        for n, source in enumerate((key_ref, value_ref)):
            for s in range(B):
                outs[k][s, n] = source[s, :, cols]


def pack_stale(u, stale_keys, stale_values):
    return pl.pallas_call(
        pack_kernel,
        out_shape=[jax.ShapeDtypeStruct((B, 2, TOK, HD), BF16)] * 5,
        in_specs=[smem(), vmem(), vmem()],
        out_specs=[vmem()] * 5,
        compiler_params=params(VMEM_MIB),
        cost_estimate=pl.CostEstimate(
            flops=0, bytes_accessed=8 * ROWS * WIDTH, transcendentals=0
        ),
        name="pack_stale",
    )(u, stale_keys, stale_values)


def tables_kernel(place_hbm, freq, rows, shift, scale, after, *refs):
    cond, cos, sin, mod, rows_out, places_s, place_ref, sem = refs
    copy = pltpu.make_async_copy(place_hbm, place_ref, sem.at[0])
    copy.start()
    copy.wait()
    for row in range(TOK):
        places_s[row : row + 1] = jnp.full((1, HD), place_ref[row], jnp.int32)
    place = places_s[...]
    frame_tok = TOK * N_PATCH // FRAMES
    frame = jnp.where(place >= frame_tok, 1, 0) + jnp.where(place >= 2 * frame_tok, 1, 0)
    within = place - frame * frame_tok
    grid_row = ((within.astype(F32) + 0.5) * (1.0 / GRID_W)).astype(jnp.int32)
    grid_col = within - grid_row * GRID_W
    lane = lax.broadcasted_iota(jnp.int32, (TOK, HD), 1)
    third = 2 * (HD // 6)
    frame_lanes = HD - 2 * third
    position = jnp.where(
        lane < frame_lanes, frame, jnp.where(lane < frame_lanes + third, grid_row, grid_col)
    )
    angles = position.astype(F32) * freq[...]
    cos[...] = jnp.cos(angles)
    sine = jnp.sin(angles)
    sin[...] = jnp.where(lane % 2 == 0, -sine, sine)
    flag = jnp.where((frame == 0) | (frame == FRAMES - 1), 1.0, 0.0)
    cond[0:TOK] = flag
    cond[TOK:ROWS] = flag
    mod[0:2] = 1.0 + scale[...]
    mod[2:4] = shift[...]
    rows_out[...] = rows[...]


def tables(token_place, rows, shift, scale, after):
    table = jax.ShapeDtypeStruct((TOK, HD), F32)
    return pl.pallas_call(
        tables_kernel,
        out_shape=[
            jax.ShapeDtypeStruct((ROWS, HD), F32),
            table,
            table,
            jax.ShapeDtypeStruct((4, D), F32),
            jax.ShapeDtypeStruct((ROWS, CHUNK), BF16),
        ],
        in_specs=[pl.BlockSpec(memory_space=pltpu.HBM)]
        + [vmem()] * 4
        + [pl.BlockSpec(memory_space=pl.ANY)],
        out_specs=[vmem()] * 5,
        scratch_shapes=[
            pltpu.VMEM((TOK, HD), jnp.int32),
            pltpu.SMEM((TOK,), jnp.int32),
            pltpu.SemaphoreType.DMA((1,)),
        ],
        compiler_params=params(VMEM_MIB),
        cost_estimate=pl.CostEstimate(
            flops=100 * TOK * HD, bytes_accessed=1_000_000, transcendentals=0
        ),
        name="tables",
    )(token_place, jnp.asarray(frequencies()), rows, shift, scale, after)


def assemble_kernel(*refs):
    parts, out = refs[0:5], refs[5]
    for s in range(B):
        for n in range(2):
            for r in range(5):
                out[s, n, r * TOK : (r + 1) * TOK] = parts[r][s, n]


def assemble(parts):
    return pl.pallas_call(
        assemble_kernel,
        out_shape=jax.ShapeDtypeStruct((B, 2, PIECE, HD), BF16),
        in_specs=[vmem()] * 5,
        out_specs=vmem(),
        compiler_params=params(VMEM_MIB),
        cost_estimate=pl.CostEstimate(
            flops=0, bytes_accessed=16 * PIECE * HD, transcendentals=0
        ),
        name="assemble",
    )(*parts)


def lane_sum(parts):
    total = None
    for part in parts:
        for at in range(0, part.shape[1], HD):
            piece = part[:, at : at + HD]
            total = piece if total is None else total + piece
    return jnp.sum(total, axis=1, keepdims=True)


def modulate_kernel(t_ref, h0, h1, h2, h3, cond, mod, out_ref):
    chunks = (h0, h1, h2, h3)
    for row in range(0, ROWS, GROUP):
        rows = slice(row, row + GROUP)
        lanes = [chunk[rows].astype(F32) for chunk in chunks]
        mean = lane_sum([(lanes[0] + lanes[1]) + (lanes[2] + lanes[3])]) * (1.0 / D)
        deviation = lane_sum([(part - mean) * (part - mean) for part in lanes])
        rstd = lax.rsqrt(deviation * (1.0 / D) + EPS)
        conditioned = cond[rows, 0:1] > 0.5
        for c in range(TP):
            cols = pl.ds(pl.multiple_of(t_ref[c] * CHUNK, CHUNK), CHUNK)
            gain = jnp.where(conditioned, mod[1:2, cols], mod[0:1, cols])
            bias = jnp.where(conditioned, mod[3:4, cols], mod[2:3, cols])
            normed = (lanes[c] - mean) * rstd
            out_ref[rows, cols] = (normed * gain + bias).astype(BF16)


def modulate(blocks, chunks, cond, mod):
    return pl.pallas_call(
        modulate_kernel,
        out_shape=jax.ShapeDtypeStruct((ROWS, D), BF16),
        in_specs=[smem()] + [vmem()] * 6,
        out_specs=vmem(),
        compiler_params=params(VMEM_MIB),
        cost_estimate=pl.CostEstimate(
            flops=12 * ROWS * D, bytes_accessed=45_000_000, transcendentals=0
        ),
        name="modulate",
    )(blocks, *chunks, cond, mod)


def squares_kernel(q_ref, k_ref, out_ref):
    query, key = q_ref[...], k_ref[...]
    out_ref[...] = columns_to_rows(
        jnp.sum(query * query, axis=1, keepdims=True),
        jnp.sum(key * key, axis=1, keepdims=True),
    )


def sum_squares(query, key):
    return pl.pallas_call(
        squares_kernel,
        out_shape=jax.ShapeDtypeStruct((8, STAT_LANES), F32),
        in_specs=[vmem()] * 2,
        out_specs=vmem(),
        compiler_params=params(VMEM_MIB),
        cost_estimate=pl.CostEstimate(
            flops=4 * ROWS * WIDTH, bytes_accessed=8 * ROWS * WIDTH, transcendentals=0
        ),
        name="sum_squares",
    )(query, key)


def rope_kernel(u_ref, q_ref, k_ref, s0, s1, s2, s3, qg, kg, cos, sin, k_all, *refs):
    sends, q_rot = refs[0:4], refs[4]
    total = s0[...] + s1[...] + s2[...] + s3[...]
    inverse = lax.rsqrt(total * (1.0 / (HEADS * HD)) + EPS)
    even = lax.broadcasted_iota(jnp.int32, (ROWS, HD), 1) % 2 == 0
    cos_rows = jnp.concatenate([cos[...], cos[...]], axis=0)
    sin_rows = jnp.concatenate([sin[...], sin[...]], axis=0)

    def rotate(ref, column, gain, cols):
        part = ref[:, cols] * column * gain[cols].reshape(1, HD)
        swap = jnp.where(even, pltpu.roll(part, HD - 1, 1), pltpu.roll(part, 1, 1))
        return (part * cos_rows + swap * sin_rows).astype(BF16)

    q_column = row_to_column(inverse[0:1])
    k_column = row_to_column(inverse[1:2])
    for head in range(LOCAL_HEADS):
        cols = slice(head * HD, (head + 1) * HD)
        query = rotate(q_ref, q_column, qg, cols)
        for s in range(B):
            q_rot[head, s] = query[s * TOK : (s + 1) * TOK]
        k_all[:, cols] = rotate(k_ref, k_column, kg, cols)
    for k in range(4):
        for s in range(B):
            sends[k][s, 0] = q_rot[lax.rem(u_ref[0] + k, 4), s]
            sends[k][s, 1] = q_rot[4, s]


def norm_rope(u, query, key, squares, q_gain, k_gain, cos, sin):
    send = jax.ShapeDtypeStruct((B, 2, TOK, HD), BF16)
    flat = jax.ShapeDtypeStruct((ROWS, WIDTH), BF16)
    return pl.pallas_call(
        rope_kernel,
        out_shape=[flat] + [send] * 4,
        in_specs=[smem()] + [vmem()] * 10,
        out_specs=[vmem()] * 5,
        scratch_shapes=[pltpu.VMEM((LOCAL_HEADS, B, TOK, HD), BF16)],
        compiler_params=params(VMEM_MIB),
        cost_estimate=pl.CostEstimate(
            flops=20 * ROWS * WIDTH, bytes_accessed=16 * ROWS * WIDTH, transcendentals=0
        ),
        name="norm_rope",
    )(u, query, key, *squares, q_gain, k_gain, cos, sin)


def scores_of(query, keys):
    return lax.dot_general(query, keys, (((1,), (1,)), ((), ())), preferred_element_type=F32)


def to_rows(blocks):
    lane = lax.broadcasted_iota(jnp.int32, (HD, HD), 1)
    table = jnp.zeros((HD, HD), F32)
    empty = jnp.zeros((2 * HD - TOK, HD), F32)
    for n, block in enumerate(blocks):
        rest = jnp.concatenate([block[HD:TOK], empty], axis=0)
        table = jnp.where(lane == 2 * n, block[0:HD], table)
        table = jnp.where(lane == 2 * n + 1, rest, table)
    return table.T


FRESH_ROWS = 24


def fresh_kernel(u_ref, k_ref, v_ref, *refs):
    queries, (out_ref, rows_ref) = refs[0:4], refs[4:6]
    lses = []
    for s in range(B):
        rows = slice(s * TOK, (s + 1) * TOK)
        for k in range(LOCAL_HEADS):
            head = lax.rem(u_ref[0] + k, 4) if k < 4 else 4
            cols = pl.ds(pl.multiple_of(head * HD, HD), HD)
            query = queries[k][s, 0] if k < 4 else queries[0][s, 1]
            scores = scores_of(query, k_ref[rows, cols])
            top = jnp.max(scores, axis=1, keepdims=True)
            probs = jnp.exp2((scores - top) * SCORE_SCALE)
            total = jnp.sum(probs, axis=1, keepdims=True)
            out = jnp.dot(probs.astype(BF16), v_ref[rows, cols], preferred_element_type=F32)
            out_ref[s, k] = out / total
            lses.append(jnp.broadcast_to(top * SCORE_SCALE + jnp.log2(total), (TOK, HD)))
    rows_ref[...] = to_rows(lses)[0:FRESH_ROWS]


def fresh_attention(u, key, value, queries):
    return pl.pallas_call(
        fresh_kernel,
        out_shape=[
            jax.ShapeDtypeStruct((B, LOCAL_HEADS, TOK, HD), F32),
            jax.ShapeDtypeStruct((FRESH_ROWS, HD), F32),
        ],
        in_specs=[smem()] + [vmem()] * 6,
        out_specs=[vmem()] * 2,
        compiler_params=params(VMEM_MIB),
        cost_estimate=pl.CostEstimate(
            flops=4 * ROWS * TOK * WIDTH,
            bytes_accessed=14 * ROWS * WIDTH,
            transcendentals=ROWS * TOK * LOCAL_HEADS,
        ),
        name="fresh_attention",
    )(u, key, value, *queries)


TILE = 2 * TOK
PER_PIECE = 4 * TOK
KEYS = 4 * PER_PIECE
KEYS_LAST = 4 * TOK
SPLIT = 768


def stale_kernel(far, *refs):
    queries = refs[0:4]
    pieces, rest = refs[4:8], refs[8:]
    if far:
        near_out, near_lse = rest[0:2]
        msgs = rest[3:7]
    else:
        out_ref, lse_ref = rest[0:2]
    lse_s, acc_s, k_main, v_main, k_last, v_last, scores_s, probs_s = rest[-8:]

    jobs = [(s, e, tile) for s in range(B) for e in range(2) for tile in range(2)]

    def size(i):
        return KEYS_LAST if jobs[i][1] else KEYS

    def score_steps(i):
        s, e, tile = jobs[i]
        keys = k_last if e else k_main
        out = scores_s.at[i % 2]

        def arrive():
            for n, piece in enumerate(pieces):
                main = slice(n * PER_PIECE, (n + 1) * PER_PIECE)
                last = slice(n * TOK, (n + 1) * TOK)
                k_main[s, main] = piece[s, 0, 0:PER_PIECE]
                k_last[s, last] = piece[s, 0, PER_PIECE:PIECE]
                v_main[s, main] = piece[s, 1, 0:PER_PIECE]
                v_last[s, last] = piece[s, 1, PER_PIECE:PIECE]

        def step(at, end):
            query = jnp.concatenate([queries[2 * tile][s, e], queries[2 * tile + 1][s, e]], axis=0)
            out[:, at:end] = scores_of(query, keys[s, at:end])

        def hide():
            for n in range(2):
                r = 2 * tile + n
                rows = slice(n * TOK, (n + 1) * TOK)
                if e and r:
                    continue
                out[rows, r * TOK : (r + 1) * TOK] = jnp.full((TOK, TOK), MASKED, F32)

        steps = [] if i % 4 else [arrive]
        for at in range(0, size(i), SPLIT):
            steps.append(functools.partial(step, at, min(at + SPLIT, size(i))))
        return steps if far else steps + [hide]

    def softmax_steps(i, tops, totals):
        def step(row):
            rows = slice(row, row + GROUP)
            part = scores_s[i % 2, rows, 0 : size(i)]
            top = jnp.max(part, axis=1, keepdims=True)
            probs = jnp.exp2((part - top) * SCORE_SCALE)
            totals.append(jnp.sum(probs, axis=1, keepdims=True))
            tops.append(top)
            probs_s[i % 2, rows, 0 : size(i)] = probs.astype(BF16)

        return [functools.partial(step, row) for row in range(0, TILE, GROUP)]

    def product_steps(i, tops, totals):
        s, e, tile = jobs[i]
        values = v_last if e else v_main

        def step(at, end):
            part = jnp.dot(
                probs_s[i % 2, :, at:end], values[s, at:end], preferred_element_type=F32
            )
            acc_s[...] = part if at == 0 else acc_s[...] + part

        def finish():
            top, total = jnp.concatenate(tops, axis=0), jnp.concatenate(totals, axis=0)
            out = acc_s[...] / total
            lse = top * SCORE_SCALE + jnp.log2(total)
            for n in range(2):
                r = 2 * tile + n
                half = slice(n * TOK, (n + 1) * TOK)
                if not far:
                    out_ref[s, r, e] = out[half]
                    lse_ref[s, r, e] = jnp.broadcast_to(lse[half], (TOK, HD))
                    continue
                lse_near = near_lse[s, r, e][:, 0:1]
                high = jnp.maximum(lse[half], lse_near)
                weight, weight_near = jnp.exp2(lse[half] - high), jnp.exp2(lse_near - high)
                both = weight + weight_near
                value = (out[half] * weight + near_out[s, r, e] * weight_near) / both
                lse_s[s, r, e] = jnp.broadcast_to(high + jnp.log2(both), (TOK, HD))
                msgs[r][s, e * TOK : (e + 1) * TOK] = value.astype(BF16)

        steps = []
        for at in range(0, size(i), SPLIT):
            steps.append(functools.partial(step, at, min(at + SPLIT, size(i))))
        return steps + [finish]

    def weave(*lists):
        order = []
        for steps in lists:
            order += [((n + 0.5) / len(steps), step) for n, step in enumerate(steps)]
        for _, step in sorted(order, key=lambda entry: entry[0]):
            step()

    weave(score_steps(0))
    pending = None
    for i in range(len(jobs)):
        tops, totals = [], []
        lists = [softmax_steps(i, tops, totals)]
        if i + 1 < len(jobs):
            lists.append(score_steps(i + 1))
        if pending is not None:
            lists.append(pending)
        weave(*lists)
        pending = product_steps(i, tops, totals)
    weave(pending)

    if far:
        order = [(r, s) for r in range(4) for s in range(B)]
        flat = to_rows([lse_s[s, r, e] for r, s in order for e in range(2)])
        for n, (r, s) in enumerate(order):
            part = flat[n * 4 : n * 4 + 4]
            high = part.astype(BF16).astype(F32)
            middle = (part - high).astype(BF16).astype(F32)
            low = part - high - middle
            stack = jnp.concatenate([high, middle, low, jnp.zeros((4, HD), F32)], axis=0)
            msgs[r][s, 2 * TOK : MSG_ROWS] = stack.astype(BF16)


def stale_attention(queries, pieces, near=None, after=None):
    far = near is not None
    args = [*queries, *pieces]
    in_specs = [vmem()] * 8
    if far:
        args += [*near, after]
        in_specs += [vmem(), vmem(), pl.BlockSpec(memory_space=pl.ANY)]
        out_shape = [jax.ShapeDtypeStruct((B, MSG_ROWS, HD), BF16)] * 4
    else:
        out_shape = [jax.ShapeDtypeStruct((B, 4, 2, TOK, HD), F32)] * 2
    work = B * 4 * TOK * (KEYS + KEYS_LAST)
    return pl.pallas_call(
        functools.partial(stale_kernel, far),
        out_shape=out_shape,
        in_specs=in_specs,
        out_specs=[vmem()] * len(out_shape),
        scratch_shapes=[
            pltpu.VMEM((B, 4, 2, TOK, HD), F32),
            pltpu.VMEM((TILE, HD), F32),
            pltpu.VMEM((B, KEYS, HD), BF16),
            pltpu.VMEM((B, KEYS, HD), BF16),
            pltpu.VMEM((B, KEYS_LAST, HD), BF16),
            pltpu.VMEM((B, KEYS_LAST, HD), BF16),
            pltpu.VMEM((2, TILE, KEYS), F32),
            pltpu.VMEM((2, TILE, KEYS), BF16),
        ],
        compiler_params=params(ATTENTION_MIB),
        cost_estimate=pl.CostEstimate(
            flops=4 * work * HD, bytes_accessed=8 * (KEYS + KEYS_LAST) * HD, transcendentals=work
        ),
        name="far_attention" if far else "near_attention",
    )(*args)


def merge_kernel(u_ref, fresh_out, fresh_rows, *refs):
    msgs, out_ref = refs[0:4], refs[4]
    lses = {}
    for k in range(4):
        for s in range(B):
            stack = msgs[k][s, 2 * TOK : MSG_ROWS].astype(F32)
            lses[s, k] = stack[0:4] + stack[4:8] + stack[8:12]
    weights, jobs = [], []
    for s in range(B):
        for k in range(LOCAL_HEADS):
            at = (s * LOCAL_HEADS + k) * 2
            parts = [(None, fresh_rows[at : at + 2])]
            if k < 4:
                parts.append((k, lses[s, k][0:2]))
            else:
                parts += [(n, lses[s, n][2:4]) for n in range(4)]
            top = parts[0][1]
            for _, lse in parts[1:]:
                top = jnp.maximum(top, lse)
            raw = [jnp.exp2(lse - top) for _, lse in parts]
            total = sum(raw[1:], raw[0])
            jobs.append((s, k, [(source, len(weights) + n) for n, (source, _) in enumerate(parts)]))
            weights += [one / total for one in raw]
    filler = jnp.zeros((HD - 2 * len(weights), HD), F32)
    table = jnp.concatenate(weights + [filler], axis=0).T
    for s, k, parts in jobs:
        head = lax.rem(u_ref[0] + k, 4) if k < 4 else 4
        out = [None, None]
        for source, n in parts:
            for half, rows in enumerate((slice(0, HD), slice(HD, TOK))):
                if source is None:
                    value = fresh_out[s, k, rows]
                else:
                    at = 0 if k < 4 else TOK
                    value = msgs[source][s, at + rows.start : at + rows.stop].astype(F32)
                column = table[0 : rows.stop - rows.start, 2 * n + half : 2 * n + half + 1]
                term = value * column
                out[half] = term if out[half] is None else out[half] + term
        cols = pl.ds(pl.multiple_of(head * HD, HD), HD)
        out_ref[s, :, cols] = jnp.concatenate(out, axis=0).astype(BF16)


def merge(u, fresh_out, fresh_rows, msgs):
    return pl.pallas_call(
        merge_kernel,
        out_shape=jax.ShapeDtypeStruct((B, TOK, WIDTH), BF16),
        in_specs=[smem()] + [vmem()] * 6,
        out_specs=vmem(),
        compiler_params=params(VMEM_MIB),
        cost_estimate=pl.CostEstimate(
            flops=10 * ROWS * WIDTH, bytes_accessed=14 * ROWS * WIDTH, transcendentals=0
        ),
        name="merge",
    )(u, fresh_out, fresh_rows, *msgs)


def shards(
    hidden,
    mod_shift,
    mod_scale,
    w_query,
    w_key,
    w_value,
    q_gain,
    k_gain,
    token_place,
    stale_keys,
    stale_values,
):
    patch = lax.axis_index("patch")
    tp = lax.axis_index("tp")
    y = patch // (NX * NZ)
    x = (patch // NZ) % NX
    u = jnp.where(tp % 2 == 0, y, x).astype(jnp.int32).reshape(1)
    own_rows = hidden.reshape(ROWS, CHUNK)
    z_rows = swap_tp(own_rows, 1, 0)
    core_rows = swap_tp(own_rows, 0, 1)

    packed = pack_stale(u, stale_keys, stale_values)
    arrived = exchange_u(packed)
    near = assemble([*arrived, packed[4]])
    cond, cos, sin, mod, own_rows = tables(token_place, own_rows, mod_shift, mod_scale, near)
    near_one, near_three = swap_v(near, 1), swap_v(near, 3)
    far = swap_z_hi(near)

    z_rows, cond = lax.optimization_barrier((z_rows, cond))
    cross_rows = swap_tp(z_rows, 0, 1)
    near_two = swap_v(near_one, 3)
    blocks = jnp.stack([tp, tp ^ 1, tp ^ 2, tp ^ 3]).astype(jnp.int32)
    modded = modulate(blocks, [own_rows, core_rows, z_rows, cross_rows], cond, mod)
    query = jnp.dot(modded, w_query, preferred_element_type=F32)
    key = jnp.dot(modded, w_key, preferred_element_type=F32)
    fresh_values = jnp.dot(modded, w_value, preferred_element_type=F32).astype(BF16)
    own_sq = sum_squares(query, key)
    own_sq, near_three = lax.optimization_barrier((own_sq, near_three))
    squares = [own_sq] + [swap_tp(own_sq, z, c) for z, c in ((1, 1), (1, 0), (0, 1))]
    near_two, *squares = lax.optimization_barrier((near_two, *squares))
    far_two = swap_z_hi(near_two)
    fresh_keys, *sends = norm_rope(u, query, key, squares, q_gain, k_gain, cos, sin)
    queries = exchange_u(sends)
    fresh_out, fresh_rows = fresh_attention(u, fresh_keys, fresh_values, sends)
    far, *queries = lax.optimization_barrier((far, *queries))
    far_one, far_three = swap_v(far, 1), swap_v(far, 3)

    partial = stale_attention(queries, [near, near_one, near_three, near_two])
    outs = stale_attention(
        queries, [far, far_one, far_three, far_two], near=partial, after=fresh_rows
    )
    returned = exchange_u(outs)
    attended = merge(u, fresh_out, fresh_rows, returned)
    return (
        attended,
        fresh_keys.reshape(B, TOK, WIDTH),
        fresh_values.reshape(B, TOK, WIDTH),
    )


def solution(mesh):
    in_specs = (
        P(None, "patch", "tp"),
        P(),
        P(),
        P(None, "tp"),
        P(None, "tp"),
        P(None, "tp"),
        P("tp"),
        P("tp"),
        P("patch"),
        P(None, "patch", "tp"),
        P(None, "patch", "tp"),
    )
    out_specs = (P(None, "patch", "tp"), P(None, "patch", "tp"), P(None, "patch", "tp"))
    return jax.shard_map(shards, mesh=mesh, in_specs=in_specs, out_specs=out_specs, check_vma=False)
```

```python
import functools
import math

import jax
import jax.numpy as jnp
import numpy as np
from jax import lax
from jax.experimental import pallas as pl
from jax.experimental.pallas import tpu as pltpu
from jax.sharding import PartitionSpec as P

D = 5120
HEADS = 20
HD = 128
FRAMES = 3
GRID_W = 48
EPS = 1e-06
MASKED = -1e30
NY, NX, NZ = 4, 4, 2
TP = 4
N_PATCH = NY * NX * NZ
TOK = 144
B = 2
ROWS = B * TOK
LOCAL_HEADS = 5
WIDTH = LOCAL_HEADS * HD
CHUNK = D // TP
STAT_LANES = 384
PIECE = 5 * TOK
MSG_ROWS = 2 * TOK + 16
SCORE_SCALE = math.log2(math.e) / math.sqrt(HD)
F32 = jnp.float32
BF16 = jnp.bfloat16
AXES = ("patch", "tp")
GROUP = 16
VMEM_MIB = 24
ATTENTION_MIB = 34
MODULATE_MIB = 44


def params(mib):
    return pltpu.CompilerParams(vmem_limit_bytes=mib * 1024 * 1024)


def vmem():
    return pl.BlockSpec(memory_space=pltpu.VMEM)


def smem():
    return pl.BlockSpec(memory_space=pltpu.SMEM)


def linear(u, v, z_hi, z_lo, core):
    y, x = (u, v) if core == 0 else (v, u)
    return ((y * NX + x) * NZ + z_hi) * TP + z_lo * 2 + core


def places():
    return [
        (u, v, h, l, c)
        for u in range(4)
        for v in range(4)
        for h in range(2)
        for l in range(2)
        for c in range(2)
    ]


def permute(value, move):
    return lax.ppermute(value, AXES, [(linear(*p), linear(*move(*p))) for p in places()])


def shift_u(value, k):
    return permute(value, lambda u, v, h, l, c: ((u + k) % 4, v, h, l, c))


def swap_v(value, mask):
    return permute(value, lambda u, v, h, l, c: (u, v ^ mask, h, l, c))


def exchange_u(values):
    came = {r: shift_u(values[4 - r], 4 - r) for r in (2, 1, 3)}
    return [values[0], came[1], came[2], came[3]]


def swap_z_hi(value):
    return permute(value, lambda u, v, h, l, c: (u, v, 1 - h, l, c))


def swap_tp(value, z, core):
    if core:
        return permute(value, lambda u, v, h, l, c: (v, u, h, l ^ z, 1 - c))
    return permute(value, lambda u, v, h, l, c: (u, v, h, l ^ z, c))


def frequencies():
    half_dim = HD // 2
    third_dim = half_dim // 3
    frame_pairs = half_dim - 2 * third_dim
    pair = np.arange(HD) // 2
    offset = np.where(
        pair < frame_pairs,
        pair,
        np.where(pair < frame_pairs + third_dim, pair - frame_pairs, pair - frame_pairs - third_dim),
    )
    width = np.where(pair < frame_pairs, 2 * frame_pairs, 2 * third_dim)
    return np.exp(-math.log(10000.0) * 2.0 * offset / width).astype(np.float32).reshape(1, HD)


def columns_to_rows(first, second):
    lane = lax.broadcasted_iota(jnp.int32, (ROWS, 128), 1)
    both = jnp.where(lane == 0, first, jnp.where(lane == 1, second, 0.0))
    padded = jnp.concatenate([both, jnp.zeros((STAT_LANES - ROWS, 128), F32)], axis=0)
    return padded.T[0:8]


def row_to_column(row):
    return jnp.broadcast_to(row, (128, STAT_LANES)).T[0:ROWS]


def pack_kernel(u_ref, key_ref, value_ref, *outs):
    for k in range(5):
        head = lax.rem(u_ref[0] + k, 4) if k < 4 else 4
        cols = pl.ds(pl.multiple_of(head * HD, HD), HD)
        for n, source in enumerate((key_ref, value_ref)):
            for s in range(B):
                outs[k][s, n] = source[s, :, cols]


def pack_stale(u, stale_keys, stale_values):
    return pl.pallas_call(
        pack_kernel,
        out_shape=[jax.ShapeDtypeStruct((B, 2, TOK, HD), BF16)] * 5,
        in_specs=[smem(), vmem(), vmem()],
        out_specs=[vmem()] * 5,
        compiler_params=params(VMEM_MIB),
        cost_estimate=pl.CostEstimate(
            flops=0, bytes_accessed=8 * ROWS * WIDTH, transcendentals=0
        ),
        name="pack_stale",
    )(u, stale_keys, stale_values)


def tables_kernel(place_hbm, freq, rows, shift, scale, after, *refs):
    cond, cos, sin, mod, rows_out, places_s, place_ref, sem = refs
    copy = pltpu.make_async_copy(place_hbm, place_ref, sem.at[0])
    copy.start()
    copy.wait()
    for row in range(TOK):
        places_s[row : row + 1] = jnp.full((1, HD), place_ref[row], jnp.int32)
    place = places_s[...]
    frame_tok = TOK * N_PATCH // FRAMES
    frame = jnp.where(place >= frame_tok, 1, 0) + jnp.where(place >= 2 * frame_tok, 1, 0)
    within = place - frame * frame_tok
    grid_row = ((within.astype(F32) + 0.5) * (1.0 / GRID_W)).astype(jnp.int32)
    grid_col = within - grid_row * GRID_W
    lane = lax.broadcasted_iota(jnp.int32, (TOK, HD), 1)
    third = 2 * (HD // 6)
    frame_lanes = HD - 2 * third
    position = jnp.where(
        lane < frame_lanes, frame, jnp.where(lane < frame_lanes + third, grid_row, grid_col)
    )
    angles = position.astype(F32) * freq[...]
    cos[...] = jnp.cos(angles)
    sine = jnp.sin(angles)
    sin[...] = jnp.where(lane % 2 == 0, -sine, sine)
    flag = jnp.where((frame == 0) | (frame == FRAMES - 1), 1.0, 0.0)
    cond[0:TOK] = flag
    cond[TOK:ROWS] = flag
    mod[0:2] = 1.0 + scale[...]
    mod[2:4] = shift[...]
    rows_out[...] = rows[...]


def tables(token_place, rows, shift, scale, after):
    table = jax.ShapeDtypeStruct((TOK, HD), F32)
    return pl.pallas_call(
        tables_kernel,
        out_shape=[
            jax.ShapeDtypeStruct((ROWS, HD), F32),
            table,
            table,
            jax.ShapeDtypeStruct((4, D), F32),
            jax.ShapeDtypeStruct((ROWS, CHUNK), BF16),
        ],
        in_specs=[pl.BlockSpec(memory_space=pltpu.HBM)]
        + [vmem()] * 4
        + [pl.BlockSpec(memory_space=pl.ANY)],
        out_specs=[vmem()] * 5,
        scratch_shapes=[
            pltpu.VMEM((TOK, HD), jnp.int32),
            pltpu.SMEM((TOK,), jnp.int32),
            pltpu.SemaphoreType.DMA((1,)),
        ],
        compiler_params=params(VMEM_MIB),
        cost_estimate=pl.CostEstimate(
            flops=100 * TOK * HD, bytes_accessed=1_000_000, transcendentals=0
        ),
        name="tables",
    )(token_place, jnp.asarray(frequencies()), rows, shift, scale, after)


def assemble_kernel(*refs):
    parts, out = refs[0:5], refs[5]
    for s in range(B):
        for n in range(2):
            for r in range(5):
                out[s, n, r * TOK : (r + 1) * TOK] = parts[r][s, n]


def assemble(parts):
    return pl.pallas_call(
        assemble_kernel,
        out_shape=jax.ShapeDtypeStruct((B, 2, PIECE, HD), BF16),
        in_specs=[vmem()] * 5,
        out_specs=vmem(),
        compiler_params=params(VMEM_MIB),
        cost_estimate=pl.CostEstimate(
            flops=0, bytes_accessed=16 * PIECE * HD, transcendentals=0
        ),
        name="assemble",
    )(*parts)


def lane_sum(parts):
    total = None
    for part in parts:
        for at in range(0, part.shape[1], HD):
            piece = part[:, at : at + HD]
            total = piece if total is None else total + piece
    return jnp.sum(total, axis=1, keepdims=True)


def modulate_kernel(t_ref, h0, h1, h2, h3, cond, mod, weight, out_ref, weight_out, sem):
    copy = pltpu.make_async_copy(weight, weight_out, sem.at[0])
    copy.start()
    chunks = (h0, h1, h2, h3)
    for row in range(0, ROWS, GROUP):
        rows = slice(row, row + GROUP)
        lanes = [chunk[rows].astype(F32) for chunk in chunks]
        mean = lane_sum([(lanes[0] + lanes[1]) + (lanes[2] + lanes[3])]) * (1.0 / D)
        deviation = lane_sum([(part - mean) * (part - mean) for part in lanes])
        rstd = lax.rsqrt(deviation * (1.0 / D) + EPS)
        conditioned = cond[rows, 0:1] > 0.5
        for c in range(TP):
            cols = pl.ds(pl.multiple_of(t_ref[c] * CHUNK, CHUNK), CHUNK)
            gain = jnp.where(conditioned, mod[1:2, cols], mod[0:1, cols])
            bias = jnp.where(conditioned, mod[3:4, cols], mod[2:3, cols])
            normed = (lanes[c] - mean) * rstd
            out_ref[rows, cols] = (normed * gain + bias).astype(BF16)
    copy.wait()


def modulate(blocks, chunks, cond, mod, weight):
    return pl.pallas_call(
        modulate_kernel,
        out_shape=[
            jax.ShapeDtypeStruct((ROWS, D), BF16),
            jax.ShapeDtypeStruct((D, WIDTH), BF16),
        ],
        in_specs=[smem()] + [vmem()] * 6 + [pl.BlockSpec(memory_space=pltpu.HBM)],
        out_specs=[vmem()] * 2,
        scratch_shapes=[pltpu.SemaphoreType.DMA((1,))],
        compiler_params=params(MODULATE_MIB),
        cost_estimate=pl.CostEstimate(
            flops=12 * ROWS * D, bytes_accessed=20_000_000, transcendentals=0
        ),
        name="modulate",
    )(blocks, *chunks, cond, mod, weight)


def squares_kernel(q_ref, k_ref, out_ref):
    query, key = q_ref[...], k_ref[...]
    out_ref[...] = columns_to_rows(
        jnp.sum(query * query, axis=1, keepdims=True),
        jnp.sum(key * key, axis=1, keepdims=True),
    )


def sum_squares(query, key):
    return pl.pallas_call(
        squares_kernel,
        out_shape=jax.ShapeDtypeStruct((8, STAT_LANES), F32),
        in_specs=[vmem()] * 2,
        out_specs=vmem(),
        compiler_params=params(VMEM_MIB),
        cost_estimate=pl.CostEstimate(
            flops=4 * ROWS * WIDTH, bytes_accessed=8 * ROWS * WIDTH, transcendentals=0
        ),
        name="sum_squares",
    )(query, key)


def rope_kernel(u_ref, q_ref, k_ref, s0, s1, s2, s3, qg, kg, cos, sin, k_all, *refs):
    sends, q_rot = refs[0:4], refs[4]
    total = s0[...] + s1[...] + s2[...] + s3[...]
    inverse = lax.rsqrt(total * (1.0 / (HEADS * HD)) + EPS)
    even = lax.broadcasted_iota(jnp.int32, (ROWS, HD), 1) % 2 == 0
    cos_rows = jnp.concatenate([cos[...], cos[...]], axis=0)
    sin_rows = jnp.concatenate([sin[...], sin[...]], axis=0)

    def rotate(ref, column, gain, cols):
        part = ref[:, cols] * column * gain[cols].reshape(1, HD)
        swap = jnp.where(even, pltpu.roll(part, HD - 1, 1), pltpu.roll(part, 1, 1))
        return (part * cos_rows + swap * sin_rows).astype(BF16)

    q_column = row_to_column(inverse[0:1])
    k_column = row_to_column(inverse[1:2])
    for head in range(LOCAL_HEADS):
        cols = slice(head * HD, (head + 1) * HD)
        query = rotate(q_ref, q_column, qg, cols)
        for s in range(B):
            q_rot[head, s] = query[s * TOK : (s + 1) * TOK]
        k_all[:, cols] = rotate(k_ref, k_column, kg, cols)
    for k in range(4):
        for s in range(B):
            sends[k][s, 0] = q_rot[lax.rem(u_ref[0] + k, 4), s]
            sends[k][s, 1] = q_rot[4, s]


def norm_rope(u, query, key, squares, q_gain, k_gain, cos, sin):
    send = jax.ShapeDtypeStruct((B, 2, TOK, HD), BF16)
    flat = jax.ShapeDtypeStruct((ROWS, WIDTH), BF16)
    return pl.pallas_call(
        rope_kernel,
        out_shape=[flat] + [send] * 4,
        in_specs=[smem()] + [vmem()] * 10,
        out_specs=[vmem()] * 5,
        scratch_shapes=[pltpu.VMEM((LOCAL_HEADS, B, TOK, HD), BF16)],
        compiler_params=params(VMEM_MIB),
        cost_estimate=pl.CostEstimate(
            flops=20 * ROWS * WIDTH, bytes_accessed=16 * ROWS * WIDTH, transcendentals=0
        ),
        name="norm_rope",
    )(u, query, key, *squares, q_gain, k_gain, cos, sin)


def scores_of(query, keys):
    return lax.dot_general(query, keys, (((1,), (1,)), ((), ())), preferred_element_type=F32)


def to_rows(blocks):
    lane = lax.broadcasted_iota(jnp.int32, (HD, HD), 1)
    table = jnp.zeros((HD, HD), F32)
    empty = jnp.zeros((2 * HD - TOK, HD), F32)
    for n, block in enumerate(blocks):
        rest = jnp.concatenate([block[HD:TOK], empty], axis=0)
        table = jnp.where(lane == 2 * n, block[0:HD], table)
        table = jnp.where(lane == 2 * n + 1, rest, table)
    return table.T


FRESH_ROWS = 24


def fresh_kernel(u_ref, k_ref, v_ref, *refs):
    queries, (out_ref, rows_ref) = refs[0:4], refs[4:6]
    lses = []
    for s in range(B):
        rows = slice(s * TOK, (s + 1) * TOK)
        for k in range(LOCAL_HEADS):
            head = lax.rem(u_ref[0] + k, 4) if k < 4 else 4
            cols = pl.ds(pl.multiple_of(head * HD, HD), HD)
            query = queries[k][s, 0] if k < 4 else queries[0][s, 1]
            scores = scores_of(query, k_ref[rows, cols])
            top = jnp.max(scores, axis=1, keepdims=True)
            probs = jnp.exp2((scores - top) * SCORE_SCALE)
            total = jnp.sum(probs, axis=1, keepdims=True)
            out = jnp.dot(probs.astype(BF16), v_ref[rows, cols], preferred_element_type=F32)
            out_ref[s, k] = out / total
            lses.append(jnp.broadcast_to(top * SCORE_SCALE + jnp.log2(total), (TOK, HD)))
    rows_ref[...] = to_rows(lses)[0:FRESH_ROWS]


def fresh_attention(u, key, value, queries):
    return pl.pallas_call(
        fresh_kernel,
        out_shape=[
            jax.ShapeDtypeStruct((B, LOCAL_HEADS, TOK, HD), F32),
            jax.ShapeDtypeStruct((FRESH_ROWS, HD), F32),
        ],
        in_specs=[smem()] + [vmem()] * 6,
        out_specs=[vmem()] * 2,
        compiler_params=params(VMEM_MIB),
        cost_estimate=pl.CostEstimate(
            flops=4 * ROWS * TOK * WIDTH,
            bytes_accessed=14 * ROWS * WIDTH,
            transcendentals=ROWS * TOK * LOCAL_HEADS,
        ),
        name="fresh_attention",
    )(u, key, value, *queries)


TILE = 2 * TOK
PER_PIECE = 4 * TOK
KEYS = 4 * PER_PIECE
KEYS_LAST = 4 * TOK
SPLIT = 768


def stale_kernel(far, *refs):
    queries = refs[0:4]
    pieces, rest = refs[4:8], refs[8:]
    if far:
        near_out, near_lse = rest[0:2]
        msgs = rest[3:7]
    else:
        out_ref, lse_ref = rest[0:2]
    lse_s, acc_s, k_main, v_main, k_last, v_last, scores_s, probs_s = rest[-8:]

    jobs = [(s, e, tile) for s in range(B) for e in range(2) for tile in range(2)]

    def size(i):
        return KEYS_LAST if jobs[i][1] else KEYS

    def score_steps(i):
        s, e, tile = jobs[i]
        keys = k_last if e else k_main
        out = scores_s.at[i % 2]

        def arrive():
            v_main[s, :, HD:] = jnp.ones((KEYS, HD), BF16)
            v_last[s, :, HD:] = jnp.ones((KEYS_LAST, HD), BF16)
            for n, piece in enumerate(pieces):
                main = slice(n * PER_PIECE, (n + 1) * PER_PIECE)
                last = slice(n * TOK, (n + 1) * TOK)
                k_main[s, main] = piece[s, 0, 0:PER_PIECE]
                k_last[s, last] = piece[s, 0, PER_PIECE:PIECE]
                v_main[s, main, 0:HD] = piece[s, 1, 0:PER_PIECE]
                v_last[s, last, 0:HD] = piece[s, 1, PER_PIECE:PIECE]

        def step(at, end):
            query = jnp.concatenate([queries[2 * tile][s, e], queries[2 * tile + 1][s, e]], axis=0)
            out[:, at:end] = scores_of(query, keys[s, at:end])

        def hide():
            for n in range(2):
                r = 2 * tile + n
                rows = slice(n * TOK, (n + 1) * TOK)
                if e and r:
                    continue
                out[rows, r * TOK : (r + 1) * TOK] = jnp.full((TOK, TOK), MASKED, F32)

        steps = [] if i % 4 else [arrive]
        for at in range(0, size(i), SPLIT):
            steps.append(functools.partial(step, at, min(at + SPLIT, size(i))))
        return steps if far else steps + [hide]

    def softmax_steps(i, tops):
        def step(row):
            rows = slice(row, row + GROUP)
            part = scores_s[i % 2, rows, 0 : size(i)]
            top = jnp.max(part, axis=1, keepdims=True)
            probs = jnp.exp2((part - top) * SCORE_SCALE)
            tops.append(top)
            probs_s[i % 2, rows, 0 : size(i)] = probs.astype(BF16)

        return [functools.partial(step, row) for row in range(0, TILE, GROUP)]

    def product_steps(i, tops):
        s, e, tile = jobs[i]
        values = v_last if e else v_main

        def step(at, end):
            part = jnp.dot(
                probs_s[i % 2, :, at:end], values[s, at:end], preferred_element_type=F32
            )
            acc_s[...] = part if at == 0 else acc_s[...] + part

        def finish():
            top = jnp.concatenate(tops, axis=0)
            total = acc_s[:, HD:]
            out = acc_s[:, 0:HD] / total
            lse = top * SCORE_SCALE + jnp.log2(total)
            for n in range(2):
                r = 2 * tile + n
                half = slice(n * TOK, (n + 1) * TOK)
                if not far:
                    out_ref[s, r, e] = out[half]
                    lse_ref[s, r, e] = lse[half]
                    continue
                lse_near = near_lse[s, r, e]
                high = jnp.maximum(lse[half], lse_near)
                weight, weight_near = jnp.exp2(lse[half] - high), jnp.exp2(lse_near - high)
                both = weight + weight_near
                value = (out[half] * weight + near_out[s, r, e] * weight_near) / both
                lse_s[s, r, e] = high + jnp.log2(both)
                msgs[r][s, e * TOK : (e + 1) * TOK] = value.astype(BF16)

        steps = []
        for at in range(0, size(i), SPLIT):
            steps.append(functools.partial(step, at, min(at + SPLIT, size(i))))
        return steps + [finish]

    def weave(*lists):
        order = []
        for steps in lists:
            order += [((n + 0.5) / len(steps), step) for n, step in enumerate(steps)]
        for _, step in sorted(order, key=lambda entry: entry[0]):
            step()

    weave(score_steps(0))
    pending = None
    for i in range(len(jobs)):
        tops = []
        lists = [softmax_steps(i, tops)]
        if i + 1 < len(jobs):
            lists.append(score_steps(i + 1))
        if pending is not None:
            lists.append(pending)
        weave(*lists)
        pending = product_steps(i, tops)
    weave(pending)

    if far:
        order = [(r, s) for r in range(4) for s in range(B)]
        flat = to_rows([lse_s[s, r, e] for r, s in order for e in range(2)])
        for n, (r, s) in enumerate(order):
            part = flat[n * 4 : n * 4 + 4]
            high = part.astype(BF16).astype(F32)
            middle = (part - high).astype(BF16).astype(F32)
            low = part - high - middle
            stack = jnp.concatenate([high, middle, low, jnp.zeros((4, HD), F32)], axis=0)
            msgs[r][s, 2 * TOK : MSG_ROWS] = stack.astype(BF16)


def stale_attention(queries, pieces, near=None, after=None):
    far = near is not None
    args = [*queries, *pieces]
    in_specs = [vmem()] * 8
    if far:
        args += [*near, after]
        in_specs += [vmem(), vmem(), pl.BlockSpec(memory_space=pl.ANY)]
        out_shape = [jax.ShapeDtypeStruct((B, MSG_ROWS, HD), BF16)] * 4
    else:
        out_shape = [jax.ShapeDtypeStruct((B, 4, 2, TOK, HD), F32)] * 2
    work = B * 4 * TOK * (KEYS + KEYS_LAST)
    return pl.pallas_call(
        functools.partial(stale_kernel, far),
        out_shape=out_shape,
        in_specs=in_specs,
        out_specs=[vmem()] * len(out_shape),
        scratch_shapes=[
            pltpu.VMEM((B, 4, 2, TOK, HD), F32),
            pltpu.VMEM((TILE, 2 * HD), F32),
            pltpu.VMEM((B, KEYS, HD), BF16),
            pltpu.VMEM((B, KEYS, 2 * HD), BF16),
            pltpu.VMEM((B, KEYS_LAST, HD), BF16),
            pltpu.VMEM((B, KEYS_LAST, 2 * HD), BF16),
            pltpu.VMEM((2, TILE, KEYS), F32),
            pltpu.VMEM((2, TILE, KEYS), BF16),
        ],
        compiler_params=params(ATTENTION_MIB),
        cost_estimate=pl.CostEstimate(
            flops=4 * work * HD, bytes_accessed=8 * (KEYS + KEYS_LAST) * HD, transcendentals=work
        ),
        name="far_attention" if far else "near_attention",
    )(*args)


def merge_kernel(u_ref, fresh_out, fresh_rows, *refs):
    msgs, out_ref = refs[0:4], refs[4]
    lses = {}
    for k in range(4):
        for s in range(B):
            stack = msgs[k][s, 2 * TOK : MSG_ROWS].astype(F32)
            lses[s, k] = stack[0:4] + stack[4:8] + stack[8:12]
    weights, jobs = [], []
    for s in range(B):
        for k in range(LOCAL_HEADS):
            at = (s * LOCAL_HEADS + k) * 2
            parts = [(None, fresh_rows[at : at + 2])]
            if k < 4:
                parts.append((k, lses[s, k][0:2]))
            else:
                parts += [(n, lses[s, n][2:4]) for n in range(4)]
            top = parts[0][1]
            for _, lse in parts[1:]:
                top = jnp.maximum(top, lse)
            raw = [jnp.exp2(lse - top) for _, lse in parts]
            total = sum(raw[1:], raw[0])
            jobs.append((s, k, [(source, len(weights) + n) for n, (source, _) in enumerate(parts)]))
            weights += [one / total for one in raw]
    filler = jnp.zeros((HD - 2 * len(weights), HD), F32)
    table = jnp.concatenate(weights + [filler], axis=0).T
    for s, k, parts in jobs:
        head = lax.rem(u_ref[0] + k, 4) if k < 4 else 4
        out = [None, None]
        for source, n in parts:
            for half, rows in enumerate((slice(0, HD), slice(HD, TOK))):
                if source is None:
                    value = fresh_out[s, k, rows]
                else:
                    at = 0 if k < 4 else TOK
                    value = msgs[source][s, at + rows.start : at + rows.stop].astype(F32)
                column = table[0 : rows.stop - rows.start, 2 * n + half : 2 * n + half + 1]
                term = value * column
                out[half] = term if out[half] is None else out[half] + term
        cols = pl.ds(pl.multiple_of(head * HD, HD), HD)
        out_ref[s, :, cols] = jnp.concatenate(out, axis=0).astype(BF16)


def merge(u, fresh_out, fresh_rows, msgs):
    return pl.pallas_call(
        merge_kernel,
        out_shape=jax.ShapeDtypeStruct((B, TOK, WIDTH), BF16),
        in_specs=[smem()] + [vmem()] * 6,
        out_specs=vmem(),
        compiler_params=params(VMEM_MIB),
        cost_estimate=pl.CostEstimate(
            flops=10 * ROWS * WIDTH, bytes_accessed=14 * ROWS * WIDTH, transcendentals=0
        ),
        name="merge",
    )(u, fresh_out, fresh_rows, *msgs)


def shards(
    hidden,
    mod_shift,
    mod_scale,
    w_query,
    w_key,
    w_value,
    q_gain,
    k_gain,
    token_place,
    stale_keys,
    stale_values,
):
    patch = lax.axis_index("patch")
    tp = lax.axis_index("tp")
    y = patch // (NX * NZ)
    x = (patch // NZ) % NX
    u = jnp.where(tp % 2 == 0, y, x).astype(jnp.int32).reshape(1)
    own_rows = hidden.reshape(ROWS, CHUNK)
    z_rows = swap_tp(own_rows, 1, 0)
    core_rows = swap_tp(own_rows, 0, 1)

    packed = pack_stale(u, stale_keys, stale_values)
    arrived = exchange_u(packed)
    near = assemble([*arrived, packed[4]])
    cond, cos, sin, mod, own_rows = tables(token_place, own_rows, mod_shift, mod_scale, near)
    near_one, near_three = swap_v(near, 1), swap_v(near, 3)
    far = swap_z_hi(near)

    z_rows, cond = lax.optimization_barrier((z_rows, cond))
    cross_rows = swap_tp(z_rows, 0, 1)
    near_two = swap_v(near_one, 3)
    blocks = jnp.stack([tp, tp ^ 1, tp ^ 2, tp ^ 3]).astype(jnp.int32)
    modded, key_weights = modulate(
        blocks, [own_rows, core_rows, z_rows, cross_rows], cond, mod, w_key
    )
    query = jnp.dot(modded, w_query, preferred_element_type=F32)
    key = jnp.dot(modded, key_weights, preferred_element_type=F32)
    fresh_values = jnp.dot(modded, w_value, preferred_element_type=F32).astype(BF16)
    own_sq = sum_squares(query, key)
    own_sq, near_three = lax.optimization_barrier((own_sq, near_three))
    squares = [own_sq] + [swap_tp(own_sq, z, c) for z, c in ((1, 1), (1, 0), (0, 1))]
    near_two, *squares = lax.optimization_barrier((near_two, *squares))
    far_two = swap_z_hi(near_two)
    fresh_keys, *sends = norm_rope(u, query, key, squares, q_gain, k_gain, cos, sin)
    far, fresh_keys = lax.optimization_barrier((far, fresh_keys))
    far_one, far_three = swap_v(far, 1), swap_v(far, 3)
    queries = exchange_u(sends)
    fresh_out, fresh_rows = fresh_attention(u, fresh_keys, fresh_values, sends)

    partial = stale_attention(queries, [near, near_one, near_three, near_two])
    outs = stale_attention(
        queries, [far, far_one, far_three, far_two], near=partial, after=fresh_rows
    )
    returned = exchange_u(outs)
    attended = merge(u, fresh_out, fresh_rows, returned)
    return (
        attended,
        fresh_keys.reshape(B, TOK, WIDTH),
        fresh_values.reshape(B, TOK, WIDTH),
    )


def solution(mesh):
    in_specs = (
        P(None, "patch", "tp"),
        P(),
        P(),
        P(None, "tp"),
        P(None, "tp"),
        P(None, "tp"),
        P("tp"),
        P("tp"),
        P("patch"),
        P(None, "patch", "tp"),
        P(None, "patch", "tp"),
    )
    out_specs = (P(None, "patch", "tp"), P(None, "patch", "tp"), P(None, "patch", "tp"))
    return jax.shard_map(shards, mesh=mesh, in_specs=in_specs, out_specs=out_specs, check_vma=False)
```

```python
import functools
import math

import jax
import jax.numpy as jnp
import numpy as np
from jax import lax
from jax.experimental import pallas as pl
from jax.experimental.pallas import tpu as pltpu
from jax.sharding import PartitionSpec as P

D = 5120
HEADS = 20
HD = 128
FRAMES = 3
GRID_W = 48
EPS = 1e-06
MASKED = -1e30
NY, NX, NZ = 4, 4, 2
TP = 4
N_PATCH = NY * NX * NZ
TOK = 144
B = 2
ROWS = B * TOK
LOCAL_HEADS = 5
WIDTH = LOCAL_HEADS * HD
CHUNK = D // TP
STAT_LANES = 384
PIECE = 5 * TOK
MSG_ROWS = 2 * TOK + 16
SCORE_SCALE = math.log2(math.e) / math.sqrt(HD)
F32 = jnp.float32
BF16 = jnp.bfloat16
AXES = ("patch", "tp")
GROUP = 16
VMEM_MIB = 24
ATTENTION_MIB = 34


def params(mib):
    return pltpu.CompilerParams(vmem_limit_bytes=mib * 1024 * 1024)


def vmem():
    return pl.BlockSpec(memory_space=pltpu.VMEM)


def smem():
    return pl.BlockSpec(memory_space=pltpu.SMEM)


def linear(u, v, z_hi, z_lo, core):
    y, x = (u, v) if core == 0 else (v, u)
    return ((y * NX + x) * NZ + z_hi) * TP + z_lo * 2 + core


def places():
    return [
        (u, v, h, l, c)
        for u in range(4)
        for v in range(4)
        for h in range(2)
        for l in range(2)
        for c in range(2)
    ]


def permute(value, move):
    return lax.ppermute(value, AXES, [(linear(*p), linear(*move(*p))) for p in places()])


def shift_u(value, k):
    return permute(value, lambda u, v, h, l, c: ((u + k) % 4, v, h, l, c))


def swap_v(value, mask):
    return permute(value, lambda u, v, h, l, c: (u, v ^ mask, h, l, c))


def exchange_u(values):
    came = {r: shift_u(values[4 - r], 4 - r) for r in (2, 1, 3)}
    return [values[0], came[1], came[2], came[3]]


def swap_z_hi(value):
    return permute(value, lambda u, v, h, l, c: (u, v, 1 - h, l, c))


def swap_tp(value, z, core):
    if core:
        return permute(value, lambda u, v, h, l, c: (v, u, h, l ^ z, 1 - c))
    return permute(value, lambda u, v, h, l, c: (u, v, h, l ^ z, c))


def frequencies():
    half_dim = HD // 2
    third_dim = half_dim // 3
    frame_pairs = half_dim - 2 * third_dim
    pair = np.arange(HD) // 2
    offset = np.where(
        pair < frame_pairs,
        pair,
        np.where(pair < frame_pairs + third_dim, pair - frame_pairs, pair - frame_pairs - third_dim),
    )
    width = np.where(pair < frame_pairs, 2 * frame_pairs, 2 * third_dim)
    return np.exp(-math.log(10000.0) * 2.0 * offset / width).astype(np.float32).reshape(1, HD)


def columns_to_rows(first, second):
    lane = lax.broadcasted_iota(jnp.int32, (ROWS, 128), 1)
    both = jnp.where(lane == 0, first, jnp.where(lane == 1, second, 0.0))
    padded = jnp.concatenate([both, jnp.zeros((STAT_LANES - ROWS, 128), F32)], axis=0)
    return padded.T[0:8]


def row_to_column(row):
    return jnp.broadcast_to(row, (128, STAT_LANES)).T[0:ROWS]


def pack_kernel(u_ref, key_ref, value_ref, *outs):
    for k in range(5):
        head = lax.rem(u_ref[0] + k, 4) if k < 4 else 4
        cols = pl.ds(pl.multiple_of(head * HD, HD), HD)
        for n, source in enumerate((key_ref, value_ref)):
            for s in range(B):
                outs[k][s, n] = source[s, :, cols]


def pack_stale(u, stale_keys, stale_values):
    return pl.pallas_call(
        pack_kernel,
        out_shape=[jax.ShapeDtypeStruct((B, 2, TOK, HD), BF16)] * 5,
        in_specs=[smem(), vmem(), vmem()],
        out_specs=[vmem()] * 5,
        compiler_params=params(VMEM_MIB),
        cost_estimate=pl.CostEstimate(
            flops=0, bytes_accessed=8 * ROWS * WIDTH, transcendentals=0
        ),
        name="pack_stale",
    )(u, stale_keys, stale_values)


def tables_kernel(place_hbm, freq, rows, shift, scale, after, *refs):
    cond, cos, sin, mod, rows_out, places_s, place_ref, sem = refs
    copy = pltpu.make_async_copy(place_hbm, place_ref, sem.at[0])
    copy.start()
    copy.wait()
    for row in range(TOK):
        places_s[row : row + 1] = jnp.full((1, HD), place_ref[row], jnp.int32)
    place = places_s[...]
    frame_tok = TOK * N_PATCH // FRAMES
    frame = jnp.where(place >= frame_tok, 1, 0) + jnp.where(place >= 2 * frame_tok, 1, 0)
    within = place - frame * frame_tok
    grid_row = ((within.astype(F32) + 0.5) * (1.0 / GRID_W)).astype(jnp.int32)
    grid_col = within - grid_row * GRID_W
    lane = lax.broadcasted_iota(jnp.int32, (TOK, HD), 1)
    third = 2 * (HD // 6)
    frame_lanes = HD - 2 * third
    position = jnp.where(
        lane < frame_lanes, frame, jnp.where(lane < frame_lanes + third, grid_row, grid_col)
    )
    angles = position.astype(F32) * freq[...]
    cos[...] = jnp.cos(angles)
    sine = jnp.sin(angles)
    sin[...] = jnp.where(lane % 2 == 0, -sine, sine)
    flag = jnp.where((frame == 0) | (frame == FRAMES - 1), 1.0, 0.0)
    cond[0:TOK] = flag
    cond[TOK:ROWS] = flag
    mod[0:2] = 1.0 + scale[...]
    mod[2:4] = shift[...]
    rows_out[...] = rows[...]


def tables(token_place, rows, shift, scale, after):
    table = jax.ShapeDtypeStruct((TOK, HD), F32)
    return pl.pallas_call(
        tables_kernel,
        out_shape=[
            jax.ShapeDtypeStruct((ROWS, HD), F32),
            table,
            table,
            jax.ShapeDtypeStruct((4, D), F32),
            jax.ShapeDtypeStruct((ROWS, CHUNK), BF16),
        ],
        in_specs=[pl.BlockSpec(memory_space=pltpu.HBM)]
        + [vmem()] * 4
        + [pl.BlockSpec(memory_space=pl.ANY)],
        out_specs=[vmem()] * 5,
        scratch_shapes=[
            pltpu.VMEM((TOK, HD), jnp.int32),
            pltpu.SMEM((TOK,), jnp.int32),
            pltpu.SemaphoreType.DMA((1,)),
        ],
        compiler_params=params(VMEM_MIB),
        cost_estimate=pl.CostEstimate(
            flops=100 * TOK * HD, bytes_accessed=1_000_000, transcendentals=0
        ),
        name="tables",
    )(token_place, jnp.asarray(frequencies()), rows, shift, scale, after)


def assemble_kernel(*refs):
    parts, out = refs[0:5], refs[5]
    for s in range(B):
        for n in range(2):
            for r in range(5):
                out[s, n, r * TOK : (r + 1) * TOK] = parts[r][s, n]


def assemble(parts):
    return pl.pallas_call(
        assemble_kernel,
        out_shape=jax.ShapeDtypeStruct((B, 2, PIECE, HD), BF16),
        in_specs=[vmem()] * 5,
        out_specs=vmem(),
        compiler_params=params(VMEM_MIB),
        cost_estimate=pl.CostEstimate(
            flops=0, bytes_accessed=16 * PIECE * HD, transcendentals=0
        ),
        name="assemble",
    )(*parts)


def lane_sum(parts):
    total = None
    for part in parts:
        for at in range(0, part.shape[1], HD):
            piece = part[:, at : at + HD]
            total = piece if total is None else total + piece
    return jnp.sum(total, axis=1, keepdims=True)


def modulate_kernel(t_ref, h0, h1, h2, h3, cond, mod, out_ref):
    chunks = (h0, h1, h2, h3)
    for row in range(0, ROWS, GROUP):
        rows = slice(row, row + GROUP)
        lanes = [chunk[rows].astype(F32) for chunk in chunks]
        mean = lane_sum([(lanes[0] + lanes[1]) + (lanes[2] + lanes[3])]) * (1.0 / D)
        deviation = lane_sum([(part - mean) * (part - mean) for part in lanes])
        rstd = lax.rsqrt(deviation * (1.0 / D) + EPS)
        conditioned = cond[rows, 0:1] > 0.5
        for c in range(TP):
            cols = pl.ds(pl.multiple_of(t_ref[c] * CHUNK, CHUNK), CHUNK)
            gain = jnp.where(conditioned, mod[1:2, cols], mod[0:1, cols])
            bias = jnp.where(conditioned, mod[3:4, cols], mod[2:3, cols])
            normed = (lanes[c] - mean) * rstd
            out_ref[rows, cols] = (normed * gain + bias).astype(BF16)


def modulate(blocks, chunks, cond, mod):
    return pl.pallas_call(
        modulate_kernel,
        out_shape=jax.ShapeDtypeStruct((ROWS, D), BF16),
        in_specs=[smem()] + [vmem()] * 6,
        out_specs=vmem(),
        compiler_params=params(VMEM_MIB),
        cost_estimate=pl.CostEstimate(
            flops=12 * ROWS * D, bytes_accessed=20_000_000, transcendentals=0
        ),
        name="modulate",
    )(blocks, *chunks, cond, mod)


def squares_kernel(q_ref, k_ref, out_ref):
    query, key = q_ref[...], k_ref[...]
    out_ref[...] = columns_to_rows(
        jnp.sum(query * query, axis=1, keepdims=True),
        jnp.sum(key * key, axis=1, keepdims=True),
    )


def sum_squares(query, key):
    return pl.pallas_call(
        squares_kernel,
        out_shape=jax.ShapeDtypeStruct((8, STAT_LANES), F32),
        in_specs=[vmem()] * 2,
        out_specs=vmem(),
        compiler_params=params(VMEM_MIB),
        cost_estimate=pl.CostEstimate(
            flops=4 * ROWS * WIDTH, bytes_accessed=8 * ROWS * WIDTH, transcendentals=0
        ),
        name="sum_squares",
    )(query, key)


def rope_kernel(u_ref, q_ref, k_ref, s0, s1, s2, s3, qg, kg, cos, sin, k_all, *refs):
    sends, q_rot = refs[0:4], refs[4]
    total = s0[...] + s1[...] + s2[...] + s3[...]
    inverse = lax.rsqrt(total * (1.0 / (HEADS * HD)) + EPS)
    even = lax.broadcasted_iota(jnp.int32, (ROWS, HD), 1) % 2 == 0
    cos_rows = jnp.concatenate([cos[...], cos[...]], axis=0)
    sin_rows = jnp.concatenate([sin[...], sin[...]], axis=0)

    def rotate(ref, column, gain, cols):
        part = ref[:, cols] * column * gain[cols].reshape(1, HD)
        swap = jnp.where(even, pltpu.roll(part, HD - 1, 1), pltpu.roll(part, 1, 1))
        return (part * cos_rows + swap * sin_rows).astype(BF16)

    q_column = row_to_column(inverse[0:1])
    k_column = row_to_column(inverse[1:2])
    for head in range(LOCAL_HEADS):
        cols = slice(head * HD, (head + 1) * HD)
        query = rotate(q_ref, q_column, qg, cols)
        for s in range(B):
            q_rot[head, s] = query[s * TOK : (s + 1) * TOK]
        k_all[:, cols] = rotate(k_ref, k_column, kg, cols)
    for k in range(4):
        for s in range(B):
            sends[k][s, 0] = q_rot[lax.rem(u_ref[0] + k, 4), s]
            sends[k][s, 1] = q_rot[4, s]


def norm_rope(u, query, key, squares, q_gain, k_gain, cos, sin):
    send = jax.ShapeDtypeStruct((B, 2, TOK, HD), BF16)
    flat = jax.ShapeDtypeStruct((ROWS, WIDTH), BF16)
    return pl.pallas_call(
        rope_kernel,
        out_shape=[flat] + [send] * 4,
        in_specs=[smem()] + [vmem()] * 10,
        out_specs=[vmem()] * 5,
        scratch_shapes=[pltpu.VMEM((LOCAL_HEADS, B, TOK, HD), BF16)],
        compiler_params=params(VMEM_MIB),
        cost_estimate=pl.CostEstimate(flops=1000, bytes_accessed=1000, transcendentals=0),
        name="norm_rope",
    )(u, query, key, *squares, q_gain, k_gain, cos, sin)


def scores_of(query, keys):
    return lax.dot_general(query, keys, (((1,), (1,)), ((), ())), preferred_element_type=F32)


def to_rows(blocks):
    lane = lax.broadcasted_iota(jnp.int32, (HD, HD), 1)
    table = jnp.zeros((HD, HD), F32)
    empty = jnp.zeros((2 * HD - TOK, HD), F32)
    for n, block in enumerate(blocks):
        rest = jnp.concatenate([block[HD:TOK], empty], axis=0)
        table = jnp.where(lane == 2 * n, block[0:HD], table)
        table = jnp.where(lane == 2 * n + 1, rest, table)
    return table.T


FRESH_ROWS = 24


def fresh_kernel(u_ref, k_ref, v_ref, *refs):
    queries, (out_ref, rows_ref) = refs[0:4], refs[4:6]
    lses = []
    for s in range(B):
        rows = slice(s * TOK, (s + 1) * TOK)
        for k in range(LOCAL_HEADS):
            head = lax.rem(u_ref[0] + k, 4) if k < 4 else 4
            cols = pl.ds(pl.multiple_of(head * HD, HD), HD)
            query = queries[k][s, 0] if k < 4 else queries[0][s, 1]
            scores = scores_of(query, k_ref[rows, cols])
            top = jnp.max(scores, axis=1, keepdims=True)
            probs = jnp.exp2((scores - top) * SCORE_SCALE)
            total = jnp.sum(probs, axis=1, keepdims=True)
            out = jnp.dot(probs.astype(BF16), v_ref[rows, cols], preferred_element_type=F32)
            out_ref[s, k] = out / total
            lses.append(jnp.broadcast_to(top * SCORE_SCALE + jnp.log2(total), (TOK, HD)))
    rows_ref[...] = to_rows(lses)[0:FRESH_ROWS]


def fresh_attention(u, key, value, queries):
    return pl.pallas_call(
        fresh_kernel,
        out_shape=[
            jax.ShapeDtypeStruct((B, LOCAL_HEADS, TOK, HD), F32),
            jax.ShapeDtypeStruct((FRESH_ROWS, HD), F32),
        ],
        in_specs=[smem()] + [vmem()] * 6,
        out_specs=[vmem()] * 2,
        compiler_params=params(VMEM_MIB),
        cost_estimate=pl.CostEstimate(flops=1000, bytes_accessed=1000, transcendentals=0),
        name="fresh_attention",
    )(u, key, value, *queries)


TILE = 2 * TOK
PER_PIECE = 4 * TOK
SPLIT = 768


def stale_kernel(far, count, *refs):
    queries = refs[0:4]
    pieces, rest = refs[4 : 4 + count], refs[4 + count :]
    keys_main, keys_last = count * PER_PIECE, count * TOK
    if far:
        near_out, near_lse = rest[0:2]
        msgs = rest[3:7]
    else:
        out_ref, lse_ref = rest[0:2]
    lse_s, acc_s, k_main, v_main, k_last, v_last, scores_s, probs_s = rest[-8:]

    jobs = [(s, e, tile) for s in range(B) for e in range(2) for tile in range(2)]

    def size(i):
        return keys_last if jobs[i][1] else keys_main

    def score_steps(i):
        s, e, tile = jobs[i]
        keys = k_last if e else k_main
        out = scores_s.at[i % 2]

        def arrive():
            v_main[s, :, HD:] = jnp.ones((keys_main, HD), BF16)
            v_last[s, :, HD:] = jnp.ones((keys_last, HD), BF16)
            for n, piece in enumerate(pieces):
                main = slice(n * PER_PIECE, (n + 1) * PER_PIECE)
                last = slice(n * TOK, (n + 1) * TOK)
                k_main[s, main] = piece[s, 0, 0:PER_PIECE]
                k_last[s, last] = piece[s, 0, PER_PIECE:PIECE]
                v_main[s, main, 0:HD] = piece[s, 1, 0:PER_PIECE]
                v_last[s, last, 0:HD] = piece[s, 1, PER_PIECE:PIECE]

        def step(at, end):
            query = jnp.concatenate([queries[2 * tile][s, e], queries[2 * tile + 1][s, e]], axis=0)
            out[:, at:end] = scores_of(query, keys[s, at:end])

        def hide():
            for n in range(2):
                r = 2 * tile + n
                rows = slice(n * TOK, (n + 1) * TOK)
                if e and r:
                    continue
                out[rows, r * TOK : (r + 1) * TOK] = jnp.full((TOK, TOK), MASKED, F32)

        steps = [] if i % 4 else [arrive]
        for at in range(0, size(i), SPLIT):
            steps.append(functools.partial(step, at, min(at + SPLIT, size(i))))
        return steps if far else steps + [hide]

    def softmax_steps(i, tops):
        def step(row):
            rows = slice(row, row + GROUP)
            part = scores_s[i % 2, rows, 0 : size(i)]
            top = jnp.max(part, axis=1, keepdims=True)
            probs = jnp.exp2((part - top) * SCORE_SCALE)
            tops.append(top)
            probs_s[i % 2, rows, 0 : size(i)] = probs.astype(BF16)

        return [functools.partial(step, row) for row in range(0, TILE, GROUP)]

    def product_steps(i, tops):
        s, e, tile = jobs[i]
        values = v_last if e else v_main

        def step(at, end):
            part = jnp.dot(
                probs_s[i % 2, :, at:end], values[s, at:end], preferred_element_type=F32
            )
            acc_s[...] = part if at == 0 else acc_s[...] + part

        def finish():
            top = jnp.concatenate(tops, axis=0)
            total = acc_s[:, HD:]
            out = acc_s[:, 0:HD] / total
            lse = top * SCORE_SCALE + jnp.log2(total)
            for n in range(2):
                r = 2 * tile + n
                half = slice(n * TOK, (n + 1) * TOK)
                if not far:
                    out_ref[s, r, e] = out[half]
                    lse_ref[s, r, e] = lse[half]
                    continue
                lse_near = near_lse[s, r, e]
                high = jnp.maximum(lse[half], lse_near)
                weight, weight_near = jnp.exp2(lse[half] - high), jnp.exp2(lse_near - high)
                both = weight + weight_near
                value = (out[half] * weight + near_out[s, r, e] * weight_near) / both
                lse_s[s, r, e] = high + jnp.log2(both)
                msgs[r][s, e * TOK : (e + 1) * TOK] = value.astype(BF16)

        steps = []
        for at in range(0, size(i), SPLIT):
            steps.append(functools.partial(step, at, min(at + SPLIT, size(i))))
        return steps + [finish]

    def weave(*lists):
        order = []
        for steps in lists:
            order += [((n + 0.5) / len(steps), step) for n, step in enumerate(steps)]
        for _, step in sorted(order, key=lambda entry: entry[0]):
            step()

    weave(score_steps(0))
    pending = None
    for i in range(len(jobs)):
        tops = []
        lists = [softmax_steps(i, tops)]
        if i + 1 < len(jobs):
            lists.append(score_steps(i + 1))
        if pending is not None:
            lists.append(pending)
        weave(*lists)
        pending = product_steps(i, tops)
    weave(pending)

    if far:
        order = [(r, s) for r in range(4) for s in range(B)]
        flat = to_rows([lse_s[s, r, e] for r, s in order for e in range(2)])
        for n, (r, s) in enumerate(order):
            part = flat[n * 4 : n * 4 + 4]
            high = part.astype(BF16).astype(F32)
            middle = (part - high).astype(BF16).astype(F32)
            low = part - high - middle
            stack = jnp.concatenate([high, middle, low, jnp.zeros((4, HD), F32)], axis=0)
            msgs[r][s, 2 * TOK : MSG_ROWS] = stack.astype(BF16)


def stale_attention(queries, pieces, near=None, after=None):
    far = near is not None
    args = [*queries, *pieces]
    count = len(pieces)
    keys_main, keys_last = count * PER_PIECE, count * TOK
    in_specs = [vmem()] * (4 + count)
    if far:
        args += [*near, after]
        in_specs += [vmem(), vmem(), pl.BlockSpec(memory_space=pl.ANY)]
        out_shape = [jax.ShapeDtypeStruct((B, MSG_ROWS, HD), BF16)] * 4
    else:
        out_shape = [jax.ShapeDtypeStruct((B, 4, 2, TOK, HD), F32)] * 2
    return pl.pallas_call(
        functools.partial(stale_kernel, far, count),
        out_shape=out_shape,
        in_specs=in_specs,
        out_specs=[vmem()] * len(out_shape),
        scratch_shapes=[
            pltpu.VMEM((B, 4, 2, TOK, HD), F32),
            pltpu.VMEM((TILE, 2 * HD), F32),
            pltpu.VMEM((B, keys_main, HD), BF16),
            pltpu.VMEM((B, keys_main, 2 * HD), BF16),
            pltpu.VMEM((B, keys_last, HD), BF16),
            pltpu.VMEM((B, keys_last, 2 * HD), BF16),
            pltpu.VMEM((2, TILE, keys_main), F32),
            pltpu.VMEM((2, TILE, keys_main), BF16),
        ],
        compiler_params=params(ATTENTION_MIB),
        cost_estimate=pl.CostEstimate(flops=1000, bytes_accessed=1000, transcendentals=0),
        name="far_attention" if far else "near_attention",
    )(*args)


def merge_kernel(u_ref, fresh_out, fresh_rows, *refs):
    msgs, out_ref = refs[0:4], refs[4]
    lses = {}
    for k in range(4):
        for s in range(B):
            stack = msgs[k][s, 2 * TOK : MSG_ROWS].astype(F32)
            lses[s, k] = stack[0:4] + stack[4:8] + stack[8:12]
    weights, jobs = [], []
    for s in range(B):
        for k in range(LOCAL_HEADS):
            at = (s * LOCAL_HEADS + k) * 2
            parts = [(None, fresh_rows[at : at + 2])]
            if k < 4:
                parts.append((k, lses[s, k][0:2]))
            else:
                parts += [(n, lses[s, n][2:4]) for n in range(4)]
            top = parts[0][1]
            for _, lse in parts[1:]:
                top = jnp.maximum(top, lse)
            raw = [jnp.exp2(lse - top) for _, lse in parts]
            total = sum(raw[1:], raw[0])
            jobs.append((s, k, [(source, len(weights) + n) for n, (source, _) in enumerate(parts)]))
            weights += [one / total for one in raw]
    filler = jnp.zeros((HD - 2 * len(weights), HD), F32)
    table = jnp.concatenate(weights + [filler], axis=0).T
    for s, k, parts in jobs:
        head = lax.rem(u_ref[0] + k, 4) if k < 4 else 4
        out = [None, None]
        for source, n in parts:
            for half, rows in enumerate((slice(0, HD), slice(HD, TOK))):
                if source is None:
                    value = fresh_out[s, k, rows]
                else:
                    at = 0 if k < 4 else TOK
                    value = msgs[source][s, at + rows.start : at + rows.stop].astype(F32)
                column = table[0 : rows.stop - rows.start, 2 * n + half : 2 * n + half + 1]
                term = value * column
                out[half] = term if out[half] is None else out[half] + term
        cols = pl.ds(pl.multiple_of(head * HD, HD), HD)
        out_ref[s, :, cols] = jnp.concatenate(out, axis=0).astype(BF16)


def merge(u, fresh_out, fresh_rows, msgs):
    return pl.pallas_call(
        merge_kernel,
        out_shape=jax.ShapeDtypeStruct((B, TOK, WIDTH), BF16),
        in_specs=[smem()] + [vmem()] * 6,
        out_specs=vmem(),
        compiler_params=params(VMEM_MIB),
        cost_estimate=pl.CostEstimate(
            flops=10 * ROWS * WIDTH, bytes_accessed=14 * ROWS * WIDTH, transcendentals=0
        ),
        name="merge",
    )(u, fresh_out, fresh_rows, *msgs)


def shards(
    hidden,
    mod_shift,
    mod_scale,
    w_query,
    w_key,
    w_value,
    q_gain,
    k_gain,
    token_place,
    stale_keys,
    stale_values,
):
    patch = lax.axis_index("patch")
    tp = lax.axis_index("tp")
    y = patch // (NX * NZ)
    x = (patch // NZ) % NX
    u = jnp.where(tp % 2 == 0, y, x).astype(jnp.int32).reshape(1)
    own_rows = hidden.reshape(ROWS, CHUNK)
    z_rows = swap_tp(own_rows, 1, 0)
    core_rows = swap_tp(own_rows, 0, 1)

    packed = pack_stale(u, stale_keys, stale_values)
    arrived = exchange_u(packed)
    near = assemble([*arrived, packed[4]])
    cond, cos, sin, mod, own_rows = tables(token_place, own_rows, mod_shift, mod_scale, near)
    near_one, near_three = swap_v(near, 1), swap_v(near, 3)
    far = swap_z_hi(near)

    z_rows, cond = lax.optimization_barrier((z_rows, cond))
    cross_rows = swap_tp(z_rows, 0, 1)
    near_one, near_three = lax.optimization_barrier((near_one, near_three))
    near_two = swap_v(near_one, 3)
    blocks = jnp.stack([tp, tp ^ 1, tp ^ 2, tp ^ 3]).astype(jnp.int32)
    modded = modulate(blocks, [own_rows, core_rows, z_rows, cross_rows], cond, mod)
    query = jnp.dot(modded, w_query, preferred_element_type=F32)
    key = jnp.dot(modded, w_key, preferred_element_type=F32)
    fresh_values = jnp.dot(modded, w_value, preferred_element_type=F32).astype(BF16)
    own_sq = sum_squares(query, key)
    squares = [own_sq] + [swap_tp(own_sq, z, c) for z, c in ((1, 1), (1, 0), (0, 1))]
    near_two, far, fresh_values, *squares = lax.optimization_barrier(
        (near_two, far, fresh_values, *squares)
    )
    far_two = swap_z_hi(near_two)
    far_one, far_three = swap_v(far, 1), swap_v(far, 3)
    fresh_keys, *sends = norm_rope(u, query, key, squares, q_gain, k_gain, cos, sin)
    queries = exchange_u(sends)
    fresh_out, fresh_rows = fresh_attention(u, fresh_keys, fresh_values, sends)

    partial = stale_attention(queries, [near, near_one, near_three, near_two, far])
    outs = stale_attention(
        queries, [far_one, far_three, far_two], near=partial, after=fresh_rows
    )
    returned = exchange_u(outs)
    attended = merge(u, fresh_out, fresh_rows, returned)
    return (
        attended,
        fresh_keys.reshape(B, TOK, WIDTH),
        fresh_values.reshape(B, TOK, WIDTH),
    )


def solution(mesh):
    in_specs = (
        P(None, "patch", "tp"),
        P(),
        P(),
        P(None, "tp"),
        P(None, "tp"),
        P(None, "tp"),
        P("tp"),
        P("tp"),
        P("patch"),
        P(None, "patch", "tp"),
        P(None, "patch", "tp"),
    )
    out_specs = (P(None, "patch", "tp"), P(None, "patch", "tp"), P(None, "patch", "tp"))
    return jax.shard_map(shards, mesh=mesh, in_specs=in_specs, out_specs=out_specs, check_vma=False)
```

```python
import functools
import math

import jax
import jax.numpy as jnp
import numpy as np
from jax import lax
from jax.experimental import pallas as pl
from jax.experimental.pallas import tpu as pltpu
from jax.sharding import PartitionSpec as P

D = 5120
HEADS = 20
HD = 128
FRAMES = 3
GRID_W = 48
EPS = 1e-06
MASKED = -1e30
NY, NX, NZ = 4, 4, 2
TP = 4
N_PATCH = NY * NX * NZ
TOK = 144
B = 2
ROWS = B * TOK
LOCAL_HEADS = 5
WIDTH = LOCAL_HEADS * HD
CHUNK = D // TP
STAT_LANES = 384
PIECE = 5 * TOK
MSG_ROWS = 2 * TOK + 16
SCORE_SCALE = math.log2(math.e) / math.sqrt(HD)
F32 = jnp.float32
BF16 = jnp.bfloat16
AXES = ("patch", "tp")
GROUP = 16
VMEM_MIB = 24
ATTENTION_MIB = 34


def params(mib):
    return pltpu.CompilerParams(vmem_limit_bytes=mib * 1024 * 1024)


def vmem():
    return pl.BlockSpec(memory_space=pltpu.VMEM)


def smem():
    return pl.BlockSpec(memory_space=pltpu.SMEM)


def linear(u, v, z_hi, z_lo, core):
    y, x = (u, v) if core == 0 else (v, u)
    return ((y * NX + x) * NZ + z_hi) * TP + z_lo * 2 + core


def places():
    return [
        (u, v, h, l, c)
        for u in range(4)
        for v in range(4)
        for h in range(2)
        for l in range(2)
        for c in range(2)
    ]


def permute(value, move):
    return lax.ppermute(value, AXES, [(linear(*p), linear(*move(*p))) for p in places()])


def swap_u(value, mask):
    return permute(value, lambda u, v, h, l, c: (u ^ mask, v, h, l, c))


def swap_v(value, mask):
    return permute(value, lambda u, v, h, l, c: (u, v ^ mask, h, l, c))


def exchange_u(values):
    relayed = swap_u(values[2], 1)
    came_three = swap_u(values[3], 3)
    came_one = swap_u(values[1], 1)
    return [values[0], came_one, swap_u(relayed, 3), came_three]


def swap_z_hi(value):
    return permute(value, lambda u, v, h, l, c: (u, v, 1 - h, l, c))


def swap_tp(value, z, core):
    if core:
        return permute(value, lambda u, v, h, l, c: (v, u, h, l ^ z, 1 - c))
    return permute(value, lambda u, v, h, l, c: (u, v, h, l ^ z, c))


def frequencies():
    half_dim = HD // 2
    third_dim = half_dim // 3
    frame_pairs = half_dim - 2 * third_dim
    pair = np.arange(HD) // 2
    offset = np.where(
        pair < frame_pairs,
        pair,
        np.where(pair < frame_pairs + third_dim, pair - frame_pairs, pair - frame_pairs - third_dim),
    )
    width = np.where(pair < frame_pairs, 2 * frame_pairs, 2 * third_dim)
    return np.exp(-math.log(10000.0) * 2.0 * offset / width).astype(np.float32).reshape(1, HD)


def columns_to_rows(first, second):
    lane = lax.broadcasted_iota(jnp.int32, (ROWS, 128), 1)
    both = jnp.where(lane == 0, first, jnp.where(lane == 1, second, 0.0))
    padded = jnp.concatenate([both, jnp.zeros((STAT_LANES - ROWS, 128), F32)], axis=0)
    return padded.T[0:8]


def row_to_column(row):
    return jnp.broadcast_to(row, (128, STAT_LANES)).T[0:ROWS]


def pack_kernel(u_ref, key_ref, value_ref, *outs):
    for k in range(5):
        head = (u_ref[0] ^ k) if k < 4 else 4
        cols = pl.ds(pl.multiple_of(head * HD, HD), HD)
        for n, source in enumerate((key_ref, value_ref)):
            for s in range(B):
                outs[k][s, n] = source[s, :, cols]


def pack_stale(u, stale_keys, stale_values):
    return pl.pallas_call(
        pack_kernel,
        out_shape=[jax.ShapeDtypeStruct((B, 2, TOK, HD), BF16)] * 5,
        in_specs=[smem(), vmem(), vmem()],
        out_specs=[vmem()] * 5,
        compiler_params=params(VMEM_MIB),
        cost_estimate=pl.CostEstimate(
            flops=0, bytes_accessed=8 * ROWS * WIDTH, transcendentals=0
        ),
        name="pack_stale",
    )(u, stale_keys, stale_values)


def tables_kernel(place_hbm, freq, rows, shift, scale, after, *refs):
    cond, cos, sin, mod, rows_out, places_s, place_ref, sem = refs
    copy = pltpu.make_async_copy(place_hbm, place_ref, sem.at[0])
    copy.start()
    copy.wait()
    for row in range(TOK):
        places_s[row : row + 1] = jnp.full((1, HD), place_ref[row], jnp.int32)
    place = places_s[...]
    frame_tok = TOK * N_PATCH // FRAMES
    frame = jnp.where(place >= frame_tok, 1, 0) + jnp.where(place >= 2 * frame_tok, 1, 0)
    within = place - frame * frame_tok
    grid_row = ((within.astype(F32) + 0.5) * (1.0 / GRID_W)).astype(jnp.int32)
    grid_col = within - grid_row * GRID_W
    lane = lax.broadcasted_iota(jnp.int32, (TOK, HD), 1)
    third = 2 * (HD // 6)
    frame_lanes = HD - 2 * third
    position = jnp.where(
        lane < frame_lanes, frame, jnp.where(lane < frame_lanes + third, grid_row, grid_col)
    )
    angles = position.astype(F32) * freq[...]
    cos[...] = jnp.cos(angles)
    sine = jnp.sin(angles)
    sin[...] = jnp.where(lane % 2 == 0, -sine, sine)
    flag = jnp.where((frame == 0) | (frame == FRAMES - 1), 1.0, 0.0)
    cond[0:TOK] = flag
    cond[TOK:ROWS] = flag
    mod[0:2] = 1.0 + scale[...]
    mod[2:4] = shift[...]
    rows_out[...] = rows[...]


def tables(token_place, rows, shift, scale, after):
    table = jax.ShapeDtypeStruct((TOK, HD), F32)
    return pl.pallas_call(
        tables_kernel,
        out_shape=[
            jax.ShapeDtypeStruct((ROWS, HD), F32),
            table,
            table,
            jax.ShapeDtypeStruct((4, D), F32),
            jax.ShapeDtypeStruct((ROWS, CHUNK), BF16),
        ],
        in_specs=[pl.BlockSpec(memory_space=pltpu.HBM)]
        + [vmem()] * 4
        + [pl.BlockSpec(memory_space=pl.ANY)],
        out_specs=[vmem()] * 5,
        scratch_shapes=[
            pltpu.VMEM((TOK, HD), jnp.int32),
            pltpu.SMEM((TOK,), jnp.int32),
            pltpu.SemaphoreType.DMA((1,)),
        ],
        compiler_params=params(VMEM_MIB),
        cost_estimate=pl.CostEstimate(
            flops=100 * TOK * HD, bytes_accessed=1_000_000, transcendentals=0
        ),
        name="tables",
    )(token_place, jnp.asarray(frequencies()), rows, shift, scale, after)


def assemble_kernel(*refs):
    parts, out = refs[0:5], refs[5]
    for s in range(B):
        for n in range(2):
            for r in range(5):
                out[s, n, r * TOK : (r + 1) * TOK] = parts[r][s, n]


def assemble(parts):
    return pl.pallas_call(
        assemble_kernel,
        out_shape=jax.ShapeDtypeStruct((B, 2, PIECE, HD), BF16),
        in_specs=[vmem()] * 5,
        out_specs=vmem(),
        compiler_params=params(VMEM_MIB),
        cost_estimate=pl.CostEstimate(
            flops=0, bytes_accessed=16 * PIECE * HD, transcendentals=0
        ),
        name="assemble",
    )(*parts)


def lane_sum(parts):
    total = None
    for part in parts:
        for at in range(0, part.shape[1], HD):
            piece = part[:, at : at + HD]
            total = piece if total is None else total + piece
    return jnp.sum(total, axis=1, keepdims=True)


def modulate_kernel(t_ref, h0, h1, h2, h3, cond, mod, out_ref):
    chunks = (h0, h1, h2, h3)
    for row in range(0, ROWS, GROUP):
        rows = slice(row, row + GROUP)
        lanes = [chunk[rows].astype(F32) for chunk in chunks]
        mean = lane_sum([(lanes[0] + lanes[1]) + (lanes[2] + lanes[3])]) * (1.0 / D)
        deviation = lane_sum([(part - mean) * (part - mean) for part in lanes])
        rstd = lax.rsqrt(deviation * (1.0 / D) + EPS)
        conditioned = cond[rows, 0:1] > 0.5
        for c in range(TP):
            cols = pl.ds(pl.multiple_of(t_ref[c] * CHUNK, CHUNK), CHUNK)
            gain = jnp.where(conditioned, mod[1:2, cols], mod[0:1, cols])
            bias = jnp.where(conditioned, mod[3:4, cols], mod[2:3, cols])
            normed = (lanes[c] - mean) * rstd
            out_ref[rows, cols] = (normed * gain + bias).astype(BF16)


def modulate(blocks, chunks, cond, mod):
    return pl.pallas_call(
        modulate_kernel,
        out_shape=jax.ShapeDtypeStruct((ROWS, D), BF16),
        in_specs=[smem()] + [vmem()] * 6,
        out_specs=vmem(),
        compiler_params=params(VMEM_MIB),
        cost_estimate=pl.CostEstimate(
            flops=12 * ROWS * D, bytes_accessed=20_000_000, transcendentals=0
        ),
        name="modulate",
    )(blocks, *chunks, cond, mod)


def squares_kernel(q_ref, k_ref, out_ref):
    query, key = q_ref[...], k_ref[...]
    out_ref[...] = columns_to_rows(
        jnp.sum(query * query, axis=1, keepdims=True),
        jnp.sum(key * key, axis=1, keepdims=True),
    )


def sum_squares(query, key):
    return pl.pallas_call(
        squares_kernel,
        out_shape=jax.ShapeDtypeStruct((8, STAT_LANES), F32),
        in_specs=[vmem()] * 2,
        out_specs=vmem(),
        compiler_params=params(VMEM_MIB),
        cost_estimate=pl.CostEstimate(
            flops=4 * ROWS * WIDTH, bytes_accessed=8 * ROWS * WIDTH, transcendentals=0
        ),
        name="sum_squares",
    )(query, key)


def rope_kernel(u_ref, q_ref, k_ref, s0, s1, s2, s3, qg, kg, cos, sin, k_all, *refs):
    sends, q_rot = refs[0:4], refs[4]
    total = s0[...] + s1[...] + s2[...] + s3[...]
    inverse = lax.rsqrt(total * (1.0 / (HEADS * HD)) + EPS)
    even = lax.broadcasted_iota(jnp.int32, (ROWS, HD), 1) % 2 == 0
    cos_rows = jnp.concatenate([cos[...], cos[...]], axis=0)
    sin_rows = jnp.concatenate([sin[...], sin[...]], axis=0)

    def rotate(ref, column, gain, cols):
        part = ref[:, cols] * column * gain[cols].reshape(1, HD)
        swap = jnp.where(even, pltpu.roll(part, HD - 1, 1), pltpu.roll(part, 1, 1))
        return (part * cos_rows + swap * sin_rows).astype(BF16)

    q_column = row_to_column(inverse[0:1])
    k_column = row_to_column(inverse[1:2])
    for head in range(LOCAL_HEADS):
        cols = slice(head * HD, (head + 1) * HD)
        query = rotate(q_ref, q_column, qg, cols)
        for s in range(B):
            q_rot[head, s] = query[s * TOK : (s + 1) * TOK]
        k_all[:, cols] = rotate(k_ref, k_column, kg, cols)
    for k in range(4):
        for s in range(B):
            sends[k][s, 0] = q_rot[(u_ref[0] ^ k), s]
            sends[k][s, 1] = q_rot[4, s]


def norm_rope(u, query, key, squares, q_gain, k_gain, cos, sin):
    send = jax.ShapeDtypeStruct((B, 2, TOK, HD), BF16)
    flat = jax.ShapeDtypeStruct((ROWS, WIDTH), BF16)
    return pl.pallas_call(
        rope_kernel,
        out_shape=[flat] + [send] * 4,
        in_specs=[smem()] + [vmem()] * 10,
        out_specs=[vmem()] * 5,
        scratch_shapes=[pltpu.VMEM((LOCAL_HEADS, B, TOK, HD), BF16)],
        compiler_params=params(VMEM_MIB),
        cost_estimate=pl.CostEstimate(flops=1000, bytes_accessed=1000, transcendentals=0),
        name="norm_rope",
    )(u, query, key, *squares, q_gain, k_gain, cos, sin)


def scores_of(query, keys):
    return lax.dot_general(query, keys, (((1,), (1,)), ((), ())), preferred_element_type=F32)


def to_rows(blocks):
    lane = lax.broadcasted_iota(jnp.int32, (HD, HD), 1)
    table = jnp.zeros((HD, HD), F32)
    empty = jnp.zeros((2 * HD - TOK, HD), F32)
    for n, block in enumerate(blocks):
        rest = jnp.concatenate([block[HD:TOK], empty], axis=0)
        table = jnp.where(lane == 2 * n, block[0:HD], table)
        table = jnp.where(lane == 2 * n + 1, rest, table)
    return table.T


FRESH_ROWS = 24


def fresh_kernel(u_ref, k_ref, v_ref, *refs):
    queries, (out_ref, rows_ref) = refs[0:4], refs[4:6]
    lses = []
    for s in range(B):
        rows = slice(s * TOK, (s + 1) * TOK)
        for k in range(LOCAL_HEADS):
            head = (u_ref[0] ^ k) if k < 4 else 4
            cols = pl.ds(pl.multiple_of(head * HD, HD), HD)
            query = queries[k][s, 0] if k < 4 else queries[0][s, 1]
            scores = scores_of(query, k_ref[rows, cols])
            top = jnp.max(scores, axis=1, keepdims=True)
            probs = jnp.exp2((scores - top) * SCORE_SCALE)
            total = jnp.sum(probs, axis=1, keepdims=True)
            out = jnp.dot(probs.astype(BF16), v_ref[rows, cols], preferred_element_type=F32)
            out_ref[s, k] = out / total
            lses.append(jnp.broadcast_to(top * SCORE_SCALE + jnp.log2(total), (TOK, HD)))
    rows_ref[...] = to_rows(lses)[0:FRESH_ROWS]


def fresh_attention(u, key, value, queries):
    return pl.pallas_call(
        fresh_kernel,
        out_shape=[
            jax.ShapeDtypeStruct((B, LOCAL_HEADS, TOK, HD), F32),
            jax.ShapeDtypeStruct((FRESH_ROWS, HD), F32),
        ],
        in_specs=[smem()] + [vmem()] * 6,
        out_specs=[vmem()] * 2,
        compiler_params=params(VMEM_MIB),
        cost_estimate=pl.CostEstimate(flops=1000, bytes_accessed=1000, transcendentals=0),
        name="fresh_attention",
    )(u, key, value, *queries)


TILE = 2 * TOK
PER_PIECE = 4 * TOK
SPLIT = 768


def stale_kernel(far, count, *refs):
    queries = refs[0:4]
    pieces, rest = refs[4 : 4 + count], refs[4 + count :]
    keys_main, keys_last = count * PER_PIECE, count * TOK
    if far:
        near_out, near_lse = rest[0:2]
        msgs = rest[3:7]
    else:
        out_ref, lse_ref = rest[0:2]
    lse_s, acc_s, k_main, v_main, k_last, v_last, scores_s, probs_s = rest[-8:]

    jobs = [(s, e, tile) for s in range(B) for e in range(2) for tile in range(2)]

    def size(i):
        return keys_last if jobs[i][1] else keys_main

    def score_steps(i):
        s, e, tile = jobs[i]
        keys = k_last if e else k_main
        out = scores_s.at[i % 2]

        def arrive():
            v_main[s, :, HD:] = jnp.ones((keys_main, HD), BF16)
            v_last[s, :, HD:] = jnp.ones((keys_last, HD), BF16)
            for n, piece in enumerate(pieces):
                main = slice(n * PER_PIECE, (n + 1) * PER_PIECE)
                last = slice(n * TOK, (n + 1) * TOK)
                k_main[s, main] = piece[s, 0, 0:PER_PIECE]
                k_last[s, last] = piece[s, 0, PER_PIECE:PIECE]
                v_main[s, main, 0:HD] = piece[s, 1, 0:PER_PIECE]
                v_last[s, last, 0:HD] = piece[s, 1, PER_PIECE:PIECE]

        def step(at, end):
            query = jnp.concatenate([queries[2 * tile][s, e], queries[2 * tile + 1][s, e]], axis=0)
            out[:, at:end] = scores_of(query, keys[s, at:end])

        def hide():
            for n in range(2):
                r = 2 * tile + n
                rows = slice(n * TOK, (n + 1) * TOK)
                if e and r:
                    continue
                out[rows, r * TOK : (r + 1) * TOK] = jnp.full((TOK, TOK), MASKED, F32)

        steps = [] if i % 4 else [arrive]
        for at in range(0, size(i), SPLIT):
            steps.append(functools.partial(step, at, min(at + SPLIT, size(i))))
        return steps if far else steps + [hide]

    def softmax_steps(i, tops):
        def step(row):
            rows = slice(row, row + GROUP)
            part = scores_s[i % 2, rows, 0 : size(i)]
            top = jnp.max(part, axis=1, keepdims=True)
            probs = jnp.exp2((part - top) * SCORE_SCALE)
            tops.append(top)
            probs_s[i % 2, rows, 0 : size(i)] = probs.astype(BF16)

        return [functools.partial(step, row) for row in range(0, TILE, GROUP)]

    def product_steps(i, tops):
        s, e, tile = jobs[i]
        values = v_last if e else v_main

        def step(at, end):
            part = jnp.dot(
                probs_s[i % 2, :, at:end], values[s, at:end], preferred_element_type=F32
            )
            acc_s[...] = part if at == 0 else acc_s[...] + part

        def finish():
            top = jnp.concatenate(tops, axis=0)
            total = acc_s[:, HD:]
            out = acc_s[:, 0:HD] / total
            lse = top * SCORE_SCALE + jnp.log2(total)
            for n in range(2):
                r = 2 * tile + n
                half = slice(n * TOK, (n + 1) * TOK)
                if not far:
                    out_ref[s, r, e] = out[half]
                    lse_ref[s, r, e] = lse[half]
                    continue
                lse_near = near_lse[s, r, e]
                high = jnp.maximum(lse[half], lse_near)
                weight, weight_near = jnp.exp2(lse[half] - high), jnp.exp2(lse_near - high)
                both = weight + weight_near
                value = (out[half] * weight + near_out[s, r, e] * weight_near) / both
                lse_s[s, r, e] = high + jnp.log2(both)
                msgs[r][s, e * TOK : (e + 1) * TOK] = value.astype(BF16)

        steps = []
        for at in range(0, size(i), SPLIT):
            steps.append(functools.partial(step, at, min(at + SPLIT, size(i))))
        return steps + [finish]

    def weave(*lists):
        order = []
        for steps in lists:
            order += [((n + 0.5) / len(steps), step) for n, step in enumerate(steps)]
        for _, step in sorted(order, key=lambda entry: entry[0]):
            step()

    weave(score_steps(0))
    pending = None
    for i in range(len(jobs)):
        tops = []
        lists = [softmax_steps(i, tops)]
        if i + 1 < len(jobs):
            lists.append(score_steps(i + 1))
        if pending is not None:
            lists.append(pending)
        weave(*lists)
        pending = product_steps(i, tops)
    weave(pending)

    if far:
        order = [(r, s) for r in range(4) for s in range(B)]
        flat = to_rows([lse_s[s, r, e] for r, s in order for e in range(2)])
        for n, (r, s) in enumerate(order):
            part = flat[n * 4 : n * 4 + 4]
            high = part.astype(BF16).astype(F32)
            middle = (part - high).astype(BF16).astype(F32)
            low = part - high - middle
            stack = jnp.concatenate([high, middle, low, jnp.zeros((4, HD), F32)], axis=0)
            msgs[r][s, 2 * TOK : MSG_ROWS] = stack.astype(BF16)


def stale_attention(queries, pieces, near=None, after=None):
    far = near is not None
    args = [*queries, *pieces]
    count = len(pieces)
    keys_main, keys_last = count * PER_PIECE, count * TOK
    in_specs = [vmem()] * (4 + count)
    if far:
        args += [*near, after]
        in_specs += [vmem(), vmem(), pl.BlockSpec(memory_space=pl.ANY)]
        out_shape = [jax.ShapeDtypeStruct((B, MSG_ROWS, HD), BF16)] * 4
    else:
        out_shape = [jax.ShapeDtypeStruct((B, 4, 2, TOK, HD), F32)] * 2
    return pl.pallas_call(
        functools.partial(stale_kernel, far, count),
        out_shape=out_shape,
        in_specs=in_specs,
        out_specs=[vmem()] * len(out_shape),
        scratch_shapes=[
            pltpu.VMEM((B, 4, 2, TOK, HD), F32),
            pltpu.VMEM((TILE, 2 * HD), F32),
            pltpu.VMEM((B, keys_main, HD), BF16),
            pltpu.VMEM((B, keys_main, 2 * HD), BF16),
            pltpu.VMEM((B, keys_last, HD), BF16),
            pltpu.VMEM((B, keys_last, 2 * HD), BF16),
            pltpu.VMEM((2, TILE, keys_main), F32),
            pltpu.VMEM((2, TILE, keys_main), BF16),
        ],
        compiler_params=params(ATTENTION_MIB),
        cost_estimate=pl.CostEstimate(flops=1000, bytes_accessed=1000, transcendentals=0),
        name="far_attention" if far else "near_attention",
    )(*args)


def merge_kernel(u_ref, fresh_out, fresh_rows, *refs):
    msgs, out_ref = refs[0:4], refs[4]
    lses = {}
    for k in range(4):
        for s in range(B):
            stack = msgs[k][s, 2 * TOK : MSG_ROWS].astype(F32)
            lses[s, k] = stack[0:4] + stack[4:8] + stack[8:12]
    weights, jobs = [], []
    for s in range(B):
        for k in range(LOCAL_HEADS):
            at = (s * LOCAL_HEADS + k) * 2
            parts = [(None, fresh_rows[at : at + 2])]
            if k < 4:
                parts.append((k, lses[s, k][0:2]))
            else:
                parts += [(n, lses[s, n][2:4]) for n in range(4)]
            top = parts[0][1]
            for _, lse in parts[1:]:
                top = jnp.maximum(top, lse)
            raw = [jnp.exp2(lse - top) for _, lse in parts]
            total = sum(raw[1:], raw[0])
            jobs.append((s, k, [(source, len(weights) + n) for n, (source, _) in enumerate(parts)]))
            weights += [one / total for one in raw]
    filler = jnp.zeros((HD - 2 * len(weights), HD), F32)
    table = jnp.concatenate(weights + [filler], axis=0).T
    for s, k, parts in jobs:
        head = (u_ref[0] ^ k) if k < 4 else 4
        out = [None, None]
        for source, n in parts:
            for half, rows in enumerate((slice(0, HD), slice(HD, TOK))):
                if source is None:
                    value = fresh_out[s, k, rows]
                else:
                    at = 0 if k < 4 else TOK
                    value = msgs[source][s, at + rows.start : at + rows.stop].astype(F32)
                column = table[0 : rows.stop - rows.start, 2 * n + half : 2 * n + half + 1]
                term = value * column
                out[half] = term if out[half] is None else out[half] + term
        cols = pl.ds(pl.multiple_of(head * HD, HD), HD)
        out_ref[s, :, cols] = jnp.concatenate(out, axis=0).astype(BF16)


def merge(u, fresh_out, fresh_rows, msgs):
    return pl.pallas_call(
        merge_kernel,
        out_shape=jax.ShapeDtypeStruct((B, TOK, WIDTH), BF16),
        in_specs=[smem()] + [vmem()] * 6,
        out_specs=vmem(),
        compiler_params=params(VMEM_MIB),
        cost_estimate=pl.CostEstimate(
            flops=10 * ROWS * WIDTH, bytes_accessed=14 * ROWS * WIDTH, transcendentals=0
        ),
        name="merge",
    )(u, fresh_out, fresh_rows, *msgs)


def shards(
    hidden,
    mod_shift,
    mod_scale,
    w_query,
    w_key,
    w_value,
    q_gain,
    k_gain,
    token_place,
    stale_keys,
    stale_values,
):
    patch = lax.axis_index("patch")
    tp = lax.axis_index("tp")
    y = patch // (NX * NZ)
    x = (patch // NZ) % NX
    u = jnp.where(tp % 2 == 0, y, x).astype(jnp.int32).reshape(1)
    own_rows = hidden.reshape(ROWS, CHUNK)
    z_rows = swap_tp(own_rows, 1, 0)
    core_rows = swap_tp(own_rows, 0, 1)

    packed = pack_stale(u, stale_keys, stale_values)
    arrived = exchange_u(packed)
    near = assemble([*arrived, packed[4]])
    cond, cos, sin, mod, own_rows = tables(token_place, own_rows, mod_shift, mod_scale, near)
    near_one, near_three = swap_v(near, 1), swap_v(near, 3)
    far = swap_z_hi(near)

    z_rows, cond = lax.optimization_barrier((z_rows, cond))
    cross_rows = swap_tp(z_rows, 0, 1)
    blocks = jnp.stack([tp, tp ^ 1, tp ^ 2, tp ^ 3]).astype(jnp.int32)
    modded = modulate(blocks, [own_rows, core_rows, z_rows, cross_rows], cond, mod)
    query = jnp.dot(modded, w_query, preferred_element_type=F32)
    near_one, near_three, query = lax.optimization_barrier((near_one, near_three, query))
    near_two = swap_v(near_one, 3)
    key = jnp.dot(modded, w_key, preferred_element_type=F32)
    fresh_values = jnp.dot(modded, w_value, preferred_element_type=F32).astype(BF16)
    own_sq = sum_squares(query, key)
    squares = [own_sq] + [swap_tp(own_sq, z, c) for z, c in ((1, 1), (1, 0), (0, 1))]
    far, fresh_values, *squares = lax.optimization_barrier((far, fresh_values, *squares))
    far_one, far_three = swap_v(far, 1), swap_v(far, 3)
    fresh_keys, *sends = norm_rope(u, query, key, squares, q_gain, k_gain, cos, sin)
    near_two, fresh_keys = lax.optimization_barrier((near_two, fresh_keys))
    far_two = swap_z_hi(near_two)
    queries = exchange_u(sends)
    fresh_out, fresh_rows = fresh_attention(u, fresh_keys, fresh_values, sends)

    partial = stale_attention(queries, [near, near_one, near_three, near_two, far])
    outs = stale_attention(
        queries, [far_one, far_three, far_two], near=partial, after=fresh_rows
    )
    returned = exchange_u(outs)
    attended = merge(u, fresh_out, fresh_rows, returned)
    return (
        attended,
        fresh_keys.reshape(B, TOK, WIDTH),
        fresh_values.reshape(B, TOK, WIDTH),
    )


def solution(mesh):
    in_specs = (
        P(None, "patch", "tp"),
        P(),
        P(),
        P(None, "tp"),
        P(None, "tp"),
        P(None, "tp"),
        P("tp"),
        P("tp"),
        P("patch"),
        P(None, "patch", "tp"),
        P(None, "patch", "tp"),
    )
    out_specs = (P(None, "patch", "tp"), P(None, "patch", "tp"), P(None, "patch", "tp"))
    return jax.shard_map(shards, mesh=mesh, in_specs=in_specs, out_specs=out_specs, check_vma=False)
```

```python
import functools
import math

import jax
import jax.numpy as jnp
import numpy as np
from jax import lax
from jax.experimental import pallas as pl
from jax.experimental.pallas import tpu as pltpu
from jax.sharding import PartitionSpec as P

D = 5120
HEADS = 20
HD = 128
FRAMES = 3
GRID_W = 48
EPS = 1e-06
MASKED = -1e30
NY, NX, NZ = 4, 4, 2
TP = 4
N_PATCH = NY * NX * NZ
TOK = 144
B = 2
ROWS = B * TOK
LOCAL_HEADS = 5
WIDTH = LOCAL_HEADS * HD
CHUNK = D // TP
STAT_LANES = 384
PIECE = 5 * TOK
MSG_ROWS = 2 * TOK + 16
SCORE_SCALE = math.log2(math.e) / math.sqrt(HD)
F32 = jnp.float32
BF16 = jnp.bfloat16
AXES = ("patch", "tp")
GROUP = 16
VMEM_MIB = 24
ATTENTION_MIB = 34
MODULATE_MIB = 42


def params(mib):
    return pltpu.CompilerParams(vmem_limit_bytes=mib * 1024 * 1024)


def vmem():
    return pl.BlockSpec(memory_space=pltpu.VMEM)


def smem():
    return pl.BlockSpec(memory_space=pltpu.SMEM)


def linear(u, v, z_hi, z_lo, core):
    y, x = (u, v) if core == 0 else (v, u)
    return ((y * NX + x) * NZ + z_hi) * TP + z_lo * 2 + core


def places():
    return [
        (u, v, h, l, c)
        for u in range(4)
        for v in range(4)
        for h in range(2)
        for l in range(2)
        for c in range(2)
    ]


def permute(value, move):
    return lax.ppermute(value, AXES, [(linear(*p), linear(*move(*p))) for p in places()])


def shift_u(value, k):
    return permute(value, lambda u, v, h, l, c: ((u + k) % 4, v, h, l, c))


def swap_v(value, mask):
    return permute(value, lambda u, v, h, l, c: (u, v ^ mask, h, l, c))


def exchange_u(values):
    came = {r: shift_u(values[4 - r], 4 - r) for r in (2, 1, 3)}
    return [values[0], came[1], came[2], came[3]]


def swap_z_hi(value):
    return permute(value, lambda u, v, h, l, c: (u, v, 1 - h, l, c))


def swap_tp(value, z, core):
    if core:
        return permute(value, lambda u, v, h, l, c: (v, u, h, l ^ z, 1 - c))
    return permute(value, lambda u, v, h, l, c: (u, v, h, l ^ z, c))


def frequencies():
    half_dim = HD // 2
    third_dim = half_dim // 3
    frame_pairs = half_dim - 2 * third_dim
    pair = np.arange(HD) // 2
    offset = np.where(
        pair < frame_pairs,
        pair,
        np.where(pair < frame_pairs + third_dim, pair - frame_pairs, pair - frame_pairs - third_dim),
    )
    width = np.where(pair < frame_pairs, 2 * frame_pairs, 2 * third_dim)
    return np.exp(-math.log(10000.0) * 2.0 * offset / width).astype(np.float32).reshape(1, HD)


def columns_to_rows(first, second):
    lane = lax.broadcasted_iota(jnp.int32, (ROWS, 128), 1)
    both = jnp.where(lane == 0, first, jnp.where(lane == 1, second, 0.0))
    padded = jnp.concatenate([both, jnp.zeros((STAT_LANES - ROWS, 128), F32)], axis=0)
    return padded.T[0:8]


def row_to_column(row):
    return jnp.broadcast_to(row, (128, STAT_LANES)).T[0:ROWS]


def pack_kernel(u_ref, key_ref, value_ref, *outs):
    for k in range(5):
        head = lax.rem(u_ref[0] + k, 4) if k < 4 else 4
        cols = pl.ds(pl.multiple_of(head * HD, HD), HD)
        for n, source in enumerate((key_ref, value_ref)):
            for s in range(B):
                outs[k][s, n] = source[s, :, cols]


def pack_stale(u, stale_keys, stale_values):
    return pl.pallas_call(
        pack_kernel,
        out_shape=[jax.ShapeDtypeStruct((B, 2, TOK, HD), BF16)] * 5,
        in_specs=[smem(), vmem(), vmem()],
        out_specs=[vmem()] * 5,
        compiler_params=params(VMEM_MIB),
        cost_estimate=pl.CostEstimate(
            flops=0, bytes_accessed=8 * ROWS * WIDTH, transcendentals=0
        ),
        name="pack_stale",
    )(u, stale_keys, stale_values)


def tables_kernel(place_hbm, freq, rows, shift, scale, after, *refs):
    cond, cos, sin, mod, rows_out, places_s, place_ref, sem = refs
    copy = pltpu.make_async_copy(place_hbm, place_ref, sem.at[0])
    copy.start()
    copy.wait()
    for row in range(TOK):
        places_s[row : row + 1] = jnp.full((1, HD), place_ref[row], jnp.int32)
    place = places_s[...]
    frame_tok = TOK * N_PATCH // FRAMES
    frame = jnp.where(place >= frame_tok, 1, 0) + jnp.where(place >= 2 * frame_tok, 1, 0)
    within = place - frame * frame_tok
    grid_row = ((within.astype(F32) + 0.5) * (1.0 / GRID_W)).astype(jnp.int32)
    grid_col = within - grid_row * GRID_W
    lane = lax.broadcasted_iota(jnp.int32, (TOK, HD), 1)
    third = 2 * (HD // 6)
    frame_lanes = HD - 2 * third
    position = jnp.where(
        lane < frame_lanes, frame, jnp.where(lane < frame_lanes + third, grid_row, grid_col)
    )
    angles = position.astype(F32) * freq[...]
    cos[...] = jnp.cos(angles)
    sine = jnp.sin(angles)
    sin[...] = jnp.where(lane % 2 == 0, -sine, sine)
    flag = jnp.where((frame == 0) | (frame == FRAMES - 1), 1.0, 0.0)
    cond[0:TOK] = flag
    cond[TOK:ROWS] = flag
    mod[0:2] = 1.0 + scale[...]
    mod[2:4] = shift[...]
    rows_out[...] = rows[...]


def tables(token_place, rows, shift, scale, after):
    table = jax.ShapeDtypeStruct((TOK, HD), F32)
    return pl.pallas_call(
        tables_kernel,
        out_shape=[
            jax.ShapeDtypeStruct((ROWS, HD), F32),
            table,
            table,
            jax.ShapeDtypeStruct((4, D), F32),
            jax.ShapeDtypeStruct((ROWS, CHUNK), BF16),
        ],
        in_specs=[pl.BlockSpec(memory_space=pltpu.HBM)]
        + [vmem()] * 4
        + [pl.BlockSpec(memory_space=pl.ANY)],
        out_specs=[vmem()] * 5,
        scratch_shapes=[
            pltpu.VMEM((TOK, HD), jnp.int32),
            pltpu.SMEM((TOK,), jnp.int32),
            pltpu.SemaphoreType.DMA((1,)),
        ],
        compiler_params=params(VMEM_MIB),
        cost_estimate=pl.CostEstimate(
            flops=100 * TOK * HD, bytes_accessed=1_000_000, transcendentals=0
        ),
        name="tables",
    )(token_place, jnp.asarray(frequencies()), rows, shift, scale, after)


def assemble_kernel(*refs):
    parts, out = refs[0:5], refs[5]
    for s in range(B):
        for n in range(2):
            for r in range(5):
                out[s, n, r * TOK : (r + 1) * TOK] = parts[r][s, n]


def assemble(parts):
    return pl.pallas_call(
        assemble_kernel,
        out_shape=jax.ShapeDtypeStruct((B, 2, PIECE, HD), BF16),
        in_specs=[vmem()] * 5,
        out_specs=vmem(),
        compiler_params=params(VMEM_MIB),
        cost_estimate=pl.CostEstimate(
            flops=0, bytes_accessed=16 * PIECE * HD, transcendentals=0
        ),
        name="assemble",
    )(*parts)


def lane_sum(parts):
    total = None
    for part in parts:
        for at in range(0, part.shape[1], HD):
            piece = part[:, at : at + HD]
            total = piece if total is None else total + piece
    return jnp.sum(total, axis=1, keepdims=True)


def modulate_kernel(t_ref, h0, h1, h2, h3, cond, mod, weight, out_ref, query_ref, *scratch):
    weight_s, modded_s, mean_s, rstd_s, sems = scratch
    chunks = (h0, h1, h2, h3)
    copies = []
    for c in range(TP):
        rows = pl.ds(pl.multiple_of(t_ref[c] * CHUNK, CHUNK), CHUNK)
        copies.append(pltpu.make_async_copy(weight.at[rows], weight_s.at[c], sems.at[c]))
        copies[c].start()
    for row in range(0, ROWS, GROUP):
        rows = slice(row, row + GROUP)
        lanes = [chunk[rows].astype(F32) for chunk in chunks]
        mean = lane_sum([(lanes[0] + lanes[1]) + (lanes[2] + lanes[3])]) * (1.0 / D)
        deviation = lane_sum([(part - mean) * (part - mean) for part in lanes])
        mean_s[rows] = jnp.broadcast_to(mean, (GROUP, HD))
        rstd_s[rows] = jnp.broadcast_to(lax.rsqrt(deviation * (1.0 / D) + EPS), (GROUP, HD))

    def product(c):
        copies[c].wait()
        part = jnp.dot(modded_s[c % 2], weight_s[c], preferred_element_type=F32)
        if c == 0:
            query_ref[...] = part
        else:
            query_ref[...] += part

    for c in range(TP):
        if c:
            product(c - 1)
        cols = pl.ds(pl.multiple_of(t_ref[c] * CHUNK, CHUNK), CHUNK)
        for row in range(0, ROWS, GROUP):
            rows = slice(row, row + GROUP)
            conditioned = cond[rows, 0:1] > 0.5
            gain = jnp.where(conditioned, mod[1:2, cols], mod[0:1, cols])
            bias = jnp.where(conditioned, mod[3:4, cols], mod[2:3, cols])
            normed = (chunks[c][rows].astype(F32) - mean_s[rows, 0:1]) * rstd_s[rows, 0:1]
            value = (normed * gain + bias).astype(BF16)
            modded_s[c % 2, rows] = value
            out_ref[rows, cols] = value
    product(TP - 1)


def modulate(blocks, chunks, cond, mod, weight):
    return pl.pallas_call(
        modulate_kernel,
        out_shape=[
            jax.ShapeDtypeStruct((ROWS, D), BF16),
            jax.ShapeDtypeStruct((ROWS, WIDTH), F32),
        ],
        in_specs=[smem()] + [vmem()] * 6 + [pl.BlockSpec(memory_space=pltpu.HBM)],
        out_specs=[vmem()] * 2,
        scratch_shapes=[
            pltpu.VMEM((TP, CHUNK, WIDTH), BF16),
            pltpu.VMEM((2, ROWS, CHUNK), BF16),
            pltpu.VMEM((ROWS, HD), F32),
            pltpu.VMEM((ROWS, HD), F32),
            pltpu.SemaphoreType.DMA((TP,)),
        ],
        compiler_params=params(MODULATE_MIB),
        cost_estimate=pl.CostEstimate(flops=1000, bytes_accessed=30_000_000, transcendentals=0),
        name="modulate",
    )(blocks, *chunks, cond, mod, weight)


def squares_kernel(q_ref, k_ref, out_ref):
    query, key = q_ref[...], k_ref[...]
    out_ref[...] = columns_to_rows(
        jnp.sum(query * query, axis=1, keepdims=True),
        jnp.sum(key * key, axis=1, keepdims=True),
    )


def sum_squares(query, key):
    return pl.pallas_call(
        squares_kernel,
        out_shape=jax.ShapeDtypeStruct((8, STAT_LANES), F32),
        in_specs=[vmem()] * 2,
        out_specs=vmem(),
        compiler_params=params(VMEM_MIB),
        cost_estimate=pl.CostEstimate(
            flops=4 * ROWS * WIDTH, bytes_accessed=8 * ROWS * WIDTH, transcendentals=0
        ),
        name="sum_squares",
    )(query, key)


def rope_kernel(u_ref, q_ref, k_ref, s0, s1, s2, s3, qg, kg, cos, sin, k_all, *refs):
    sends, q_rot = refs[0:4], refs[4]
    total = s0[...] + s1[...] + s2[...] + s3[...]
    inverse = lax.rsqrt(total * (1.0 / (HEADS * HD)) + EPS)
    even = lax.broadcasted_iota(jnp.int32, (ROWS, HD), 1) % 2 == 0
    cos_rows = jnp.concatenate([cos[...], cos[...]], axis=0)
    sin_rows = jnp.concatenate([sin[...], sin[...]], axis=0)

    def rotate(ref, column, gain, cols):
        part = ref[:, cols] * column * gain[cols].reshape(1, HD)
        swap = jnp.where(even, pltpu.roll(part, HD - 1, 1), pltpu.roll(part, 1, 1))
        return (part * cos_rows + swap * sin_rows).astype(BF16)

    q_column = row_to_column(inverse[0:1])
    k_column = row_to_column(inverse[1:2])
    for head in range(LOCAL_HEADS):
        cols = slice(head * HD, (head + 1) * HD)
        query = rotate(q_ref, q_column, qg, cols)
        for s in range(B):
            q_rot[head, s] = query[s * TOK : (s + 1) * TOK]
        k_all[:, cols] = rotate(k_ref, k_column, kg, cols)
    for k in range(4):
        for s in range(B):
            sends[k][s, 0] = q_rot[lax.rem(u_ref[0] + k, 4), s]
            sends[k][s, 1] = q_rot[4, s]


def norm_rope(u, query, key, squares, q_gain, k_gain, cos, sin):
    send = jax.ShapeDtypeStruct((B, 2, TOK, HD), BF16)
    flat = jax.ShapeDtypeStruct((ROWS, WIDTH), BF16)
    return pl.pallas_call(
        rope_kernel,
        out_shape=[flat] + [send] * 4,
        in_specs=[smem()] + [vmem()] * 10,
        out_specs=[vmem()] * 5,
        scratch_shapes=[pltpu.VMEM((LOCAL_HEADS, B, TOK, HD), BF16)],
        compiler_params=params(VMEM_MIB),
        cost_estimate=pl.CostEstimate(flops=1000, bytes_accessed=1000, transcendentals=0),
        name="norm_rope",
    )(u, query, key, *squares, q_gain, k_gain, cos, sin)


def scores_of(query, keys):
    return lax.dot_general(query, keys, (((1,), (1,)), ((), ())), preferred_element_type=F32)


def to_rows(blocks):
    lane = lax.broadcasted_iota(jnp.int32, (HD, HD), 1)
    table = jnp.zeros((HD, HD), F32)
    empty = jnp.zeros((2 * HD - TOK, HD), F32)
    for n, block in enumerate(blocks):
        rest = jnp.concatenate([block[HD:TOK], empty], axis=0)
        table = jnp.where(lane == 2 * n, block[0:HD], table)
        table = jnp.where(lane == 2 * n + 1, rest, table)
    return table.T


FRESH_ROWS = 24


def fresh_kernel(u_ref, k_ref, v_ref, *refs):
    queries, (out_ref, rows_ref) = refs[0:4], refs[4:6]
    lses = []
    for s in range(B):
        rows = slice(s * TOK, (s + 1) * TOK)
        for k in range(LOCAL_HEADS):
            head = lax.rem(u_ref[0] + k, 4) if k < 4 else 4
            cols = pl.ds(pl.multiple_of(head * HD, HD), HD)
            query = queries[k][s, 0] if k < 4 else queries[0][s, 1]
            scores = scores_of(query, k_ref[rows, cols])
            top = jnp.max(scores, axis=1, keepdims=True)
            probs = jnp.exp2((scores - top) * SCORE_SCALE)
            total = jnp.sum(probs, axis=1, keepdims=True)
            out = jnp.dot(probs.astype(BF16), v_ref[rows, cols], preferred_element_type=F32)
            out_ref[s, k] = out / total
            lses.append(jnp.broadcast_to(top * SCORE_SCALE + jnp.log2(total), (TOK, HD)))
    rows_ref[...] = to_rows(lses)[0:FRESH_ROWS]


def fresh_attention(u, key, value, queries):
    return pl.pallas_call(
        fresh_kernel,
        out_shape=[
            jax.ShapeDtypeStruct((B, LOCAL_HEADS, TOK, HD), F32),
            jax.ShapeDtypeStruct((FRESH_ROWS, HD), F32),
        ],
        in_specs=[smem()] + [vmem()] * 6,
        out_specs=[vmem()] * 2,
        compiler_params=params(VMEM_MIB),
        cost_estimate=pl.CostEstimate(flops=1000, bytes_accessed=1000, transcendentals=0),
        name="fresh_attention",
    )(u, key, value, *queries)


TILE = 2 * TOK
PER_PIECE = 4 * TOK
SPLIT = 768


def stale_kernel(far, count, *refs):
    queries = refs[0:4]
    pieces, rest = refs[4 : 4 + count], refs[4 + count :]
    keys_main, keys_last = count * PER_PIECE, count * TOK
    if far:
        near_out, near_lse = rest[0:2]
        msgs = rest[3:7]
    else:
        out_ref, lse_ref = rest[0:2]
    lse_s, acc_s, k_main, v_main, k_last, v_last, scores_s, probs_s = rest[-8:]

    jobs = [(s, e, tile) for s in range(B) for e in range(2) for tile in range(2)]

    def size(i):
        return keys_last if jobs[i][1] else keys_main

    def score_steps(i):
        s, e, tile = jobs[i]
        keys = k_last if e else k_main
        out = scores_s.at[i % 2]

        def arrive():
            v_main[s, :, HD:] = jnp.ones((keys_main, HD), BF16)
            v_last[s, :, HD:] = jnp.ones((keys_last, HD), BF16)
            for n, piece in enumerate(pieces):
                main = slice(n * PER_PIECE, (n + 1) * PER_PIECE)
                last = slice(n * TOK, (n + 1) * TOK)
                k_main[s, main] = piece[s, 0, 0:PER_PIECE]
                k_last[s, last] = piece[s, 0, PER_PIECE:PIECE]
                v_main[s, main, 0:HD] = piece[s, 1, 0:PER_PIECE]
                v_last[s, last, 0:HD] = piece[s, 1, PER_PIECE:PIECE]

        def step(at, end):
            query = jnp.concatenate([queries[2 * tile][s, e], queries[2 * tile + 1][s, e]], axis=0)
            out[:, at:end] = scores_of(query, keys[s, at:end])

        def hide():
            for n in range(2):
                r = 2 * tile + n
                rows = slice(n * TOK, (n + 1) * TOK)
                if e and r:
                    continue
                out[rows, r * TOK : (r + 1) * TOK] = jnp.full((TOK, TOK), MASKED, F32)

        steps = [] if i % 4 else [arrive]
        for at in range(0, size(i), SPLIT):
            steps.append(functools.partial(step, at, min(at + SPLIT, size(i))))
        return steps if far else steps + [hide]

    def softmax_steps(i, tops):
        def step(row):
            rows = slice(row, row + GROUP)
            part = scores_s[i % 2, rows, 0 : size(i)]
            top = jnp.max(part, axis=1, keepdims=True)
            probs = jnp.exp2((part - top) * SCORE_SCALE)
            tops.append(top)
            probs_s[i % 2, rows, 0 : size(i)] = probs.astype(BF16)

        return [functools.partial(step, row) for row in range(0, TILE, GROUP)]

    def product_steps(i, tops):
        s, e, tile = jobs[i]
        values = v_last if e else v_main

        def step(at, end):
            part = jnp.dot(
                probs_s[i % 2, :, at:end], values[s, at:end], preferred_element_type=F32
            )
            acc_s[...] = part if at == 0 else acc_s[...] + part

        def finish():
            top = jnp.concatenate(tops, axis=0)
            total = acc_s[:, HD:]
            out = acc_s[:, 0:HD] / total
            lse = top * SCORE_SCALE + jnp.log2(total)
            for n in range(2):
                r = 2 * tile + n
                half = slice(n * TOK, (n + 1) * TOK)
                if not far:
                    out_ref[s, r, e] = out[half]
                    lse_ref[s, r, e] = lse[half]
                    continue
                lse_near = near_lse[s, r, e]
                high = jnp.maximum(lse[half], lse_near)
                weight, weight_near = jnp.exp2(lse[half] - high), jnp.exp2(lse_near - high)
                both = weight + weight_near
                value = (out[half] * weight + near_out[s, r, e] * weight_near) / both
                lse_s[s, r, e] = high + jnp.log2(both)
                msgs[r][s, e * TOK : (e + 1) * TOK] = value.astype(BF16)

        steps = []
        for at in range(0, size(i), SPLIT):
            steps.append(functools.partial(step, at, min(at + SPLIT, size(i))))
        return steps + [finish]

    def weave(*lists):
        order = []
        for steps in lists:
            order += [((n + 0.5) / len(steps), step) for n, step in enumerate(steps)]
        for _, step in sorted(order, key=lambda entry: entry[0]):
            step()

    weave(score_steps(0))
    pending = None
    for i in range(len(jobs)):
        tops = []
        lists = [softmax_steps(i, tops)]
        if i + 1 < len(jobs):
            lists.append(score_steps(i + 1))
        if pending is not None:
            lists.append(pending)
        weave(*lists)
        pending = product_steps(i, tops)
    weave(pending)

    if far:
        order = [(r, s) for r in range(4) for s in range(B)]
        flat = to_rows([lse_s[s, r, e] for r, s in order for e in range(2)])
        for n, (r, s) in enumerate(order):
            part = flat[n * 4 : n * 4 + 4]
            high = part.astype(BF16).astype(F32)
            middle = (part - high).astype(BF16).astype(F32)
            low = part - high - middle
            stack = jnp.concatenate([high, middle, low, jnp.zeros((4, HD), F32)], axis=0)
            msgs[r][s, 2 * TOK : MSG_ROWS] = stack.astype(BF16)


def stale_attention(queries, pieces, near=None, after=None):
    far = near is not None
    args = [*queries, *pieces]
    count = len(pieces)
    keys_main, keys_last = count * PER_PIECE, count * TOK
    in_specs = [vmem()] * (4 + count)
    if far:
        args += [*near, after]
        in_specs += [vmem(), vmem(), pl.BlockSpec(memory_space=pl.ANY)]
        out_shape = [jax.ShapeDtypeStruct((B, MSG_ROWS, HD), BF16)] * 4
    else:
        out_shape = [jax.ShapeDtypeStruct((B, 4, 2, TOK, HD), F32)] * 2
    return pl.pallas_call(
        functools.partial(stale_kernel, far, count),
        out_shape=out_shape,
        in_specs=in_specs,
        out_specs=[vmem()] * len(out_shape),
        scratch_shapes=[
            pltpu.VMEM((B, 4, 2, TOK, HD), F32),
            pltpu.VMEM((TILE, 2 * HD), F32),
            pltpu.VMEM((B, keys_main, HD), BF16),
            pltpu.VMEM((B, keys_main, 2 * HD), BF16),
            pltpu.VMEM((B, keys_last, HD), BF16),
            pltpu.VMEM((B, keys_last, 2 * HD), BF16),
            pltpu.VMEM((2, TILE, keys_main), F32),
            pltpu.VMEM((2, TILE, keys_main), BF16),
        ],
        compiler_params=params(ATTENTION_MIB),
        cost_estimate=pl.CostEstimate(flops=1000, bytes_accessed=1000, transcendentals=0),
        name="far_attention" if far else "near_attention",
    )(*args)


def merge_kernel(u_ref, fresh_out, fresh_rows, *refs):
    msgs, out_ref = refs[0:4], refs[4]
    lses = {}
    for k in range(4):
        for s in range(B):
            stack = msgs[k][s, 2 * TOK : MSG_ROWS].astype(F32)
            lses[s, k] = stack[0:4] + stack[4:8] + stack[8:12]
    weights, jobs = [], []
    for s in range(B):
        for k in range(LOCAL_HEADS):
            at = (s * LOCAL_HEADS + k) * 2
            parts = [(None, fresh_rows[at : at + 2])]
            if k < 4:
                parts.append((k, lses[s, k][0:2]))
            else:
                parts += [(n, lses[s, n][2:4]) for n in range(4)]
            top = parts[0][1]
            for _, lse in parts[1:]:
                top = jnp.maximum(top, lse)
            raw = [jnp.exp2(lse - top) for _, lse in parts]
            total = sum(raw[1:], raw[0])
            jobs.append((s, k, [(source, len(weights) + n) for n, (source, _) in enumerate(parts)]))
            weights += [one / total for one in raw]
    filler = jnp.zeros((HD - 2 * len(weights), HD), F32)
    table = jnp.concatenate(weights + [filler], axis=0).T
    for s, k, parts in jobs:
        head = lax.rem(u_ref[0] + k, 4) if k < 4 else 4
        out = [None, None]
        for source, n in parts:
            for half, rows in enumerate((slice(0, HD), slice(HD, TOK))):
                if source is None:
                    value = fresh_out[s, k, rows]
                else:
                    at = 0 if k < 4 else TOK
                    value = msgs[source][s, at + rows.start : at + rows.stop].astype(F32)
                column = table[0 : rows.stop - rows.start, 2 * n + half : 2 * n + half + 1]
                term = value * column
                out[half] = term if out[half] is None else out[half] + term
        cols = pl.ds(pl.multiple_of(head * HD, HD), HD)
        out_ref[s, :, cols] = jnp.concatenate(out, axis=0).astype(BF16)


def merge(u, fresh_out, fresh_rows, msgs):
    return pl.pallas_call(
        merge_kernel,
        out_shape=jax.ShapeDtypeStruct((B, TOK, WIDTH), BF16),
        in_specs=[smem()] + [vmem()] * 6,
        out_specs=vmem(),
        compiler_params=params(VMEM_MIB),
        cost_estimate=pl.CostEstimate(
            flops=10 * ROWS * WIDTH, bytes_accessed=14 * ROWS * WIDTH, transcendentals=0
        ),
        name="merge",
    )(u, fresh_out, fresh_rows, *msgs)


def shards(
    hidden,
    mod_shift,
    mod_scale,
    w_query,
    w_key,
    w_value,
    q_gain,
    k_gain,
    token_place,
    stale_keys,
    stale_values,
):
    patch = lax.axis_index("patch")
    tp = lax.axis_index("tp")
    y = patch // (NX * NZ)
    x = (patch // NZ) % NX
    u = jnp.where(tp % 2 == 0, y, x).astype(jnp.int32).reshape(1)
    own_rows = hidden.reshape(ROWS, CHUNK)
    z_rows = swap_tp(own_rows, 1, 0)
    core_rows = swap_tp(own_rows, 0, 1)

    packed = pack_stale(u, stale_keys, stale_values)
    arrived = exchange_u(packed)
    near = assemble([*arrived, packed[4]])
    cond, cos, sin, mod, own_rows = tables(token_place, own_rows, mod_shift, mod_scale, near)
    near_one, near_three = swap_v(near, 1), swap_v(near, 3)
    far = swap_z_hi(near)

    z_rows, cond = lax.optimization_barrier((z_rows, cond))
    cross_rows = swap_tp(z_rows, 0, 1)
    blocks = jnp.stack([tp, tp ^ 1, tp ^ 2, tp ^ 3]).astype(jnp.int32)
    modded, query = modulate(blocks, [own_rows, core_rows, z_rows, cross_rows], cond, mod, w_query)
    key = jnp.dot(modded, w_key, preferred_element_type=F32)
    near_one, near_three, key = lax.optimization_barrier((near_one, near_three, key))
    near_two = swap_v(near_one, 3)
    fresh_values = jnp.dot(modded, w_value, preferred_element_type=F32).astype(BF16)
    own_sq = sum_squares(query, key)
    squares = [own_sq] + [swap_tp(own_sq, z, c) for z, c in ((1, 1), (1, 0), (0, 1))]
    far, fresh_values, *squares = lax.optimization_barrier((far, fresh_values, *squares))
    far_one, far_three = swap_v(far, 1), swap_v(far, 3)
    fresh_keys, *sends = norm_rope(u, query, key, squares, q_gain, k_gain, cos, sin)
    near_two, fresh_keys = lax.optimization_barrier((near_two, fresh_keys))
    far_two = swap_z_hi(near_two)
    queries = exchange_u(sends)
    fresh_out, fresh_rows = fresh_attention(u, fresh_keys, fresh_values, sends)

    partial = stale_attention(queries, [near, near_one, near_three, near_two, far])
    outs = stale_attention(
        queries, [far_one, far_three, far_two], near=partial, after=fresh_rows
    )
    returned = exchange_u(outs)
    attended = merge(u, fresh_out, fresh_rows, returned)
    return (
        attended,
        fresh_keys.reshape(B, TOK, WIDTH),
        fresh_values.reshape(B, TOK, WIDTH),
    )


def solution(mesh):
    in_specs = (
        P(None, "patch", "tp"),
        P(),
        P(),
        P(None, "tp"),
        P(None, "tp"),
        P(None, "tp"),
        P("tp"),
        P("tp"),
        P("patch"),
        P(None, "patch", "tp"),
        P(None, "patch", "tp"),
    )
    out_specs = (P(None, "patch", "tp"), P(None, "patch", "tp"), P(None, "patch", "tp"))
    return jax.shard_map(shards, mesh=mesh, in_specs=in_specs, out_specs=out_specs, check_vma=False)
```

```python
import functools
import math

import jax
import jax.numpy as jnp
import numpy as np
from jax import lax
from jax.experimental import pallas as pl
from jax.experimental.pallas import tpu as pltpu
from jax.sharding import PartitionSpec as P

D = 5120
HEADS = 20
HD = 128
FRAMES = 3
GRID_W = 48
EPS = 1e-06
MASKED = -1e30
NY, NX, NZ = 4, 4, 2
TP = 4
N_PATCH = NY * NX * NZ
TOK = 144
B = 2
ROWS = B * TOK
LOCAL_HEADS = 5
WIDTH = LOCAL_HEADS * HD
CHUNK = D // TP
STAT_LANES = 384
PIECE = 5 * TOK
MSG_ROWS = 2 * TOK + 16
SCORE_SCALE = math.log2(math.e) / math.sqrt(HD)
F32 = jnp.float32
BF16 = jnp.bfloat16
AXES = ("patch", "tp")
GROUP = 16
VMEM_MIB = 24
ATTENTION_MIB = 40
MODULATE_MIB = 42


def params(mib):
    return pltpu.CompilerParams(vmem_limit_bytes=mib * 1024 * 1024)


def vmem():
    return pl.BlockSpec(memory_space=pltpu.VMEM)


def smem():
    return pl.BlockSpec(memory_space=pltpu.SMEM)


def linear(u, v, z_hi, z_lo, core):
    y, x = (u, v) if core == 0 else (v, u)
    return ((y * NX + x) * NZ + z_hi) * TP + z_lo * 2 + core


def places():
    return [
        (u, v, h, l, c)
        for u in range(4)
        for v in range(4)
        for h in range(2)
        for l in range(2)
        for c in range(2)
    ]


def permute(value, move):
    return lax.ppermute(value, AXES, [(linear(*p), linear(*move(*p))) for p in places()])


def shift_u(value, k):
    return permute(value, lambda u, v, h, l, c: ((u + k) % 4, v, h, l, c))


def swap_v(value, mask):
    return permute(value, lambda u, v, h, l, c: (u, v ^ mask, h, l, c))


def exchange_u(values):
    came = {r: shift_u(values[4 - r], 4 - r) for r in (2, 1, 3)}
    return [values[0], came[1], came[2], came[3]]


def swap_z_hi(value):
    return permute(value, lambda u, v, h, l, c: (u, v, 1 - h, l, c))


def swap_tp(value, z, core):
    if core:
        return permute(value, lambda u, v, h, l, c: (v, u, h, l ^ z, 1 - c))
    return permute(value, lambda u, v, h, l, c: (u, v, h, l ^ z, c))


def frequencies():
    half_dim = HD // 2
    third_dim = half_dim // 3
    frame_pairs = half_dim - 2 * third_dim
    pair = np.arange(HD) // 2
    offset = np.where(
        pair < frame_pairs,
        pair,
        np.where(pair < frame_pairs + third_dim, pair - frame_pairs, pair - frame_pairs - third_dim),
    )
    width = np.where(pair < frame_pairs, 2 * frame_pairs, 2 * third_dim)
    return np.exp(-math.log(10000.0) * 2.0 * offset / width).astype(np.float32).reshape(1, HD)


def columns_to_rows(first, second):
    lane = lax.broadcasted_iota(jnp.int32, (ROWS, 128), 1)
    both = jnp.where(lane == 0, first, jnp.where(lane == 1, second, 0.0))
    padded = jnp.concatenate([both, jnp.zeros((STAT_LANES - ROWS, 128), F32)], axis=0)
    return padded.T[0:8]


def row_to_column(row):
    return jnp.broadcast_to(row, (128, STAT_LANES)).T[0:ROWS]


def pack_kernel(u_ref, key_ref, value_ref, *outs):
    for k in range(5):
        head = lax.rem(u_ref[0] + k, 4) if k < 4 else 4
        cols = pl.ds(pl.multiple_of(head * HD, HD), HD)
        for n, source in enumerate((key_ref, value_ref)):
            for s in range(B):
                outs[k][s, n] = source[s, :, cols]


def pack_stale(u, stale_keys, stale_values):
    return pl.pallas_call(
        pack_kernel,
        out_shape=[jax.ShapeDtypeStruct((B, 2, TOK, HD), BF16)] * 5,
        in_specs=[smem(), vmem(), vmem()],
        out_specs=[vmem()] * 5,
        compiler_params=params(VMEM_MIB),
        cost_estimate=pl.CostEstimate(
            flops=0, bytes_accessed=8 * ROWS * WIDTH, transcendentals=0
        ),
        name="pack_stale",
    )(u, stale_keys, stale_values)


def tables_kernel(place_hbm, freq, rows, shift, scale, after, *refs):
    cond, cos, sin, mod, rows_out, places_s, place_ref, sem = refs
    copy = pltpu.make_async_copy(place_hbm, place_ref, sem.at[0])
    copy.start()
    copy.wait()
    for row in range(TOK):
        places_s[row : row + 1] = jnp.full((1, HD), place_ref[row], jnp.int32)
    place = places_s[...]
    frame_tok = TOK * N_PATCH // FRAMES
    frame = jnp.where(place >= frame_tok, 1, 0) + jnp.where(place >= 2 * frame_tok, 1, 0)
    within = place - frame * frame_tok
    grid_row = ((within.astype(F32) + 0.5) * (1.0 / GRID_W)).astype(jnp.int32)
    grid_col = within - grid_row * GRID_W
    lane = lax.broadcasted_iota(jnp.int32, (TOK, HD), 1)
    third = 2 * (HD // 6)
    frame_lanes = HD - 2 * third
    position = jnp.where(
        lane < frame_lanes, frame, jnp.where(lane < frame_lanes + third, grid_row, grid_col)
    )
    angles = position.astype(F32) * freq[...]
    cos[...] = jnp.cos(angles)
    sine = jnp.sin(angles)
    sin[...] = jnp.where(lane % 2 == 0, -sine, sine)
    flag = jnp.where((frame == 0) | (frame == FRAMES - 1), 1.0, 0.0)
    cond[0:TOK] = flag
    cond[TOK:ROWS] = flag
    mod[0:2] = 1.0 + scale[...]
    mod[2:4] = shift[...]
    rows_out[...] = rows[...]


def tables(token_place, rows, shift, scale, after):
    table = jax.ShapeDtypeStruct((TOK, HD), F32)
    return pl.pallas_call(
        tables_kernel,
        out_shape=[
            jax.ShapeDtypeStruct((ROWS, HD), F32),
            table,
            table,
            jax.ShapeDtypeStruct((4, D), F32),
            jax.ShapeDtypeStruct((ROWS, CHUNK), BF16),
        ],
        in_specs=[pl.BlockSpec(memory_space=pltpu.HBM)]
        + [vmem()] * 4
        + [pl.BlockSpec(memory_space=pl.ANY)],
        out_specs=[vmem()] * 5,
        scratch_shapes=[
            pltpu.VMEM((TOK, HD), jnp.int32),
            pltpu.SMEM((TOK,), jnp.int32),
            pltpu.SemaphoreType.DMA((1,)),
        ],
        compiler_params=params(VMEM_MIB),
        cost_estimate=pl.CostEstimate(
            flops=100 * TOK * HD, bytes_accessed=1_000_000, transcendentals=0
        ),
        name="tables",
    )(token_place, jnp.asarray(frequencies()), rows, shift, scale, after)


def assemble_kernel(*refs):
    parts, out = refs[0:5], refs[5]
    for s in range(B):
        for n in range(2):
            for r in range(5):
                out[s, n, r * TOK : (r + 1) * TOK] = parts[r][s, n]


def assemble(parts):
    return pl.pallas_call(
        assemble_kernel,
        out_shape=jax.ShapeDtypeStruct((B, 2, PIECE, HD), BF16),
        in_specs=[vmem()] * 5,
        out_specs=vmem(),
        compiler_params=params(VMEM_MIB),
        cost_estimate=pl.CostEstimate(
            flops=0, bytes_accessed=16 * PIECE * HD, transcendentals=0
        ),
        name="assemble",
    )(*parts)


def lane_sum(parts):
    total = None
    for part in parts:
        for at in range(0, part.shape[1], HD):
            piece = part[:, at : at + HD]
            total = piece if total is None else total + piece
    return jnp.sum(total, axis=1, keepdims=True)


def modulate_kernel(t_ref, h0, h1, h2, h3, cond, mod, weight, out_ref, query_ref, *scratch):
    weight_s, modded_s, mean_s, rstd_s, sems = scratch
    chunks = (h0, h1, h2, h3)
    copies = []
    for c in range(TP):
        rows = pl.ds(pl.multiple_of(t_ref[c] * CHUNK, CHUNK), CHUNK)
        copies.append(pltpu.make_async_copy(weight.at[rows], weight_s.at[c], sems.at[c]))
        copies[c].start()
    for row in range(0, ROWS, GROUP):
        rows = slice(row, row + GROUP)
        lanes = [chunk[rows].astype(F32) for chunk in chunks]
        mean = lane_sum([(lanes[0] + lanes[1]) + (lanes[2] + lanes[3])]) * (1.0 / D)
        deviation = lane_sum([(part - mean) * (part - mean) for part in lanes])
        mean_s[rows] = jnp.broadcast_to(mean, (GROUP, HD))
        rstd_s[rows] = jnp.broadcast_to(lax.rsqrt(deviation * (1.0 / D) + EPS), (GROUP, HD))

    def product(c):
        copies[c].wait()
        part = jnp.dot(modded_s[c % 2], weight_s[c], preferred_element_type=F32)
        if c == 0:
            query_ref[...] = part
        else:
            query_ref[...] += part

    for c in range(TP):
        if c:
            product(c - 1)
        cols = pl.ds(pl.multiple_of(t_ref[c] * CHUNK, CHUNK), CHUNK)
        for row in range(0, ROWS, GROUP):
            rows = slice(row, row + GROUP)
            conditioned = cond[rows, 0:1] > 0.5
            gain = jnp.where(conditioned, mod[1:2, cols], mod[0:1, cols])
            bias = jnp.where(conditioned, mod[3:4, cols], mod[2:3, cols])
            normed = (chunks[c][rows].astype(F32) - mean_s[rows, 0:1]) * rstd_s[rows, 0:1]
            value = (normed * gain + bias).astype(BF16)
            modded_s[c % 2, rows] = value
            out_ref[rows, cols] = value
    product(TP - 1)


def modulate(blocks, chunks, cond, mod, weight):
    return pl.pallas_call(
        modulate_kernel,
        out_shape=[
            jax.ShapeDtypeStruct((ROWS, D), BF16),
            jax.ShapeDtypeStruct((ROWS, WIDTH), F32),
        ],
        in_specs=[smem()] + [vmem()] * 6 + [pl.BlockSpec(memory_space=pltpu.HBM)],
        out_specs=[vmem()] * 2,
        scratch_shapes=[
            pltpu.VMEM((TP, CHUNK, WIDTH), BF16),
            pltpu.VMEM((2, ROWS, CHUNK), BF16),
            pltpu.VMEM((ROWS, HD), F32),
            pltpu.VMEM((ROWS, HD), F32),
            pltpu.SemaphoreType.DMA((TP,)),
        ],
        compiler_params=params(MODULATE_MIB),
        cost_estimate=pl.CostEstimate(flops=1000, bytes_accessed=30_000_000, transcendentals=0),
        name="modulate",
    )(blocks, *chunks, cond, mod, weight)


def squares_kernel(q_ref, k_ref, out_ref):
    query, key = q_ref[...], k_ref[...]
    out_ref[...] = columns_to_rows(
        jnp.sum(query * query, axis=1, keepdims=True),
        jnp.sum(key * key, axis=1, keepdims=True),
    )


def sum_squares(query, key):
    return pl.pallas_call(
        squares_kernel,
        out_shape=jax.ShapeDtypeStruct((8, STAT_LANES), F32),
        in_specs=[vmem()] * 2,
        out_specs=vmem(),
        compiler_params=params(VMEM_MIB),
        cost_estimate=pl.CostEstimate(
            flops=4 * ROWS * WIDTH, bytes_accessed=8 * ROWS * WIDTH, transcendentals=0
        ),
        name="sum_squares",
    )(query, key)


def rope_kernel(u_ref, q_ref, k_ref, s0, s1, s2, s3, qg, kg, cos, sin, k_all, *refs):
    sends, q_rot = refs[0:4], refs[4]
    total = s0[...] + s1[...] + s2[...] + s3[...]
    inverse = lax.rsqrt(total * (1.0 / (HEADS * HD)) + EPS)
    even = lax.broadcasted_iota(jnp.int32, (ROWS, HD), 1) % 2 == 0
    cos_rows = jnp.concatenate([cos[...], cos[...]], axis=0)
    sin_rows = jnp.concatenate([sin[...], sin[...]], axis=0)

    def rotate(ref, column, gain, cols):
        part = ref[:, cols] * column * gain[cols].reshape(1, HD)
        swap = jnp.where(even, pltpu.roll(part, HD - 1, 1), pltpu.roll(part, 1, 1))
        return (part * cos_rows + swap * sin_rows).astype(BF16)

    q_column = row_to_column(inverse[0:1])
    k_column = row_to_column(inverse[1:2])
    for head in range(LOCAL_HEADS):
        cols = slice(head * HD, (head + 1) * HD)
        query = rotate(q_ref, q_column, qg, cols)
        for s in range(B):
            q_rot[head, s] = query[s * TOK : (s + 1) * TOK]
        k_all[:, cols] = rotate(k_ref, k_column, kg, cols)
    for k in range(4):
        for s in range(B):
            sends[k][s, 0] = q_rot[lax.rem(u_ref[0] + k, 4), s]
            sends[k][s, 1] = q_rot[4, s]


def norm_rope(u, query, key, squares, q_gain, k_gain, cos, sin):
    send = jax.ShapeDtypeStruct((B, 2, TOK, HD), BF16)
    flat = jax.ShapeDtypeStruct((ROWS, WIDTH), BF16)
    return pl.pallas_call(
        rope_kernel,
        out_shape=[flat] + [send] * 4,
        in_specs=[smem()] + [vmem()] * 10,
        out_specs=[vmem()] * 5,
        scratch_shapes=[pltpu.VMEM((LOCAL_HEADS, B, TOK, HD), BF16)],
        compiler_params=params(VMEM_MIB),
        cost_estimate=pl.CostEstimate(flops=1000, bytes_accessed=1000, transcendentals=0),
        name="norm_rope",
    )(u, query, key, *squares, q_gain, k_gain, cos, sin)


def scores_of(query, keys):
    return lax.dot_general(query, keys, (((1,), (1,)), ((), ())), preferred_element_type=F32)


def to_rows(blocks):
    lane = lax.broadcasted_iota(jnp.int32, (HD, HD), 1)
    table = jnp.zeros((HD, HD), F32)
    empty = jnp.zeros((2 * HD - TOK, HD), F32)
    for n, block in enumerate(blocks):
        rest = jnp.concatenate([block[HD:TOK], empty], axis=0)
        table = jnp.where(lane == 2 * n, block[0:HD], table)
        table = jnp.where(lane == 2 * n + 1, rest, table)
    return table.T


FRESH_ROWS = 24


def fresh_kernel(u_ref, k_ref, v_ref, *refs):
    queries, (out_ref, rows_ref) = refs[0:4], refs[4:6]
    lses = []
    for s in range(B):
        rows = slice(s * TOK, (s + 1) * TOK)
        for k in range(LOCAL_HEADS):
            head = lax.rem(u_ref[0] + k, 4) if k < 4 else 4
            cols = pl.ds(pl.multiple_of(head * HD, HD), HD)
            query = queries[k][s, 0] if k < 4 else queries[0][s, 1]
            scores = scores_of(query, k_ref[rows, cols])
            top = jnp.max(scores, axis=1, keepdims=True)
            probs = jnp.exp2((scores - top) * SCORE_SCALE)
            total = jnp.sum(probs, axis=1, keepdims=True)
            out = jnp.dot(probs.astype(BF16), v_ref[rows, cols], preferred_element_type=F32)
            out_ref[s, k] = out / total
            lses.append(jnp.broadcast_to(top * SCORE_SCALE + jnp.log2(total), (TOK, HD)))
    rows_ref[...] = to_rows(lses)[0:FRESH_ROWS]


def fresh_attention(u, key, value, queries):
    return pl.pallas_call(
        fresh_kernel,
        out_shape=[
            jax.ShapeDtypeStruct((B, LOCAL_HEADS, TOK, HD), F32),
            jax.ShapeDtypeStruct((FRESH_ROWS, HD), F32),
        ],
        in_specs=[smem()] + [vmem()] * 6,
        out_specs=[vmem()] * 2,
        compiler_params=params(VMEM_MIB),
        cost_estimate=pl.CostEstimate(flops=1000, bytes_accessed=1000, transcendentals=0),
        name="fresh_attention",
    )(u, key, value, *queries)


TILE = 2 * TOK
PER_PIECE = 4 * TOK
SPLIT = 768


def stale_kernel(far, count, *refs):
    queries = refs[0:4]
    pieces, rest = refs[4 : 4 + count], refs[4 + count :]
    keys_main, keys_last = count * PER_PIECE, count * TOK
    if far:
        near_out, near_lse = rest[0:2]
        msgs = rest[3:7]
    else:
        out_ref, lse_ref = rest[0:2]
    lse_s, acc_s, k_main, v_main, k_last, v_last, scores_s, probs_s = rest[-8:]

    jobs = [(s, e, tile) for s in range(B) for e in range(2) for tile in range(2)]

    def size(i):
        return keys_last if jobs[i][1] else keys_main

    def score_steps(i):
        s, e, tile = jobs[i]
        keys = k_last if e else k_main
        out = scores_s.at[i % 2]

        def arrive():
            v_main[s, :, HD:] = jnp.ones((keys_main, HD), BF16)
            v_last[s, :, HD:] = jnp.ones((keys_last, HD), BF16)
            for n, piece in enumerate(pieces):
                main = slice(n * PER_PIECE, (n + 1) * PER_PIECE)
                last = slice(n * TOK, (n + 1) * TOK)
                k_main[s, main] = piece[s, 0, 0:PER_PIECE]
                k_last[s, last] = piece[s, 0, PER_PIECE:PIECE]
                v_main[s, main, 0:HD] = piece[s, 1, 0:PER_PIECE]
                v_last[s, last, 0:HD] = piece[s, 1, PER_PIECE:PIECE]

        def step(at, end):
            query = jnp.concatenate([queries[2 * tile][s, e], queries[2 * tile + 1][s, e]], axis=0)
            out[:, at:end] = scores_of(query, keys[s, at:end])

        def hide():
            for n in range(2):
                r = 2 * tile + n
                rows = slice(n * TOK, (n + 1) * TOK)
                if e and r:
                    continue
                out[rows, r * TOK : (r + 1) * TOK] = jnp.full((TOK, TOK), MASKED, F32)

        steps = [] if i % 4 else [arrive]
        for at in range(0, size(i), SPLIT):
            steps.append(functools.partial(step, at, min(at + SPLIT, size(i))))
        return steps if far else steps + [hide]

    def softmax_steps(i, tops):
        def step(row):
            rows = slice(row, row + GROUP)
            part = scores_s[i % 2, rows, 0 : size(i)]
            top = jnp.max(part, axis=1, keepdims=True)
            probs = jnp.exp2((part - top) * SCORE_SCALE)
            tops.append(top)
            probs_s[i % 2, rows, 0 : size(i)] = probs.astype(BF16)

        return [functools.partial(step, row) for row in range(0, TILE, GROUP)]

    def product_steps(i, tops):
        s, e, tile = jobs[i]
        values = v_last if e else v_main

        def step(at, end):
            part = jnp.dot(
                probs_s[i % 2, :, at:end], values[s, at:end], preferred_element_type=F32
            )
            acc_s[...] = part if at == 0 else acc_s[...] + part

        def finish():
            top = jnp.concatenate(tops, axis=0)
            total = acc_s[:, HD:]
            out = acc_s[:, 0:HD] / total
            lse = top * SCORE_SCALE + jnp.log2(total)
            for n in range(2):
                r = 2 * tile + n
                half = slice(n * TOK, (n + 1) * TOK)
                if not far:
                    out_ref[s, r, e] = out[half]
                    lse_ref[s, r, e] = lse[half]
                    continue
                lse_near = near_lse[s, r, e]
                high = jnp.maximum(lse[half], lse_near)
                weight, weight_near = jnp.exp2(lse[half] - high), jnp.exp2(lse_near - high)
                both = weight + weight_near
                value = (out[half] * weight + near_out[s, r, e] * weight_near) / both
                lse_s[s, r, e] = high + jnp.log2(both)
                msgs[r][s, e * TOK : (e + 1) * TOK] = value.astype(BF16)

        steps = []
        for at in range(0, size(i), SPLIT):
            steps.append(functools.partial(step, at, min(at + SPLIT, size(i))))
        return steps + [finish]

    def weave(*lists):
        order = []
        for steps in lists:
            order += [((n + 0.5) / len(steps), step) for n, step in enumerate(steps)]
        for _, step in sorted(order, key=lambda entry: entry[0]):
            step()

    weave(score_steps(0))
    pending = None
    for i in range(len(jobs)):
        tops = []
        lists = [softmax_steps(i, tops)]
        if i + 1 < len(jobs):
            lists.append(score_steps(i + 1))
        if pending is not None:
            lists.append(pending)
        weave(*lists)
        pending = product_steps(i, tops)
    weave(pending)

    if far:
        order = [(r, s) for r in range(4) for s in range(B)]
        flat = to_rows([lse_s[s, r, e] for r, s in order for e in range(2)])
        for n, (r, s) in enumerate(order):
            part = flat[n * 4 : n * 4 + 4]
            high = part.astype(BF16).astype(F32)
            middle = (part - high).astype(BF16).astype(F32)
            low = part - high - middle
            stack = jnp.concatenate([high, middle, low, jnp.zeros((4, HD), F32)], axis=0)
            msgs[r][s, 2 * TOK : MSG_ROWS] = stack.astype(BF16)


def stale_attention(queries, pieces, near=None, after=None):
    far = near is not None
    args = [*queries, *pieces]
    count = len(pieces)
    keys_main, keys_last = count * PER_PIECE, count * TOK
    in_specs = [vmem()] * (4 + count)
    if far:
        args += [*near, after]
        in_specs += [vmem(), vmem(), pl.BlockSpec(memory_space=pl.ANY)]
        out_shape = [jax.ShapeDtypeStruct((B, MSG_ROWS, HD), BF16)] * 4
    else:
        out_shape = [jax.ShapeDtypeStruct((B, 4, 2, TOK, HD), F32)] * 2
    return pl.pallas_call(
        functools.partial(stale_kernel, far, count),
        out_shape=out_shape,
        in_specs=in_specs,
        out_specs=[vmem()] * len(out_shape),
        scratch_shapes=[
            pltpu.VMEM((B, 4, 2, TOK, HD), F32),
            pltpu.VMEM((TILE, 2 * HD), F32),
            pltpu.VMEM((B, keys_main, HD), BF16),
            pltpu.VMEM((B, keys_main, 2 * HD), BF16),
            pltpu.VMEM((B, keys_last, HD), BF16),
            pltpu.VMEM((B, keys_last, 2 * HD), BF16),
            pltpu.VMEM((2, TILE, keys_main), F32),
            pltpu.VMEM((2, TILE, keys_main), BF16),
        ],
        compiler_params=params(ATTENTION_MIB),
        cost_estimate=pl.CostEstimate(flops=1000, bytes_accessed=1000, transcendentals=0),
        name="far_attention" if far else "near_attention",
    )(*args)


def merge_kernel(u_ref, fresh_out, fresh_rows, *refs):
    msgs, out_ref = refs[0:4], refs[4]
    lses = {}
    for k in range(4):
        for s in range(B):
            stack = msgs[k][s, 2 * TOK : MSG_ROWS].astype(F32)
            lses[s, k] = stack[0:4] + stack[4:8] + stack[8:12]
    weights, jobs = [], []
    for s in range(B):
        for k in range(LOCAL_HEADS):
            at = (s * LOCAL_HEADS + k) * 2
            parts = [(None, fresh_rows[at : at + 2])]
            if k < 4:
                parts.append((k, lses[s, k][0:2]))
            else:
                parts += [(n, lses[s, n][2:4]) for n in range(4)]
            top = parts[0][1]
            for _, lse in parts[1:]:
                top = jnp.maximum(top, lse)
            raw = [jnp.exp2(lse - top) for _, lse in parts]
            total = sum(raw[1:], raw[0])
            jobs.append((s, k, [(source, len(weights) + n) for n, (source, _) in enumerate(parts)]))
            weights += [one / total for one in raw]
    filler = jnp.zeros((HD - 2 * len(weights), HD), F32)
    table = jnp.concatenate(weights + [filler], axis=0).T
    for s, k, parts in jobs:
        head = lax.rem(u_ref[0] + k, 4) if k < 4 else 4
        out = [None, None]
        for source, n in parts:
            for half, rows in enumerate((slice(0, HD), slice(HD, TOK))):
                if source is None:
                    value = fresh_out[s, k, rows]
                else:
                    at = 0 if k < 4 else TOK
                    value = msgs[source][s, at + rows.start : at + rows.stop].astype(F32)
                column = table[0 : rows.stop - rows.start, 2 * n + half : 2 * n + half + 1]
                term = value * column
                out[half] = term if out[half] is None else out[half] + term
        cols = pl.ds(pl.multiple_of(head * HD, HD), HD)
        out_ref[s, :, cols] = jnp.concatenate(out, axis=0).astype(BF16)


def merge(u, fresh_out, fresh_rows, msgs):
    return pl.pallas_call(
        merge_kernel,
        out_shape=jax.ShapeDtypeStruct((B, TOK, WIDTH), BF16),
        in_specs=[smem()] + [vmem()] * 6,
        out_specs=vmem(),
        compiler_params=params(VMEM_MIB),
        cost_estimate=pl.CostEstimate(
            flops=10 * ROWS * WIDTH, bytes_accessed=14 * ROWS * WIDTH, transcendentals=0
        ),
        name="merge",
    )(u, fresh_out, fresh_rows, *msgs)


def shards(
    hidden,
    mod_shift,
    mod_scale,
    w_query,
    w_key,
    w_value,
    q_gain,
    k_gain,
    token_place,
    stale_keys,
    stale_values,
):
    patch = lax.axis_index("patch")
    tp = lax.axis_index("tp")
    y = patch // (NX * NZ)
    x = (patch // NZ) % NX
    u = jnp.where(tp % 2 == 0, y, x).astype(jnp.int32).reshape(1)
    own_rows = hidden.reshape(ROWS, CHUNK)
    z_rows = swap_tp(own_rows, 1, 0)
    core_rows = swap_tp(own_rows, 0, 1)

    packed = pack_stale(u, stale_keys, stale_values)
    arrived = exchange_u(packed)
    near = assemble([*arrived, packed[4]])
    cond, cos, sin, mod, own_rows = tables(token_place, own_rows, mod_shift, mod_scale, near)
    near_one, near_three = swap_v(near, 1), swap_v(near, 3)
    far = swap_z_hi(near)

    z_rows, cond = lax.optimization_barrier((z_rows, cond))
    cross_rows = swap_tp(z_rows, 0, 1)
    blocks = jnp.stack([tp, tp ^ 1, tp ^ 2, tp ^ 3]).astype(jnp.int32)
    modded, query = modulate(blocks, [own_rows, core_rows, z_rows, cross_rows], cond, mod, w_query)
    key = jnp.dot(modded, w_key, preferred_element_type=F32)
    fresh_values = jnp.dot(modded, w_value, preferred_element_type=F32).astype(BF16)
    own_sq = sum_squares(query, key)
    near_one, near_three, own_sq = lax.optimization_barrier((near_one, near_three, own_sq))
    near_two = swap_v(near_one, 3)
    squares = [own_sq] + [swap_tp(own_sq, z, c) for z, c in ((1, 1), (1, 0), (0, 1))]
    fresh_values, *squares = lax.optimization_barrier((fresh_values, *squares))
    fresh_keys, *sends = norm_rope(u, query, key, squares, q_gain, k_gain, cos, sin)
    far, fresh_keys = lax.optimization_barrier((far, fresh_keys))
    far_one, far_three = swap_v(far, 1), swap_v(far, 3)
    queries = exchange_u(sends)
    fresh_out, fresh_rows = fresh_attention(u, fresh_keys, fresh_values, sends)

    far_one, near_two, *queries = lax.optimization_barrier((far_one, near_two, *queries))
    far_two = swap_v(far_one, 3)
    partial = stale_attention(queries, [near, near_one, near_three, near_two, far, far_one])
    outs = stale_attention(
        queries, [far_three, far_two], near=partial, after=fresh_rows
    )
    returned = exchange_u(outs)
    attended = merge(u, fresh_out, fresh_rows, returned)
    return (
        attended,
        fresh_keys.reshape(B, TOK, WIDTH),
        fresh_values.reshape(B, TOK, WIDTH),
    )


def solution(mesh):
    in_specs = (
        P(None, "patch", "tp"),
        P(),
        P(),
        P(None, "tp"),
        P(None, "tp"),
        P(None, "tp"),
        P("tp"),
        P("tp"),
        P("patch"),
        P(None, "patch", "tp"),
        P(None, "patch", "tp"),
    )
    out_specs = (P(None, "patch", "tp"), P(None, "patch", "tp"), P(None, "patch", "tp"))
    return jax.shard_map(shards, mesh=mesh, in_specs=in_specs, out_specs=out_specs, check_vma=False)
```

```python
import functools
import math

import jax
import jax.numpy as jnp
import numpy as np
from jax import lax
from jax.experimental import pallas as pl
from jax.experimental.pallas import tpu as pltpu
from jax.sharding import PartitionSpec as P

D = 5120
HEADS = 20
HD = 128
FRAMES = 3
GRID_W = 48
EPS = 1e-06
MASKED = -1e30
NY, NX, NZ = 4, 4, 2
TP = 4
N_PATCH = NY * NX * NZ
TOK = 144
B = 2
ROWS = B * TOK
LOCAL_HEADS = 5
WIDTH = LOCAL_HEADS * HD
CHUNK = D // TP
STAT_LANES = 384
PIECE = 5 * TOK
MSG_ROWS = 2 * TOK + 16
SCORE_SCALE = math.log2(math.e) / math.sqrt(HD)
F32 = jnp.float32
BF16 = jnp.bfloat16
AXES = ("patch", "tp")
GROUP = 16
VMEM_MIB = 24
ATTENTION_MIB = 34
MODULATE_MIB = 42


def params(mib):
    return pltpu.CompilerParams(vmem_limit_bytes=mib * 1024 * 1024)


def vmem():
    return pl.BlockSpec(memory_space=pltpu.VMEM)


def smem():
    return pl.BlockSpec(memory_space=pltpu.SMEM)


def linear(u, v, z_hi, z_lo, core):
    y, x = (u, v) if core == 0 else (v, u)
    return ((y * NX + x) * NZ + z_hi) * TP + z_lo * 2 + core


def places():
    return [
        (u, v, h, l, c)
        for u in range(4)
        for v in range(4)
        for h in range(2)
        for l in range(2)
        for c in range(2)
    ]


def permute(value, move):
    return lax.ppermute(value, AXES, [(linear(*p), linear(*move(*p))) for p in places()])


def shift_u(value, k):
    return permute(value, lambda u, v, h, l, c: ((u + k) % 4, v, h, l, c))


def swap_v(value, mask):
    return permute(value, lambda u, v, h, l, c: (u, v ^ mask, h, l, c))


def exchange_u(values):
    came = {r: shift_u(values[4 - r], 4 - r) for r in (2, 1, 3)}
    return [values[0], came[1], came[2], came[3]]


def swap_z_hi(value):
    return permute(value, lambda u, v, h, l, c: (u, v, 1 - h, l, c))


def swap_tp(value, z, core):
    if core:
        return permute(value, lambda u, v, h, l, c: (v, u, h, l ^ z, 1 - c))
    return permute(value, lambda u, v, h, l, c: (u, v, h, l ^ z, c))


def frequencies():
    half_dim = HD // 2
    third_dim = half_dim // 3
    frame_pairs = half_dim - 2 * third_dim
    pair = np.arange(HD) // 2
    offset = np.where(
        pair < frame_pairs,
        pair,
        np.where(pair < frame_pairs + third_dim, pair - frame_pairs, pair - frame_pairs - third_dim),
    )
    width = np.where(pair < frame_pairs, 2 * frame_pairs, 2 * third_dim)
    return np.exp(-math.log(10000.0) * 2.0 * offset / width).astype(np.float32).reshape(1, HD)


def columns_to_rows(first, second):
    lane = lax.broadcasted_iota(jnp.int32, (ROWS, 128), 1)
    both = jnp.where(lane == 0, first, jnp.where(lane == 1, second, 0.0))
    padded = jnp.concatenate([both, jnp.zeros((STAT_LANES - ROWS, 128), F32)], axis=0)
    return padded.T[0:8]


def row_to_column(row):
    return jnp.broadcast_to(row, (128, STAT_LANES)).T[0:ROWS]


def pack_kernel(u_ref, key_ref, value_ref, *outs):
    for k in range(5):
        head = lax.rem(u_ref[0] + k, 4) if k < 4 else 4
        cols = pl.ds(pl.multiple_of(head * HD, HD), HD)
        for n, source in enumerate((key_ref, value_ref)):
            for s in range(B):
                outs[k][s, n] = source[s, :, cols]


def pack_stale(u, stale_keys, stale_values):
    return pl.pallas_call(
        pack_kernel,
        out_shape=[jax.ShapeDtypeStruct((B, 2, TOK, HD), BF16)] * 5,
        in_specs=[smem(), vmem(), vmem()],
        out_specs=[vmem()] * 5,
        compiler_params=params(VMEM_MIB),
        cost_estimate=pl.CostEstimate(
            flops=0, bytes_accessed=8 * ROWS * WIDTH, transcendentals=0
        ),
        name="pack_stale",
    )(u, stale_keys, stale_values)


def tables_kernel(place_hbm, freq, rows, shift, scale, after, *refs):
    cond, cos, sin, mod, rows_out, places_s, place_ref, sem = refs
    copy = pltpu.make_async_copy(place_hbm, place_ref, sem.at[0])
    copy.start()
    copy.wait()
    for row in range(TOK):
        places_s[row : row + 1] = jnp.full((1, HD), place_ref[row], jnp.int32)
    place = places_s[...]
    frame_tok = TOK * N_PATCH // FRAMES
    frame = jnp.where(place >= frame_tok, 1, 0) + jnp.where(place >= 2 * frame_tok, 1, 0)
    within = place - frame * frame_tok
    grid_row = ((within.astype(F32) + 0.5) * (1.0 / GRID_W)).astype(jnp.int32)
    grid_col = within - grid_row * GRID_W
    lane = lax.broadcasted_iota(jnp.int32, (TOK, HD), 1)
    third = 2 * (HD // 6)
    frame_lanes = HD - 2 * third
    position = jnp.where(
        lane < frame_lanes, frame, jnp.where(lane < frame_lanes + third, grid_row, grid_col)
    )
    angles = position.astype(F32) * freq[...]
    cos[...] = jnp.cos(angles)
    sine = jnp.sin(angles)
    sin[...] = jnp.where(lane % 2 == 0, -sine, sine)
    flag = jnp.where((frame == 0) | (frame == FRAMES - 1), 1.0, 0.0)
    cond[0:TOK] = flag
    cond[TOK:ROWS] = flag
    mod[0:2] = 1.0 + scale[...]
    mod[2:4] = shift[...]
    rows_out[...] = rows[...]


def tables(token_place, rows, shift, scale, after):
    table = jax.ShapeDtypeStruct((TOK, HD), F32)
    return pl.pallas_call(
        tables_kernel,
        out_shape=[
            jax.ShapeDtypeStruct((ROWS, HD), F32),
            table,
            table,
            jax.ShapeDtypeStruct((4, D), F32),
            jax.ShapeDtypeStruct((ROWS, CHUNK), BF16),
        ],
        in_specs=[pl.BlockSpec(memory_space=pltpu.HBM)]
        + [vmem()] * 4
        + [pl.BlockSpec(memory_space=pl.ANY)],
        out_specs=[vmem()] * 5,
        scratch_shapes=[
            pltpu.VMEM((TOK, HD), jnp.int32),
            pltpu.SMEM((TOK,), jnp.int32),
            pltpu.SemaphoreType.DMA((1,)),
        ],
        compiler_params=params(VMEM_MIB),
        cost_estimate=pl.CostEstimate(
            flops=100 * TOK * HD, bytes_accessed=1_000_000, transcendentals=0
        ),
        name="tables",
    )(token_place, jnp.asarray(frequencies()), rows, shift, scale, after)


def assemble_kernel(*refs):
    parts, out = refs[0:5], refs[5]
    for s in range(B):
        for n in range(2):
            for r in range(5):
                out[s, n, r * TOK : (r + 1) * TOK] = parts[r][s, n]


def assemble(parts):
    return pl.pallas_call(
        assemble_kernel,
        out_shape=jax.ShapeDtypeStruct((B, 2, PIECE, HD), BF16),
        in_specs=[vmem()] * 5,
        out_specs=vmem(),
        compiler_params=params(VMEM_MIB),
        cost_estimate=pl.CostEstimate(
            flops=0, bytes_accessed=16 * PIECE * HD, transcendentals=0
        ),
        name="assemble",
    )(*parts)


def lane_sum(parts):
    total = None
    for part in parts:
        for at in range(0, part.shape[1], HD):
            piece = part[:, at : at + HD]
            total = piece if total is None else total + piece
    return jnp.sum(total, axis=1, keepdims=True)


def modulate_kernel(t_ref, h0, h1, h2, h3, cond, mod, weight, out_ref, query_ref, *scratch):
    weight_s, modded_s, mean_s, rstd_s, sems = scratch
    chunks = (h0, h1, h2, h3)
    copies = []
    for c in range(TP):
        rows = pl.ds(pl.multiple_of(t_ref[c] * CHUNK, CHUNK), CHUNK)
        copies.append(pltpu.make_async_copy(weight.at[rows], weight_s.at[c], sems.at[c]))
        copies[c].start()
    for row in range(0, ROWS, GROUP):
        rows = slice(row, row + GROUP)
        lanes = [chunk[rows].astype(F32) for chunk in chunks]
        mean = lane_sum([(lanes[0] + lanes[1]) + (lanes[2] + lanes[3])]) * (1.0 / D)
        deviation = lane_sum([(part - mean) * (part - mean) for part in lanes])
        mean_s[rows] = jnp.broadcast_to(mean, (GROUP, HD))
        rstd_s[rows] = jnp.broadcast_to(lax.rsqrt(deviation * (1.0 / D) + EPS), (GROUP, HD))

    def product(c):
        copies[c].wait()
        part = jnp.dot(modded_s[c % 2], weight_s[c], preferred_element_type=F32)
        if c == 0:
            query_ref[...] = part
        else:
            query_ref[...] += part

    for c in range(TP):
        if c:
            product(c - 1)
        cols = pl.ds(pl.multiple_of(t_ref[c] * CHUNK, CHUNK), CHUNK)
        for row in range(0, ROWS, GROUP):
            rows = slice(row, row + GROUP)
            conditioned = cond[rows, 0:1] > 0.5
            gain = jnp.where(conditioned, mod[1:2, cols], mod[0:1, cols])
            bias = jnp.where(conditioned, mod[3:4, cols], mod[2:3, cols])
            normed = (chunks[c][rows].astype(F32) - mean_s[rows, 0:1]) * rstd_s[rows, 0:1]
            value = (normed * gain + bias).astype(BF16)
            modded_s[c % 2, rows] = value
            out_ref[rows, cols] = value
    product(TP - 1)


def modulate(blocks, chunks, cond, mod, weight):
    return pl.pallas_call(
        modulate_kernel,
        out_shape=[
            jax.ShapeDtypeStruct((ROWS, D), BF16),
            jax.ShapeDtypeStruct((ROWS, WIDTH), F32),
        ],
        in_specs=[smem()] + [vmem()] * 6 + [pl.BlockSpec(memory_space=pltpu.HBM)],
        out_specs=[vmem()] * 2,
        scratch_shapes=[
            pltpu.VMEM((TP, CHUNK, WIDTH), BF16),
            pltpu.VMEM((2, ROWS, CHUNK), BF16),
            pltpu.VMEM((ROWS, HD), F32),
            pltpu.VMEM((ROWS, HD), F32),
            pltpu.SemaphoreType.DMA((TP,)),
        ],
        compiler_params=params(MODULATE_MIB),
        cost_estimate=pl.CostEstimate(flops=1000, bytes_accessed=30_000_000, transcendentals=0),
        name="modulate",
    )(blocks, *chunks, cond, mod, weight)


def squares_kernel(q_ref, k_ref, out_ref):
    query, key = q_ref[...], k_ref[...]
    out_ref[...] = columns_to_rows(
        jnp.sum(query * query, axis=1, keepdims=True),
        jnp.sum(key * key, axis=1, keepdims=True),
    )


def sum_squares(query, key):
    return pl.pallas_call(
        squares_kernel,
        out_shape=jax.ShapeDtypeStruct((8, STAT_LANES), F32),
        in_specs=[vmem()] * 2,
        out_specs=vmem(),
        compiler_params=params(VMEM_MIB),
        cost_estimate=pl.CostEstimate(
            flops=4 * ROWS * WIDTH, bytes_accessed=8 * ROWS * WIDTH, transcendentals=0
        ),
        name="sum_squares",
    )(query, key)


def rope_kernel(u_ref, q_ref, k_ref, s0, s1, s2, s3, qg, kg, cos, sin, k_all, *refs):
    sends, q_rot = refs[0:4], refs[4]
    total = s0[...] + s1[...] + s2[...] + s3[...]
    inverse = lax.rsqrt(total * (1.0 / (HEADS * HD)) + EPS)
    even = lax.broadcasted_iota(jnp.int32, (ROWS, HD), 1) % 2 == 0
    cos_rows = jnp.concatenate([cos[...], cos[...]], axis=0)
    sin_rows = jnp.concatenate([sin[...], sin[...]], axis=0)

    def rotate(ref, column, gain, cols):
        part = ref[:, cols] * column * gain[cols].reshape(1, HD)
        swap = jnp.where(even, pltpu.roll(part, HD - 1, 1), pltpu.roll(part, 1, 1))
        return (part * cos_rows + swap * sin_rows).astype(BF16)

    q_column = row_to_column(inverse[0:1])
    k_column = row_to_column(inverse[1:2])
    for head in range(LOCAL_HEADS):
        cols = slice(head * HD, (head + 1) * HD)
        query = rotate(q_ref, q_column, qg, cols)
        for s in range(B):
            q_rot[head, s] = query[s * TOK : (s + 1) * TOK]
        k_all[:, cols] = rotate(k_ref, k_column, kg, cols)
    for k in range(4):
        for s in range(B):
            sends[k][s, 0] = q_rot[lax.rem(u_ref[0] + k, 4), s]
            sends[k][s, 1] = q_rot[4, s]


def norm_rope(u, query, key, squares, q_gain, k_gain, cos, sin):
    send = jax.ShapeDtypeStruct((B, 2, TOK, HD), BF16)
    flat = jax.ShapeDtypeStruct((ROWS, WIDTH), BF16)
    return pl.pallas_call(
        rope_kernel,
        out_shape=[flat] + [send] * 4,
        in_specs=[smem()] + [vmem()] * 10,
        out_specs=[vmem()] * 5,
        scratch_shapes=[pltpu.VMEM((LOCAL_HEADS, B, TOK, HD), BF16)],
        compiler_params=params(VMEM_MIB),
        cost_estimate=pl.CostEstimate(flops=1000, bytes_accessed=1000, transcendentals=0),
        name="norm_rope",
    )(u, query, key, *squares, q_gain, k_gain, cos, sin)


def scores_of(query, keys):
    return lax.dot_general(query, keys, (((1,), (1,)), ((), ())), preferred_element_type=F32)


def to_rows(blocks):
    lane = lax.broadcasted_iota(jnp.int32, (HD, HD), 1)
    table = jnp.zeros((HD, HD), F32)
    empty = jnp.zeros((2 * HD - TOK, HD), F32)
    for n, block in enumerate(blocks):
        rest = jnp.concatenate([block[HD:TOK], empty], axis=0)
        table = jnp.where(lane == 2 * n, block[0:HD], table)
        table = jnp.where(lane == 2 * n + 1, rest, table)
    return table.T


FRESH_ROWS = 24


def fresh_kernel(u_ref, k_ref, v_ref, *refs):
    queries, (out_ref, rows_ref) = refs[0:4], refs[4:6]
    lses = []
    for s in range(B):
        rows = slice(s * TOK, (s + 1) * TOK)
        for k in range(LOCAL_HEADS):
            head = lax.rem(u_ref[0] + k, 4) if k < 4 else 4
            cols = pl.ds(pl.multiple_of(head * HD, HD), HD)
            query = queries[k][s, 0] if k < 4 else queries[0][s, 1]
            scores = scores_of(query, k_ref[rows, cols])
            top = jnp.max(scores, axis=1, keepdims=True)
            probs = jnp.exp2((scores - top) * SCORE_SCALE)
            total = jnp.sum(probs, axis=1, keepdims=True)
            out = jnp.dot(probs.astype(BF16), v_ref[rows, cols], preferred_element_type=F32)
            out_ref[s, k] = out / total
            lses.append(jnp.broadcast_to(top * SCORE_SCALE + jnp.log2(total), (TOK, HD)))
    rows_ref[...] = to_rows(lses)[0:FRESH_ROWS]


def fresh_attention(u, key, value, queries):
    return pl.pallas_call(
        fresh_kernel,
        out_shape=[
            jax.ShapeDtypeStruct((B, LOCAL_HEADS, TOK, HD), F32),
            jax.ShapeDtypeStruct((FRESH_ROWS, HD), F32),
        ],
        in_specs=[smem()] + [vmem()] * 6,
        out_specs=[vmem()] * 2,
        compiler_params=params(VMEM_MIB),
        cost_estimate=pl.CostEstimate(flops=1000, bytes_accessed=1000, transcendentals=0),
        name="fresh_attention",
    )(u, key, value, *queries)


TILE = 2 * TOK
PER_PIECE = 4 * TOK
SPLIT = 768


def stale_kernel(far, count, *refs):
    queries = refs[0:4]
    pieces, rest = refs[4 : 4 + count], refs[4 + count :]
    keys_main, keys_last = count * PER_PIECE, count * TOK
    if far:
        near_out, near_lse = rest[0:2]
        msgs = rest[3:7]
    else:
        out_ref, lse_ref = rest[0:2]
    lse_s, acc_s, k_main, v_main, k_last, v_last, scores_s, probs_s = rest[-8:]

    jobs = [(s, e, tile) for s in range(B) for e in range(2) for tile in range(2)]

    def size(i):
        return keys_last if jobs[i][1] else keys_main

    def score_steps(i):
        s, e, tile = jobs[i]
        keys = k_last if e else k_main
        out = scores_s.at[i % 2]

        def arrive():
            v_main[s, :, HD:] = jnp.ones((keys_main, HD), BF16)
            v_last[s, :, HD:] = jnp.ones((keys_last, HD), BF16)
            for n, piece in enumerate(pieces):
                main = slice(n * PER_PIECE, (n + 1) * PER_PIECE)
                last = slice(n * TOK, (n + 1) * TOK)
                k_main[s, main] = piece[s, 0, 0:PER_PIECE]
                k_last[s, last] = piece[s, 0, PER_PIECE:PIECE]
                v_main[s, main, 0:HD] = piece[s, 1, 0:PER_PIECE]
                v_last[s, last, 0:HD] = piece[s, 1, PER_PIECE:PIECE]

        def step(at, end):
            query = jnp.concatenate([queries[2 * tile][s, e], queries[2 * tile + 1][s, e]], axis=0)
            out[:, at:end] = scores_of(query, keys[s, at:end])

        def hide():
            for n in range(2):
                r = 2 * tile + n
                rows = slice(n * TOK, (n + 1) * TOK)
                if e and r:
                    continue
                out[rows, r * TOK : (r + 1) * TOK] = jnp.full((TOK, TOK), MASKED, F32)

        steps = [] if i % 4 else [arrive]
        for at in range(0, size(i), SPLIT):
            steps.append(functools.partial(step, at, min(at + SPLIT, size(i))))
        return steps if far else steps + [hide]

    def softmax_steps(i, tops):
        def step(row):
            rows = slice(row, row + GROUP)
            part = scores_s[i % 2, rows, 0 : size(i)]
            top = jnp.max(part, axis=1, keepdims=True)
            probs = jnp.exp2((part - top) * SCORE_SCALE)
            tops.append(top)
            probs_s[i % 2, rows, 0 : size(i)] = probs.astype(BF16)

        return [functools.partial(step, row) for row in range(0, TILE, GROUP)]

    def product_steps(i, tops):
        s, e, tile = jobs[i]
        values = v_last if e else v_main

        def step(at, end):
            part = jnp.dot(
                probs_s[i % 2, :, at:end], values[s, at:end], preferred_element_type=F32
            )
            acc_s[...] = part if at == 0 else acc_s[...] + part

        def finish():
            top = jnp.concatenate(tops, axis=0)
            total = acc_s[:, HD:]
            out = acc_s[:, 0:HD] / total
            lse = top * SCORE_SCALE + jnp.log2(total)
            for n in range(2):
                r = 2 * tile + n
                half = slice(n * TOK, (n + 1) * TOK)
                if not far:
                    out_ref[s, r, e] = out[half]
                    lse_ref[s, r, e] = lse[half]
                    continue
                lse_near = near_lse[s, r, e]
                high = jnp.maximum(lse[half], lse_near)
                weight, weight_near = jnp.exp2(lse[half] - high), jnp.exp2(lse_near - high)
                both = weight + weight_near
                value = (out[half] * weight + near_out[s, r, e] * weight_near) / both
                lse_s[s, r, e] = high + jnp.log2(both)
                msgs[r][s, e * TOK : (e + 1) * TOK] = value.astype(BF16)

        steps = []
        for at in range(0, size(i), SPLIT):
            steps.append(functools.partial(step, at, min(at + SPLIT, size(i))))
        return steps + [finish]

    def weave(*lists):
        order = []
        for steps in lists:
            order += [((n + 0.5) / len(steps), step) for n, step in enumerate(steps)]
        for _, step in sorted(order, key=lambda entry: entry[0]):
            step()

    weave(score_steps(0))
    pending = None
    for i in range(len(jobs)):
        tops = []
        lists = [softmax_steps(i, tops)]
        if i + 1 < len(jobs):
            lists.append(score_steps(i + 1))
        if pending is not None:
            lists.append(pending)
        weave(*lists)
        pending = product_steps(i, tops)
    weave(pending)

    if far:
        order = [(r, s) for r in range(4) for s in range(B)]
        flat = to_rows([lse_s[s, r, e] for r, s in order for e in range(2)])
        for n, (r, s) in enumerate(order):
            part = flat[n * 4 : n * 4 + 4]
            high = part.astype(BF16).astype(F32)
            middle = (part - high).astype(BF16).astype(F32)
            low = part - high - middle
            stack = jnp.concatenate([high, middle, low, jnp.zeros((4, HD), F32)], axis=0)
            msgs[r][s, 2 * TOK : MSG_ROWS] = stack.astype(BF16)


def stale_attention(queries, pieces, near=None, after=None):
    far = near is not None
    args = [*queries, *pieces]
    count = len(pieces)
    keys_main, keys_last = count * PER_PIECE, count * TOK
    in_specs = [vmem()] * (4 + count)
    if far:
        args += [*near, after]
        in_specs += [vmem(), vmem(), pl.BlockSpec(memory_space=pl.ANY)]
        out_shape = [jax.ShapeDtypeStruct((B, MSG_ROWS, HD), BF16)] * 4
    else:
        out_shape = [jax.ShapeDtypeStruct((B, 4, 2, TOK, HD), F32)] * 2
    return pl.pallas_call(
        functools.partial(stale_kernel, far, count),
        out_shape=out_shape,
        in_specs=in_specs,
        out_specs=[vmem()] * len(out_shape),
        scratch_shapes=[
            pltpu.VMEM((B, 4, 2, TOK, HD), F32),
            pltpu.VMEM((TILE, 2 * HD), F32),
            pltpu.VMEM((B, keys_main, HD), BF16),
            pltpu.VMEM((B, keys_main, 2 * HD), BF16),
            pltpu.VMEM((B, keys_last, HD), BF16),
            pltpu.VMEM((B, keys_last, 2 * HD), BF16),
            pltpu.VMEM((2, TILE, keys_main), F32),
            pltpu.VMEM((2, TILE, keys_main), BF16),
        ],
        compiler_params=params(ATTENTION_MIB),
        cost_estimate=pl.CostEstimate(flops=1000, bytes_accessed=1000, transcendentals=0),
        name="far_attention" if far else "near_attention",
    )(*args)


def merge_kernel(u_ref, fresh_out, fresh_rows, *refs):
    msgs, out_ref = refs[0:4], refs[4]
    lses = {}
    for k in range(4):
        for s in range(B):
            stack = msgs[k][s, 2 * TOK : MSG_ROWS].astype(F32)
            lses[s, k] = stack[0:4] + stack[4:8] + stack[8:12]
    weights, jobs = [], []
    for s in range(B):
        for k in range(LOCAL_HEADS):
            at = (s * LOCAL_HEADS + k) * 2
            parts = [(None, fresh_rows[at : at + 2])]
            if k < 4:
                parts.append((k, lses[s, k][0:2]))
            else:
                parts += [(n, lses[s, n][2:4]) for n in range(4)]
            top = parts[0][1]
            for _, lse in parts[1:]:
                top = jnp.maximum(top, lse)
            raw = [jnp.exp2(lse - top) for _, lse in parts]
            total = sum(raw[1:], raw[0])
            jobs.append((s, k, [(source, len(weights) + n) for n, (source, _) in enumerate(parts)]))
            weights += [one / total for one in raw]
    filler = jnp.zeros((HD - 2 * len(weights), HD), F32)
    table = jnp.concatenate(weights + [filler], axis=0).T
    for s, k, parts in jobs:
        head = lax.rem(u_ref[0] + k, 4) if k < 4 else 4
        out = [None, None]
        for source, n in parts:
            for half, rows in enumerate((slice(0, HD), slice(HD, TOK))):
                if source is None:
                    value = fresh_out[s, k, rows]
                else:
                    at = 0 if k < 4 else TOK
                    value = msgs[source][s, at + rows.start : at + rows.stop].astype(F32)
                column = table[0 : rows.stop - rows.start, 2 * n + half : 2 * n + half + 1]
                term = value * column
                out[half] = term if out[half] is None else out[half] + term
        cols = pl.ds(pl.multiple_of(head * HD, HD), HD)
        out_ref[s, :, cols] = jnp.concatenate(out, axis=0).astype(BF16)


def merge(u, fresh_out, fresh_rows, msgs):
    return pl.pallas_call(
        merge_kernel,
        out_shape=jax.ShapeDtypeStruct((B, TOK, WIDTH), BF16),
        in_specs=[smem()] + [vmem()] * 6,
        out_specs=vmem(),
        compiler_params=params(VMEM_MIB),
        cost_estimate=pl.CostEstimate(
            flops=10 * ROWS * WIDTH, bytes_accessed=14 * ROWS * WIDTH, transcendentals=0
        ),
        name="merge",
    )(u, fresh_out, fresh_rows, *msgs)


def shards(
    hidden,
    mod_shift,
    mod_scale,
    w_query,
    w_key,
    w_value,
    q_gain,
    k_gain,
    token_place,
    stale_keys,
    stale_values,
):
    patch = lax.axis_index("patch")
    tp = lax.axis_index("tp")
    y = patch // (NX * NZ)
    x = (patch // NZ) % NX
    u = jnp.where(tp % 2 == 0, y, x).astype(jnp.int32).reshape(1)
    own_rows = hidden.reshape(ROWS, CHUNK)
    z_rows = swap_tp(own_rows, 1, 0)
    core_rows = swap_tp(own_rows, 0, 1)

    packed = pack_stale(u, stale_keys, stale_values)
    arrived = exchange_u(packed)
    near = assemble([*arrived, packed[4]])
    cond, cos, sin, mod, own_rows = tables(token_place, own_rows, mod_shift, mod_scale, near)
    near_one, near_three = swap_v(near, 1), swap_v(near, 3)
    far = swap_z_hi(near)

    z_rows, cond = lax.optimization_barrier((z_rows, cond))
    cross_rows = swap_tp(z_rows, 0, 1)
    near_two = swap_v(near_one, 3)
    blocks = jnp.stack([tp, tp ^ 1, tp ^ 2, tp ^ 3]).astype(jnp.int32)
    modded, query = modulate(blocks, [own_rows, core_rows, z_rows, cross_rows], cond, mod, w_query)
    key = jnp.dot(modded, w_key, preferred_element_type=F32)
    fresh_values = jnp.dot(modded, w_value, preferred_element_type=F32).astype(BF16)
    own_sq = sum_squares(query, key)
    near_three, own_sq = lax.optimization_barrier((near_three, own_sq))
    squares = [own_sq] + [swap_tp(own_sq, z, c) for z, c in ((1, 1), (1, 0), (0, 1))]
    near_two, fresh_values, *squares = lax.optimization_barrier((near_two, fresh_values, *squares))
    far_two = swap_z_hi(near_two)
    fresh_keys, *sends = norm_rope(u, query, key, squares, q_gain, k_gain, cos, sin)
    far, fresh_keys = lax.optimization_barrier((far, fresh_keys))
    far_one, far_three = swap_v(far, 1), swap_v(far, 3)
    queries = exchange_u(sends)
    fresh_out, fresh_rows = fresh_attention(u, fresh_keys, fresh_values, sends)

    partial = stale_attention(queries, [near, near_one, near_three, near_two, far])
    outs = stale_attention(
        queries, [far_one, far_three, far_two], near=partial, after=fresh_rows
    )
    returned = exchange_u(outs)
    attended = merge(u, fresh_out, fresh_rows, returned)
    return (
        attended,
        fresh_keys.reshape(B, TOK, WIDTH),
        fresh_values.reshape(B, TOK, WIDTH),
    )


def solution(mesh):
    in_specs = (
        P(None, "patch", "tp"),
        P(),
        P(),
        P(None, "tp"),
        P(None, "tp"),
        P(None, "tp"),
        P("tp"),
        P("tp"),
        P("patch"),
        P(None, "patch", "tp"),
        P(None, "patch", "tp"),
    )
    out_specs = (P(None, "patch", "tp"), P(None, "patch", "tp"), P(None, "patch", "tp"))
    return jax.shard_map(shards, mesh=mesh, in_specs=in_specs, out_specs=out_specs, check_vma=False)
```

```python
import functools
import math

import jax
import jax.numpy as jnp
import numpy as np
from jax import lax
from jax.experimental import pallas as pl
from jax.experimental.pallas import tpu as pltpu
from jax.sharding import PartitionSpec as P

D = 5120
HEADS = 20
HD = 128
FRAMES = 3
GRID_W = 48
EPS = 1e-06
MASKED = -1e30
NY, NX, NZ = 4, 4, 2
TP = 4
N_PATCH = NY * NX * NZ
TOK = 144
B = 2
ROWS = B * TOK
LOCAL_HEADS = 5
WIDTH = LOCAL_HEADS * HD
CHUNK = D // TP
STAT_LANES = 384
PIECE = 5 * TOK
MSG_ROWS = 2 * TOK + 16
SCORE_SCALE = math.log2(math.e) / math.sqrt(HD)
F32 = jnp.float32
BF16 = jnp.bfloat16
AXES = ("patch", "tp")
GROUP = 16
VMEM_MIB = 24
ATTENTION_MIB = 40
MODULATE_MIB = 42


def params(mib):
    return pltpu.CompilerParams(vmem_limit_bytes=mib * 1024 * 1024)


def vmem():
    return pl.BlockSpec(memory_space=pltpu.VMEM)


def smem():
    return pl.BlockSpec(memory_space=pltpu.SMEM)


def linear(u, v, z_hi, z_lo, core):
    y, x = (u, v) if core == 0 else (v, u)
    return ((y * NX + x) * NZ + z_hi) * TP + z_lo * 2 + core


def places():
    return [
        (u, v, h, l, c)
        for u in range(4)
        for v in range(4)
        for h in range(2)
        for l in range(2)
        for c in range(2)
    ]


def permute(value, move):
    return lax.ppermute(value, AXES, [(linear(*p), linear(*move(*p))) for p in places()])


def shift_u(value, k):
    return permute(value, lambda u, v, h, l, c: ((u + k) % 4, v, h, l, c))


def swap_v(value, mask):
    return permute(value, lambda u, v, h, l, c: (u, v ^ mask, h, l, c))


def exchange_u(values):
    came = {r: shift_u(values[4 - r], 4 - r) for r in (2, 1, 3)}
    return [values[0], came[1], came[2], came[3]]


def swap_z_hi(value):
    return permute(value, lambda u, v, h, l, c: (u, v, 1 - h, l, c))


def swap_tp(value, z, core):
    if core:
        return permute(value, lambda u, v, h, l, c: (v, u, h, l ^ z, 1 - c))
    return permute(value, lambda u, v, h, l, c: (u, v, h, l ^ z, c))


def frequencies():
    half_dim = HD // 2
    third_dim = half_dim // 3
    frame_pairs = half_dim - 2 * third_dim
    pair = np.arange(HD) // 2
    offset = np.where(
        pair < frame_pairs,
        pair,
        np.where(pair < frame_pairs + third_dim, pair - frame_pairs, pair - frame_pairs - third_dim),
    )
    width = np.where(pair < frame_pairs, 2 * frame_pairs, 2 * third_dim)
    return np.exp(-math.log(10000.0) * 2.0 * offset / width).astype(np.float32).reshape(1, HD)


def columns_to_rows(first, second):
    lane = lax.broadcasted_iota(jnp.int32, (ROWS, 128), 1)
    both = jnp.where(lane == 0, first, jnp.where(lane == 1, second, 0.0))
    padded = jnp.concatenate([both, jnp.zeros((STAT_LANES - ROWS, 128), F32)], axis=0)
    return padded.T[0:8]


def row_to_column(row):
    return jnp.broadcast_to(row, (128, STAT_LANES)).T[0:ROWS]


def pack_kernel(u_ref, key_ref, value_ref, *outs):
    for k in range(5):
        head = lax.rem(u_ref[0] + k, 4) if k < 4 else 4
        cols = pl.ds(pl.multiple_of(head * HD, HD), HD)
        for n, source in enumerate((key_ref, value_ref)):
            for s in range(B):
                outs[k][s, n] = source[s, :, cols]


def pack_stale(u, stale_keys, stale_values):
    return pl.pallas_call(
        pack_kernel,
        out_shape=[jax.ShapeDtypeStruct((B, 2, TOK, HD), BF16)] * 5,
        in_specs=[smem(), vmem(), vmem()],
        out_specs=[vmem()] * 5,
        compiler_params=params(VMEM_MIB),
        cost_estimate=pl.CostEstimate(
            flops=0, bytes_accessed=8 * ROWS * WIDTH, transcendentals=0
        ),
        name="pack_stale",
    )(u, stale_keys, stale_values)


def tables_kernel(place_hbm, freq, rows, shift, scale, after, *refs):
    cond, cos, sin, mod, rows_out, places_s, place_ref, sem = refs
    copy = pltpu.make_async_copy(place_hbm, place_ref, sem.at[0])
    copy.start()
    copy.wait()
    for row in range(TOK):
        places_s[row : row + 1] = jnp.full((1, HD), place_ref[row], jnp.int32)
    place = places_s[...]
    frame_tok = TOK * N_PATCH // FRAMES
    frame = jnp.where(place >= frame_tok, 1, 0) + jnp.where(place >= 2 * frame_tok, 1, 0)
    within = place - frame * frame_tok
    grid_row = ((within.astype(F32) + 0.5) * (1.0 / GRID_W)).astype(jnp.int32)
    grid_col = within - grid_row * GRID_W
    lane = lax.broadcasted_iota(jnp.int32, (TOK, HD), 1)
    third = 2 * (HD // 6)
    frame_lanes = HD - 2 * third
    position = jnp.where(
        lane < frame_lanes, frame, jnp.where(lane < frame_lanes + third, grid_row, grid_col)
    )
    angles = position.astype(F32) * freq[...]
    cos[...] = jnp.cos(angles)
    sine = jnp.sin(angles)
    sin[...] = jnp.where(lane % 2 == 0, -sine, sine)
    flag = jnp.where((frame == 0) | (frame == FRAMES - 1), 1.0, 0.0)
    cond[0:TOK] = flag
    cond[TOK:ROWS] = flag
    mod[0:2] = 1.0 + scale[...]
    mod[2:4] = shift[...]
    rows_out[...] = rows[...]


def tables(token_place, rows, shift, scale, after):
    table = jax.ShapeDtypeStruct((TOK, HD), F32)
    return pl.pallas_call(
        tables_kernel,
        out_shape=[
            jax.ShapeDtypeStruct((ROWS, HD), F32),
            table,
            table,
            jax.ShapeDtypeStruct((4, D), F32),
            jax.ShapeDtypeStruct((ROWS, CHUNK), BF16),
        ],
        in_specs=[pl.BlockSpec(memory_space=pltpu.HBM)]
        + [vmem()] * 4
        + [pl.BlockSpec(memory_space=pl.ANY)],
        out_specs=[vmem()] * 5,
        scratch_shapes=[
            pltpu.VMEM((TOK, HD), jnp.int32),
            pltpu.SMEM((TOK,), jnp.int32),
            pltpu.SemaphoreType.DMA((1,)),
        ],
        compiler_params=params(VMEM_MIB),
        cost_estimate=pl.CostEstimate(
            flops=100 * TOK * HD, bytes_accessed=1_000_000, transcendentals=0
        ),
        name="tables",
    )(token_place, jnp.asarray(frequencies()), rows, shift, scale, after)


def assemble_kernel(*refs):
    parts, out = refs[0:5], refs[5]
    for s in range(B):
        for n in range(2):
            for r in range(5):
                out[s, n, r * TOK : (r + 1) * TOK] = parts[r][s, n]


def assemble(parts):
    return pl.pallas_call(
        assemble_kernel,
        out_shape=jax.ShapeDtypeStruct((B, 2, PIECE, HD), BF16),
        in_specs=[vmem()] * 5,
        out_specs=vmem(),
        compiler_params=params(VMEM_MIB),
        cost_estimate=pl.CostEstimate(
            flops=0, bytes_accessed=16 * PIECE * HD, transcendentals=0
        ),
        name="assemble",
    )(*parts)


def lane_sum(parts):
    total = None
    for part in parts:
        for at in range(0, part.shape[1], HD):
            piece = part[:, at : at + HD]
            total = piece if total is None else total + piece
    return jnp.sum(total, axis=1, keepdims=True)


def modulate_kernel(t_ref, h0, h1, h2, h3, cond, mod, weight, out_ref, query_ref, *scratch):
    weight_s, modded_s, mean_s, rstd_s, sems = scratch
    chunks = (h0, h1, h2, h3)
    copies = []
    for c in range(TP):
        rows = pl.ds(pl.multiple_of(t_ref[c] * CHUNK, CHUNK), CHUNK)
        copies.append(pltpu.make_async_copy(weight.at[rows], weight_s.at[c], sems.at[c]))
        copies[c].start()
    for row in range(0, ROWS, GROUP):
        rows = slice(row, row + GROUP)
        lanes = [chunk[rows].astype(F32) for chunk in chunks]
        mean = lane_sum([(lanes[0] + lanes[1]) + (lanes[2] + lanes[3])]) * (1.0 / D)
        deviation = lane_sum([(part - mean) * (part - mean) for part in lanes])
        mean_s[rows] = jnp.broadcast_to(mean, (GROUP, HD))
        rstd_s[rows] = jnp.broadcast_to(lax.rsqrt(deviation * (1.0 / D) + EPS), (GROUP, HD))

    def product(c):
        copies[c].wait()
        part = jnp.dot(modded_s[c % 2], weight_s[c], preferred_element_type=F32)
        if c == 0:
            query_ref[...] = part
        else:
            query_ref[...] += part

    for c in range(TP):
        if c:
            product(c - 1)
        cols = pl.ds(pl.multiple_of(t_ref[c] * CHUNK, CHUNK), CHUNK)
        for row in range(0, ROWS, GROUP):
            rows = slice(row, row + GROUP)
            conditioned = cond[rows, 0:1] > 0.5
            gain = jnp.where(conditioned, mod[1:2, cols], mod[0:1, cols])
            bias = jnp.where(conditioned, mod[3:4, cols], mod[2:3, cols])
            normed = (chunks[c][rows].astype(F32) - mean_s[rows, 0:1]) * rstd_s[rows, 0:1]
            value = (normed * gain + bias).astype(BF16)
            modded_s[c % 2, rows] = value
            out_ref[rows, cols] = value
    product(TP - 1)


def modulate(blocks, chunks, cond, mod, weight):
    return pl.pallas_call(
        modulate_kernel,
        out_shape=[
            jax.ShapeDtypeStruct((ROWS, D), BF16),
            jax.ShapeDtypeStruct((ROWS, WIDTH), F32),
        ],
        in_specs=[smem()] + [vmem()] * 6 + [pl.BlockSpec(memory_space=pltpu.HBM)],
        out_specs=[vmem()] * 2,
        scratch_shapes=[
            pltpu.VMEM((TP, CHUNK, WIDTH), BF16),
            pltpu.VMEM((2, ROWS, CHUNK), BF16),
            pltpu.VMEM((ROWS, HD), F32),
            pltpu.VMEM((ROWS, HD), F32),
            pltpu.SemaphoreType.DMA((TP,)),
        ],
        compiler_params=params(MODULATE_MIB),
        cost_estimate=pl.CostEstimate(flops=1000, bytes_accessed=30_000_000, transcendentals=0),
        name="modulate",
    )(blocks, *chunks, cond, mod, weight)


def squares_kernel(q_ref, k_ref, out_ref):
    query, key = q_ref[...], k_ref[...]
    out_ref[...] = columns_to_rows(
        jnp.sum(query * query, axis=1, keepdims=True),
        jnp.sum(key * key, axis=1, keepdims=True),
    )


def sum_squares(query, key):
    return pl.pallas_call(
        squares_kernel,
        out_shape=jax.ShapeDtypeStruct((8, STAT_LANES), F32),
        in_specs=[vmem()] * 2,
        out_specs=vmem(),
        compiler_params=params(VMEM_MIB),
        cost_estimate=pl.CostEstimate(
            flops=4 * ROWS * WIDTH, bytes_accessed=8 * ROWS * WIDTH, transcendentals=0
        ),
        name="sum_squares",
    )(query, key)


def rope_kernel(u_ref, q_ref, k_ref, s0, s1, s2, s3, qg, kg, cos, sin, k_all, *refs):
    sends, q_rot = refs[0:4], refs[4]
    total = s0[...] + s1[...] + s2[...] + s3[...]
    inverse = lax.rsqrt(total * (1.0 / (HEADS * HD)) + EPS)
    even = lax.broadcasted_iota(jnp.int32, (ROWS, HD), 1) % 2 == 0
    cos_rows = jnp.concatenate([cos[...], cos[...]], axis=0)
    sin_rows = jnp.concatenate([sin[...], sin[...]], axis=0)

    def rotate(ref, column, gain, cols):
        part = ref[:, cols] * column * gain[cols].reshape(1, HD)
        swap = jnp.where(even, pltpu.roll(part, HD - 1, 1), pltpu.roll(part, 1, 1))
        return (part * cos_rows + swap * sin_rows).astype(BF16)

    q_column = row_to_column(inverse[0:1])
    k_column = row_to_column(inverse[1:2])
    for head in range(LOCAL_HEADS):
        cols = slice(head * HD, (head + 1) * HD)
        query = rotate(q_ref, q_column, qg, cols)
        for s in range(B):
            q_rot[head, s] = query[s * TOK : (s + 1) * TOK]
        k_all[:, cols] = rotate(k_ref, k_column, kg, cols)
    for k in range(4):
        for s in range(B):
            sends[k][s, 0] = q_rot[lax.rem(u_ref[0] + k, 4), s]
            sends[k][s, 1] = q_rot[4, s]


def norm_rope(u, query, key, squares, q_gain, k_gain, cos, sin):
    send = jax.ShapeDtypeStruct((B, 2, TOK, HD), BF16)
    flat = jax.ShapeDtypeStruct((ROWS, WIDTH), BF16)
    return pl.pallas_call(
        rope_kernel,
        out_shape=[flat] + [send] * 4,
        in_specs=[smem()] + [vmem()] * 10,
        out_specs=[vmem()] * 5,
        scratch_shapes=[pltpu.VMEM((LOCAL_HEADS, B, TOK, HD), BF16)],
        compiler_params=params(VMEM_MIB),
        cost_estimate=pl.CostEstimate(flops=1000, bytes_accessed=1000, transcendentals=0),
        name="norm_rope",
    )(u, query, key, *squares, q_gain, k_gain, cos, sin)


def scores_of(query, keys):
    return lax.dot_general(query, keys, (((1,), (1,)), ((), ())), preferred_element_type=F32)


def to_rows(blocks):
    lane = lax.broadcasted_iota(jnp.int32, (HD, HD), 1)
    table = jnp.zeros((HD, HD), F32)
    empty = jnp.zeros((2 * HD - TOK, HD), F32)
    for n, block in enumerate(blocks):
        rest = jnp.concatenate([block[HD:TOK], empty], axis=0)
        table = jnp.where(lane == 2 * n, block[0:HD], table)
        table = jnp.where(lane == 2 * n + 1, rest, table)
    return table.T


FRESH_ROWS = 24


def fresh_kernel(u_ref, k_ref, v_ref, *refs):
    queries, (out_ref, rows_ref) = refs[0:4], refs[4:6]
    lses = []
    for s in range(B):
        rows = slice(s * TOK, (s + 1) * TOK)
        for k in range(LOCAL_HEADS):
            head = lax.rem(u_ref[0] + k, 4) if k < 4 else 4
            cols = pl.ds(pl.multiple_of(head * HD, HD), HD)
            query = queries[k][s, 0] if k < 4 else queries[0][s, 1]
            scores = scores_of(query, k_ref[rows, cols])
            top = jnp.max(scores, axis=1, keepdims=True)
            probs = jnp.exp2((scores - top) * SCORE_SCALE)
            total = jnp.sum(probs, axis=1, keepdims=True)
            out = jnp.dot(probs.astype(BF16), v_ref[rows, cols], preferred_element_type=F32)
            out_ref[s, k] = out / total
            lses.append(jnp.broadcast_to(top * SCORE_SCALE + jnp.log2(total), (TOK, HD)))
    rows_ref[...] = to_rows(lses)[0:FRESH_ROWS]


def fresh_attention(u, key, value, queries):
    return pl.pallas_call(
        fresh_kernel,
        out_shape=[
            jax.ShapeDtypeStruct((B, LOCAL_HEADS, TOK, HD), F32),
            jax.ShapeDtypeStruct((FRESH_ROWS, HD), F32),
        ],
        in_specs=[smem()] + [vmem()] * 6,
        out_specs=[vmem()] * 2,
        compiler_params=params(VMEM_MIB),
        cost_estimate=pl.CostEstimate(flops=1000, bytes_accessed=1000, transcendentals=0),
        name="fresh_attention",
    )(u, key, value, *queries)


TILE = 2 * TOK
PER_PIECE = 4 * TOK
SPLIT = 768


def stale_kernel(far, count, *refs):
    queries = refs[0:4]
    pieces, rest = refs[4 : 4 + count], refs[4 + count :]
    keys_main, keys_last = count * PER_PIECE, count * TOK
    if far:
        near_out, near_lse = rest[0:2]
        msgs = rest[3:7]
    else:
        out_ref, lse_ref = rest[0:2]
    lse_s, acc_s, k_main, v_main, k_last, v_last, scores_s, probs_s = rest[-8:]

    jobs = [(s, e, tile) for s in range(B) for e in range(2) for tile in range(2)]

    def size(i):
        return keys_last if jobs[i][1] else keys_main

    def score_steps(i):
        s, e, tile = jobs[i]
        keys = k_last if e else k_main
        out = scores_s.at[i % 2]

        def arrive():
            v_main[s, :, HD:] = jnp.ones((keys_main, HD), BF16)
            v_last[s, :, HD:] = jnp.ones((keys_last, HD), BF16)
            for n, piece in enumerate(pieces):
                main = slice(n * PER_PIECE, (n + 1) * PER_PIECE)
                last = slice(n * TOK, (n + 1) * TOK)
                k_main[s, main] = piece[s, 0, 0:PER_PIECE]
                k_last[s, last] = piece[s, 0, PER_PIECE:PIECE]
                v_main[s, main, 0:HD] = piece[s, 1, 0:PER_PIECE]
                v_last[s, last, 0:HD] = piece[s, 1, PER_PIECE:PIECE]

        def step(at, end):
            query = jnp.concatenate([queries[2 * tile][s, e], queries[2 * tile + 1][s, e]], axis=0)
            out[:, at:end] = scores_of(query, keys[s, at:end])

        def hide():
            for n in range(2):
                r = 2 * tile + n
                rows = slice(n * TOK, (n + 1) * TOK)
                if e and r:
                    continue
                out[rows, r * TOK : (r + 1) * TOK] = jnp.full((TOK, TOK), MASKED, F32)

        steps = [] if i % 4 else [arrive]
        for at in range(0, size(i), SPLIT):
            steps.append(functools.partial(step, at, min(at + SPLIT, size(i))))
        return steps if far else steps + [hide]

    def softmax_steps(i, tops):
        def step(row):
            rows = slice(row, row + GROUP)
            part = scores_s[i % 2, rows, 0 : size(i)]
            top = jnp.max(part, axis=1, keepdims=True)
            probs = jnp.exp2((part - top) * SCORE_SCALE)
            tops.append(top)
            probs_s[i % 2, rows, 0 : size(i)] = probs.astype(BF16)

        return [functools.partial(step, row) for row in range(0, TILE, GROUP)]

    def product_steps(i, tops):
        s, e, tile = jobs[i]
        values = v_last if e else v_main

        def step(at, end):
            part = jnp.dot(
                probs_s[i % 2, :, at:end], values[s, at:end], preferred_element_type=F32
            )
            acc_s[...] = part if at == 0 else acc_s[...] + part

        def finish():
            top = jnp.concatenate(tops, axis=0)
            total = acc_s[:, HD:]
            out = acc_s[:, 0:HD] / total
            lse = top * SCORE_SCALE + jnp.log2(total)
            for n in range(2):
                r = 2 * tile + n
                half = slice(n * TOK, (n + 1) * TOK)
                if not far:
                    out_ref[s, r, e] = out[half]
                    lse_ref[s, r, e] = lse[half]
                    continue
                lse_near = near_lse[s, r, e]
                high = jnp.maximum(lse[half], lse_near)
                weight, weight_near = jnp.exp2(lse[half] - high), jnp.exp2(lse_near - high)
                both = weight + weight_near
                value = (out[half] * weight + near_out[s, r, e] * weight_near) / both
                lse_s[s, r, e] = high + jnp.log2(both)
                msgs[r][s, e * TOK : (e + 1) * TOK] = value.astype(BF16)

        steps = []
        for at in range(0, size(i), SPLIT):
            steps.append(functools.partial(step, at, min(at + SPLIT, size(i))))
        return steps + [finish]

    def weave(*lists):
        order = []
        for steps in lists:
            order += [((n + 0.5) / len(steps), step) for n, step in enumerate(steps)]
        for _, step in sorted(order, key=lambda entry: entry[0]):
            step()

    weave(score_steps(0))
    pending = None
    for i in range(len(jobs)):
        tops = []
        lists = [softmax_steps(i, tops)]
        if i + 1 < len(jobs):
            lists.append(score_steps(i + 1))
        if pending is not None:
            lists.append(pending)
        weave(*lists)
        pending = product_steps(i, tops)
    weave(pending)

    if far:
        order = [(r, s) for r in range(4) for s in range(B)]
        flat = to_rows([lse_s[s, r, e] for r, s in order for e in range(2)])
        for n, (r, s) in enumerate(order):
            part = flat[n * 4 : n * 4 + 4]
            high = part.astype(BF16).astype(F32)
            middle = (part - high).astype(BF16).astype(F32)
            low = part - high - middle
            stack = jnp.concatenate([high, middle, low, jnp.zeros((4, HD), F32)], axis=0)
            msgs[r][s, 2 * TOK : MSG_ROWS] = stack.astype(BF16)


def stale_attention(queries, pieces, near=None, after=None):
    far = near is not None
    args = [*queries, *pieces]
    count = len(pieces)
    keys_main, keys_last = count * PER_PIECE, count * TOK
    in_specs = [vmem()] * (4 + count)
    if far:
        args += [*near, after]
        in_specs += [vmem(), vmem(), pl.BlockSpec(memory_space=pl.ANY)]
        out_shape = [jax.ShapeDtypeStruct((B, MSG_ROWS, HD), BF16)] * 4
    else:
        out_shape = [jax.ShapeDtypeStruct((B, 4, 2, TOK, HD), F32)] * 2
    return pl.pallas_call(
        functools.partial(stale_kernel, far, count),
        out_shape=out_shape,
        in_specs=in_specs,
        out_specs=[vmem()] * len(out_shape),
        scratch_shapes=[
            pltpu.VMEM((B, 4, 2, TOK, HD), F32),
            pltpu.VMEM((TILE, 2 * HD), F32),
            pltpu.VMEM((B, keys_main, HD), BF16),
            pltpu.VMEM((B, keys_main, 2 * HD), BF16),
            pltpu.VMEM((B, keys_last, HD), BF16),
            pltpu.VMEM((B, keys_last, 2 * HD), BF16),
            pltpu.VMEM((2, TILE, keys_main), F32),
            pltpu.VMEM((2, TILE, keys_main), BF16),
        ],
        compiler_params=params(ATTENTION_MIB),
        cost_estimate=pl.CostEstimate(flops=1000, bytes_accessed=1000, transcendentals=0),
        name="far_attention" if far else "near_attention",
    )(*args)


def merge_kernel(u_ref, fresh_out, fresh_rows, *refs):
    msgs, out_ref = refs[0:4], refs[4]
    lses = {}
    for k in range(4):
        for s in range(B):
            stack = msgs[k][s, 2 * TOK : MSG_ROWS].astype(F32)
            lses[s, k] = stack[0:4] + stack[4:8] + stack[8:12]
    weights, jobs = [], []
    for s in range(B):
        for k in range(LOCAL_HEADS):
            at = (s * LOCAL_HEADS + k) * 2
            parts = [(None, fresh_rows[at : at + 2])]
            if k < 4:
                parts.append((k, lses[s, k][0:2]))
            else:
                parts += [(n, lses[s, n][2:4]) for n in range(4)]
            top = parts[0][1]
            for _, lse in parts[1:]:
                top = jnp.maximum(top, lse)
            raw = [jnp.exp2(lse - top) for _, lse in parts]
            total = sum(raw[1:], raw[0])
            jobs.append((s, k, [(source, len(weights) + n) for n, (source, _) in enumerate(parts)]))
            weights += [one / total for one in raw]
    filler = jnp.zeros((HD - 2 * len(weights), HD), F32)
    table = jnp.concatenate(weights + [filler], axis=0).T
    for s, k, parts in jobs:
        head = lax.rem(u_ref[0] + k, 4) if k < 4 else 4
        out = [None, None]
        for source, n in parts:
            for half, rows in enumerate((slice(0, HD), slice(HD, TOK))):
                if source is None:
                    value = fresh_out[s, k, rows]
                else:
                    at = 0 if k < 4 else TOK
                    value = msgs[source][s, at + rows.start : at + rows.stop].astype(F32)
                column = table[0 : rows.stop - rows.start, 2 * n + half : 2 * n + half + 1]
                term = value * column
                out[half] = term if out[half] is None else out[half] + term
        cols = pl.ds(pl.multiple_of(head * HD, HD), HD)
        out_ref[s, :, cols] = jnp.concatenate(out, axis=0).astype(BF16)


def merge(u, fresh_out, fresh_rows, msgs):
    return pl.pallas_call(
        merge_kernel,
        out_shape=jax.ShapeDtypeStruct((B, TOK, WIDTH), BF16),
        in_specs=[smem()] + [vmem()] * 6,
        out_specs=vmem(),
        compiler_params=params(VMEM_MIB),
        cost_estimate=pl.CostEstimate(
            flops=10 * ROWS * WIDTH, bytes_accessed=14 * ROWS * WIDTH, transcendentals=0
        ),
        name="merge",
    )(u, fresh_out, fresh_rows, *msgs)


def shards(
    hidden,
    mod_shift,
    mod_scale,
    w_query,
    w_key,
    w_value,
    q_gain,
    k_gain,
    token_place,
    stale_keys,
    stale_values,
):
    patch = lax.axis_index("patch")
    tp = lax.axis_index("tp")
    y = patch // (NX * NZ)
    x = (patch // NZ) % NX
    u = jnp.where(tp % 2 == 0, y, x).astype(jnp.int32).reshape(1)
    own_rows = hidden.reshape(ROWS, CHUNK)
    z_rows = swap_tp(own_rows, 1, 0)
    core_rows = swap_tp(own_rows, 0, 1)

    packed = pack_stale(u, stale_keys, stale_values)
    arrived = exchange_u(packed)
    near = assemble([*arrived, packed[4]])
    cond, cos, sin, mod, own_rows = tables(token_place, own_rows, mod_shift, mod_scale, near)
    near_one, near_three = swap_v(near, 1), swap_v(near, 3)
    far = swap_z_hi(near)

    z_rows, cond = lax.optimization_barrier((z_rows, cond))
    cross_rows = swap_tp(z_rows, 0, 1)
    blocks = jnp.stack([tp, tp ^ 1, tp ^ 2, tp ^ 3]).astype(jnp.int32)
    modded, query = modulate(blocks, [own_rows, core_rows, z_rows, cross_rows], cond, mod, w_query)
    key = jnp.dot(modded, w_key, preferred_element_type=F32)
    near_one, near_three, key = lax.optimization_barrier((near_one, near_three, key))
    near_two = swap_v(near_one, 3)
    fresh_values = jnp.dot(modded, w_value, preferred_element_type=F32).astype(BF16)
    own_sq = sum_squares(query, key)
    squares = [own_sq] + [swap_tp(own_sq, z, c) for z, c in ((1, 1), (1, 0), (0, 1))]
    fresh_values, *squares = lax.optimization_barrier((fresh_values, *squares))
    fresh_keys, *sends = norm_rope(u, query, key, squares, q_gain, k_gain, cos, sin)
    far, fresh_keys = lax.optimization_barrier((far, fresh_keys))
    far_one, far_three = swap_v(far, 1), swap_v(far, 3)
    queries = exchange_u(sends)
    fresh_out, fresh_rows = fresh_attention(u, fresh_keys, fresh_values, sends)

    near_two, fresh_rows = lax.optimization_barrier((near_two, fresh_rows))
    far_two = swap_z_hi(near_two)
    partial = stale_attention(queries, [near, near_one, near_three, near_two, far, far_one, far_three])
    outs = stale_attention(
        queries, [far_two], near=partial, after=fresh_rows
    )
    returned = exchange_u(outs)
    attended = merge(u, fresh_out, fresh_rows, returned)
    return (
        attended,
        fresh_keys.reshape(B, TOK, WIDTH),
        fresh_values.reshape(B, TOK, WIDTH),
    )


def solution(mesh):
    in_specs = (
        P(None, "patch", "tp"),
        P(),
        P(),
        P(None, "tp"),
        P(None, "tp"),
        P(None, "tp"),
        P("tp"),
        P("tp"),
        P("patch"),
        P(None, "patch", "tp"),
        P(None, "patch", "tp"),
    )
    out_specs = (P(None, "patch", "tp"), P(None, "patch", "tp"), P(None, "patch", "tp"))
    return jax.shard_map(shards, mesh=mesh, in_specs=in_specs, out_specs=out_specs, check_vma=False)
```

```python
import functools
import math

import jax
import jax.numpy as jnp
import numpy as np
from jax import lax
from jax.experimental import pallas as pl
from jax.experimental.pallas import tpu as pltpu
from jax.sharding import PartitionSpec as P

D = 5120
HEADS = 20
HD = 128
FRAMES = 3
GRID_W = 48
EPS = 1e-06
MASKED = -1e30
NY, NX, NZ = 4, 4, 2
TP = 4
N_PATCH = NY * NX * NZ
TOK = 144
B = 2
ROWS = B * TOK
LOCAL_HEADS = 5
WIDTH = LOCAL_HEADS * HD
CHUNK = D // TP
STAT_LANES = 384
PIECE = 5 * TOK
MSG_ROWS = 2 * TOK + 16
SCORE_SCALE = math.log2(math.e) / math.sqrt(HD)
F32 = jnp.float32
BF16 = jnp.bfloat16
AXES = ("patch", "tp")
GROUP = 16
VMEM_MIB = 24
ATTENTION_MIB = 34
MODULATE_MIB = 42


def params(mib):
    return pltpu.CompilerParams(vmem_limit_bytes=mib * 1024 * 1024)


def vmem():
    return pl.BlockSpec(memory_space=pltpu.VMEM)


def smem():
    return pl.BlockSpec(memory_space=pltpu.SMEM)


def linear(u, v, z_hi, z_lo, core):
    y, x = (u, v) if core == 0 else (v, u)
    return ((y * NX + x) * NZ + z_hi) * TP + z_lo * 2 + core


def places():
    return [
        (u, v, h, l, c)
        for u in range(4)
        for v in range(4)
        for h in range(2)
        for l in range(2)
        for c in range(2)
    ]


def permute(value, move):
    return lax.ppermute(value, AXES, [(linear(*p), linear(*move(*p))) for p in places()])


def shift_u(value, k):
    return permute(value, lambda u, v, h, l, c: ((u + k) % 4, v, h, l, c))


def swap_v(value, mask):
    return permute(value, lambda u, v, h, l, c: (u, v ^ mask, h, l, c))


def exchange_u(values):
    came = {r: shift_u(values[4 - r], 4 - r) for r in (2, 1, 3)}
    return [values[0], came[1], came[2], came[3]]


def swap_z_hi(value):
    return permute(value, lambda u, v, h, l, c: (u, v, 1 - h, l, c))


def swap_tp(value, z, core):
    if core:
        return permute(value, lambda u, v, h, l, c: (v, u, h, l ^ z, 1 - c))
    return permute(value, lambda u, v, h, l, c: (u, v, h, l ^ z, c))


def frequencies():
    half_dim = HD // 2
    third_dim = half_dim // 3
    frame_pairs = half_dim - 2 * third_dim
    pair = np.arange(HD) // 2
    offset = np.where(
        pair < frame_pairs,
        pair,
        np.where(pair < frame_pairs + third_dim, pair - frame_pairs, pair - frame_pairs - third_dim),
    )
    width = np.where(pair < frame_pairs, 2 * frame_pairs, 2 * third_dim)
    return np.exp(-math.log(10000.0) * 2.0 * offset / width).astype(np.float32).reshape(1, HD)


def columns_to_rows(first, second):
    lane = lax.broadcasted_iota(jnp.int32, (ROWS, 128), 1)
    both = jnp.where(lane == 0, first, jnp.where(lane == 1, second, 0.0))
    padded = jnp.concatenate([both, jnp.zeros((STAT_LANES - ROWS, 128), F32)], axis=0)
    return padded.T[0:8]


def row_to_column(row):
    return jnp.broadcast_to(row, (128, STAT_LANES)).T[0:ROWS]


def pack_kernel(u_ref, key_ref, value_ref, *outs):
    for k in range(5):
        head = lax.rem(u_ref[0] + k, 4) if k < 4 else 4
        cols = pl.ds(pl.multiple_of(head * HD, HD), HD)
        for n, source in enumerate((key_ref, value_ref)):
            for s in range(B):
                outs[k][s, n] = source[s, :, cols]


def pack_stale(u, stale_keys, stale_values):
    return pl.pallas_call(
        pack_kernel,
        out_shape=[jax.ShapeDtypeStruct((B, 2, TOK, HD), BF16)] * 5,
        in_specs=[smem(), vmem(), vmem()],
        out_specs=[vmem()] * 5,
        compiler_params=params(VMEM_MIB),
        cost_estimate=pl.CostEstimate(
            flops=0, bytes_accessed=8 * ROWS * WIDTH, transcendentals=0
        ),
        name="pack_stale",
    )(u, stale_keys, stale_values)


def tables_kernel(place_hbm, freq, rows, shift, scale, after, *refs):
    cond, cos, sin, mod, rows_out, places_s, place_ref, sem = refs
    copy = pltpu.make_async_copy(place_hbm, place_ref, sem.at[0])
    copy.start()
    copy.wait()
    for row in range(TOK):
        places_s[row : row + 1] = jnp.full((1, HD), place_ref[row], jnp.int32)
    place = places_s[...]
    frame_tok = TOK * N_PATCH // FRAMES
    frame = jnp.where(place >= frame_tok, 1, 0) + jnp.where(place >= 2 * frame_tok, 1, 0)
    within = place - frame * frame_tok
    grid_row = ((within.astype(F32) + 0.5) * (1.0 / GRID_W)).astype(jnp.int32)
    grid_col = within - grid_row * GRID_W
    lane = lax.broadcasted_iota(jnp.int32, (TOK, HD), 1)
    third = 2 * (HD // 6)
    frame_lanes = HD - 2 * third
    position = jnp.where(
        lane < frame_lanes, frame, jnp.where(lane < frame_lanes + third, grid_row, grid_col)
    )
    angles = position.astype(F32) * freq[...]
    cos[...] = jnp.cos(angles)
    sine = jnp.sin(angles)
    sin[...] = jnp.where(lane % 2 == 0, -sine, sine)
    flag = jnp.where((frame == 0) | (frame == FRAMES - 1), 1.0, 0.0)
    cond[0:TOK] = flag
    cond[TOK:ROWS] = flag
    mod[0:2] = 1.0 + scale[...]
    mod[2:4] = shift[...]
    rows_out[...] = rows[...]


def tables(token_place, rows, shift, scale, after):
    table = jax.ShapeDtypeStruct((TOK, HD), F32)
    return pl.pallas_call(
        tables_kernel,
        out_shape=[
            jax.ShapeDtypeStruct((ROWS, HD), F32),
            table,
            table,
            jax.ShapeDtypeStruct((4, D), F32),
            jax.ShapeDtypeStruct((ROWS, CHUNK), BF16),
        ],
        in_specs=[pl.BlockSpec(memory_space=pltpu.HBM)]
        + [vmem()] * 4
        + [pl.BlockSpec(memory_space=pl.ANY)],
        out_specs=[vmem()] * 5,
        scratch_shapes=[
            pltpu.VMEM((TOK, HD), jnp.int32),
            pltpu.SMEM((TOK,), jnp.int32),
            pltpu.SemaphoreType.DMA((1,)),
        ],
        compiler_params=params(VMEM_MIB),
        cost_estimate=pl.CostEstimate(
            flops=100 * TOK * HD, bytes_accessed=1_000_000, transcendentals=0
        ),
        name="tables",
    )(token_place, jnp.asarray(frequencies()), rows, shift, scale, after)


def assemble_kernel(*refs):
    parts, out = refs[0:5], refs[5]
    for s in range(B):
        for n in range(2):
            for r in range(5):
                out[s, n, r * TOK : (r + 1) * TOK] = parts[r][s, n]


def assemble(parts):
    return pl.pallas_call(
        assemble_kernel,
        out_shape=jax.ShapeDtypeStruct((B, 2, PIECE, HD), BF16),
        in_specs=[vmem()] * 5,
        out_specs=vmem(),
        compiler_params=params(VMEM_MIB),
        cost_estimate=pl.CostEstimate(
            flops=0, bytes_accessed=16 * PIECE * HD, transcendentals=0
        ),
        name="assemble",
    )(*parts)


def lane_sum(parts):
    total = None
    for part in parts:
        for at in range(0, part.shape[1], HD):
            piece = part[:, at : at + HD]
            total = piece if total is None else total + piece
    return jnp.sum(total, axis=1, keepdims=True)


def modulate_kernel(t_ref, h0, h1, h2, h3, cond, mod, weight, out_ref, query_ref, *scratch):
    weight_s, modded_s, mean_s, rstd_s, sems = scratch
    chunks = (h0, h1, h2, h3)
    copies = []
    for c in range(TP):
        rows = pl.ds(pl.multiple_of(t_ref[c] * CHUNK, CHUNK), CHUNK)
        copies.append(pltpu.make_async_copy(weight.at[rows], weight_s.at[c], sems.at[c]))
        copies[c].start()
    for row in range(0, ROWS, GROUP):
        rows = slice(row, row + GROUP)
        lanes = [chunk[rows].astype(F32) for chunk in chunks]
        mean = lane_sum([(lanes[0] + lanes[1]) + (lanes[2] + lanes[3])]) * (1.0 / D)
        deviation = lane_sum([(part - mean) * (part - mean) for part in lanes])
        mean_s[rows] = jnp.broadcast_to(mean, (GROUP, HD))
        rstd_s[rows] = jnp.broadcast_to(lax.rsqrt(deviation * (1.0 / D) + EPS), (GROUP, HD))

    def product(c):
        copies[c].wait()
        part = jnp.dot(modded_s[c % 2], weight_s[c], preferred_element_type=F32)
        if c == 0:
            query_ref[...] = part
        else:
            query_ref[...] += part

    for c in range(TP):
        if c:
            product(c - 1)
        cols = pl.ds(pl.multiple_of(t_ref[c] * CHUNK, CHUNK), CHUNK)
        for row in range(0, ROWS, GROUP):
            rows = slice(row, row + GROUP)
            conditioned = cond[rows, 0:1] > 0.5
            gain = jnp.where(conditioned, mod[1:2, cols], mod[0:1, cols])
            bias = jnp.where(conditioned, mod[3:4, cols], mod[2:3, cols])
            normed = (chunks[c][rows].astype(F32) - mean_s[rows, 0:1]) * rstd_s[rows, 0:1]
            value = (normed * gain + bias).astype(BF16)
            modded_s[c % 2, rows] = value
            out_ref[rows, cols] = value
    product(TP - 1)


def modulate(blocks, chunks, cond, mod, weight):
    return pl.pallas_call(
        modulate_kernel,
        out_shape=[
            jax.ShapeDtypeStruct((ROWS, D), BF16),
            jax.ShapeDtypeStruct((ROWS, WIDTH), F32),
        ],
        in_specs=[smem()] + [vmem()] * 6 + [pl.BlockSpec(memory_space=pltpu.HBM)],
        out_specs=[vmem()] * 2,
        scratch_shapes=[
            pltpu.VMEM((TP, CHUNK, WIDTH), BF16),
            pltpu.VMEM((2, ROWS, CHUNK), BF16),
            pltpu.VMEM((ROWS, HD), F32),
            pltpu.VMEM((ROWS, HD), F32),
            pltpu.SemaphoreType.DMA((TP,)),
        ],
        compiler_params=params(MODULATE_MIB),
        cost_estimate=pl.CostEstimate(flops=1000, bytes_accessed=30_000_000, transcendentals=0),
        name="modulate",
    )(blocks, *chunks, cond, mod, weight)


def squares_kernel(q_ref, k_ref, out_ref):
    query, key = q_ref[...], k_ref[...]
    out_ref[...] = columns_to_rows(
        jnp.sum(query * query, axis=1, keepdims=True),
        jnp.sum(key * key, axis=1, keepdims=True),
    )


def sum_squares(query, key):
    return pl.pallas_call(
        squares_kernel,
        out_shape=jax.ShapeDtypeStruct((8, STAT_LANES), F32),
        in_specs=[vmem()] * 2,
        out_specs=vmem(),
        compiler_params=params(VMEM_MIB),
        cost_estimate=pl.CostEstimate(
            flops=4 * ROWS * WIDTH, bytes_accessed=8 * ROWS * WIDTH, transcendentals=0
        ),
        name="sum_squares",
    )(query, key)


def rope_kernel(u_ref, q_ref, k_ref, s0, s1, s2, s3, qg, kg, cos, sin, k_all, *refs):
    sends, q_rot = refs[0:4], refs[4]
    total = s0[...] + s1[...] + s2[...] + s3[...]
    inverse = lax.rsqrt(total * (1.0 / (HEADS * HD)) + EPS)
    even = lax.broadcasted_iota(jnp.int32, (ROWS, HD), 1) % 2 == 0
    cos_rows = jnp.concatenate([cos[...], cos[...]], axis=0)
    sin_rows = jnp.concatenate([sin[...], sin[...]], axis=0)

    def rotate(ref, column, gain, cols):
        part = ref[:, cols] * column * gain[cols].reshape(1, HD)
        swap = jnp.where(even, pltpu.roll(part, HD - 1, 1), pltpu.roll(part, 1, 1))
        return (part * cos_rows + swap * sin_rows).astype(BF16)

    q_column = row_to_column(inverse[0:1])
    k_column = row_to_column(inverse[1:2])
    for head in range(LOCAL_HEADS):
        cols = slice(head * HD, (head + 1) * HD)
        query = rotate(q_ref, q_column, qg, cols)
        for s in range(B):
            q_rot[head, s] = query[s * TOK : (s + 1) * TOK]
        k_all[:, cols] = rotate(k_ref, k_column, kg, cols)
    for k in range(4):
        for s in range(B):
            sends[k][s, 0] = q_rot[lax.rem(u_ref[0] + k, 4), s]
            sends[k][s, 1] = q_rot[4, s]


def norm_rope(u, query, key, squares, q_gain, k_gain, cos, sin):
    send = jax.ShapeDtypeStruct((B, 2, TOK, HD), BF16)
    flat = jax.ShapeDtypeStruct((ROWS, WIDTH), BF16)
    return pl.pallas_call(
        rope_kernel,
        out_shape=[flat] + [send] * 4,
        in_specs=[smem()] + [vmem()] * 10,
        out_specs=[vmem()] * 5,
        scratch_shapes=[pltpu.VMEM((LOCAL_HEADS, B, TOK, HD), BF16)],
        compiler_params=params(VMEM_MIB),
        cost_estimate=pl.CostEstimate(flops=1000, bytes_accessed=1000, transcendentals=0),
        name="norm_rope",
    )(u, query, key, *squares, q_gain, k_gain, cos, sin)


def scores_of(query, keys):
    return lax.dot_general(query, keys, (((1,), (1,)), ((), ())), preferred_element_type=F32)


def to_rows(blocks):
    lane = lax.broadcasted_iota(jnp.int32, (HD, HD), 1)
    table = jnp.zeros((HD, HD), F32)
    empty = jnp.zeros((2 * HD - TOK, HD), F32)
    for n, block in enumerate(blocks):
        rest = jnp.concatenate([block[HD:TOK], empty], axis=0)
        table = jnp.where(lane == 2 * n, block[0:HD], table)
        table = jnp.where(lane == 2 * n + 1, rest, table)
    return table.T


FRESH_ROWS = 24


def fresh_kernel(u_ref, k_ref, v_ref, *refs):
    queries, (out_ref, rows_ref) = refs[0:4], refs[4:6]
    lses = []
    for s in range(B):
        rows = slice(s * TOK, (s + 1) * TOK)
        for k in range(LOCAL_HEADS):
            head = lax.rem(u_ref[0] + k, 4) if k < 4 else 4
            cols = pl.ds(pl.multiple_of(head * HD, HD), HD)
            query = queries[k][s, 0] if k < 4 else queries[0][s, 1]
            scores = scores_of(query, k_ref[rows, cols])
            top = jnp.max(scores, axis=1, keepdims=True)
            probs = jnp.exp2((scores - top) * SCORE_SCALE)
            total = jnp.sum(probs, axis=1, keepdims=True)
            out = jnp.dot(probs.astype(BF16), v_ref[rows, cols], preferred_element_type=F32)
            out_ref[s, k] = out / total
            lses.append(jnp.broadcast_to(top * SCORE_SCALE + jnp.log2(total), (TOK, HD)))
    rows_ref[...] = to_rows(lses)[0:FRESH_ROWS]


def fresh_attention(u, key, value, queries):
    return pl.pallas_call(
        fresh_kernel,
        out_shape=[
            jax.ShapeDtypeStruct((B, LOCAL_HEADS, TOK, HD), F32),
            jax.ShapeDtypeStruct((FRESH_ROWS, HD), F32),
        ],
        in_specs=[smem()] + [vmem()] * 6,
        out_specs=[vmem()] * 2,
        compiler_params=params(VMEM_MIB),
        cost_estimate=pl.CostEstimate(flops=1000, bytes_accessed=1000, transcendentals=0),
        name="fresh_attention",
    )(u, key, value, *queries)


TILE = 2 * TOK
PER_PIECE = 4 * TOK
SPLIT = 768


def stale_kernel(far, count, *refs):
    queries = refs[0:4]
    pieces, rest = refs[4 : 4 + count], refs[4 + count :]
    keys_main, keys_last = count * PER_PIECE, count * TOK
    if far:
        near_out, near_lse = rest[0:2]
        msgs = rest[3:7]
    else:
        out_ref, lse_ref = rest[0:2]
    lse_s, acc_s, k_main, v_main, k_last, v_last, scores_s, probs_s = rest[-8:]

    jobs = [(s, e, tile) for s in range(B) for e in range(2) for tile in range(2)]

    def size(i):
        return keys_last if jobs[i][1] else keys_main

    def score_steps(i):
        s, e, tile = jobs[i]
        keys = k_last if e else k_main
        out = scores_s.at[i % 2]

        def arrive():
            v_main[s, :, HD:] = jnp.ones((keys_main, HD), BF16)
            v_last[s, :, HD:] = jnp.ones((keys_last, HD), BF16)
            for n, piece in enumerate(pieces):
                main = slice(n * PER_PIECE, (n + 1) * PER_PIECE)
                last = slice(n * TOK, (n + 1) * TOK)
                k_main[s, main] = piece[s, 0, 0:PER_PIECE]
                k_last[s, last] = piece[s, 0, PER_PIECE:PIECE]
                v_main[s, main, 0:HD] = piece[s, 1, 0:PER_PIECE]
                v_last[s, last, 0:HD] = piece[s, 1, PER_PIECE:PIECE]

        def step(at, end):
            query = jnp.concatenate([queries[2 * tile][s, e], queries[2 * tile + 1][s, e]], axis=0)
            out[:, at:end] = scores_of(query, keys[s, at:end])

        def hide():
            for n in range(2):
                r = 2 * tile + n
                rows = slice(n * TOK, (n + 1) * TOK)
                if e and r:
                    continue
                out[rows, r * TOK : (r + 1) * TOK] = jnp.full((TOK, TOK), MASKED, F32)

        steps = [] if i % 4 else [arrive]
        for at in range(0, size(i), SPLIT):
            steps.append(functools.partial(step, at, min(at + SPLIT, size(i))))
        return steps if far else steps + [hide]

    def softmax_steps(i, tops):
        def step(row):
            rows = slice(row, row + GROUP)
            part = scores_s[i % 2, rows, 0 : size(i)]
            top = jnp.max(part, axis=1, keepdims=True)
            probs = jnp.exp2((part - top) * SCORE_SCALE)
            tops.append(top)
            probs_s[i % 2, rows, 0 : size(i)] = probs.astype(BF16)

        return [functools.partial(step, row) for row in range(0, TILE, GROUP)]

    def product_steps(i, tops):
        s, e, tile = jobs[i]
        values = v_last if e else v_main

        def step(at, end):
            part = jnp.dot(
                probs_s[i % 2, :, at:end], values[s, at:end], preferred_element_type=F32
            )
            acc_s[...] = part if at == 0 else acc_s[...] + part

        def finish():
            top = jnp.concatenate(tops, axis=0)
            total = acc_s[:, HD:]
            out = acc_s[:, 0:HD] / total
            lse = top * SCORE_SCALE + jnp.log2(total)
            for n in range(2):
                r = 2 * tile + n
                half = slice(n * TOK, (n + 1) * TOK)
                if not far:
                    out_ref[s, r, e] = out[half]
                    lse_ref[s, r, e] = lse[half]
                    continue
                lse_near = near_lse[s, r, e]
                high = jnp.maximum(lse[half], lse_near)
                weight, weight_near = jnp.exp2(lse[half] - high), jnp.exp2(lse_near - high)
                both = weight + weight_near
                value = (out[half] * weight + near_out[s, r, e] * weight_near) / both
                lse_s[s, r, e] = high + jnp.log2(both)
                msgs[r][s, e * TOK : (e + 1) * TOK] = value.astype(BF16)

        steps = []
        for at in range(0, size(i), SPLIT):
            steps.append(functools.partial(step, at, min(at + SPLIT, size(i))))
        return steps + [finish]

    def weave(*lists):
        order = []
        for steps in lists:
            order += [((n + 0.5) / len(steps), step) for n, step in enumerate(steps)]
        for _, step in sorted(order, key=lambda entry: entry[0]):
            step()

    weave(score_steps(0))
    pending = None
    for i in range(len(jobs)):
        tops = []
        lists = [softmax_steps(i, tops)]
        if i + 1 < len(jobs):
            lists.append(score_steps(i + 1))
        if pending is not None:
            lists.append(pending)
        weave(*lists)
        pending = product_steps(i, tops)
    weave(pending)

    if far:
        order = [(r, s) for r in range(4) for s in range(B)]
        flat = to_rows([lse_s[s, r, e] for r, s in order for e in range(2)])
        for n, (r, s) in enumerate(order):
            part = flat[n * 4 : n * 4 + 4]
            high = part.astype(BF16).astype(F32)
            middle = (part - high).astype(BF16).astype(F32)
            low = part - high - middle
            stack = jnp.concatenate([high, middle, low, jnp.zeros((4, HD), F32)], axis=0)
            msgs[r][s, 2 * TOK : MSG_ROWS] = stack.astype(BF16)


def stale_attention(queries, pieces, near=None, after=None):
    far = near is not None
    args = [*queries, *pieces]
    count = len(pieces)
    keys_main, keys_last = count * PER_PIECE, count * TOK
    in_specs = [vmem()] * (4 + count)
    if far:
        args += [*near, after]
        in_specs += [vmem(), vmem(), pl.BlockSpec(memory_space=pl.ANY)]
        out_shape = [jax.ShapeDtypeStruct((B, MSG_ROWS, HD), BF16)] * 4
    else:
        out_shape = [jax.ShapeDtypeStruct((B, 4, 2, TOK, HD), F32)] * 2
    return pl.pallas_call(
        functools.partial(stale_kernel, far, count),
        out_shape=out_shape,
        in_specs=in_specs,
        out_specs=[vmem()] * len(out_shape),
        scratch_shapes=[
            pltpu.VMEM((B, 4, 2, TOK, HD), F32),
            pltpu.VMEM((TILE, 2 * HD), F32),
            pltpu.VMEM((B, keys_main, HD), BF16),
            pltpu.VMEM((B, keys_main, 2 * HD), BF16),
            pltpu.VMEM((B, keys_last, HD), BF16),
            pltpu.VMEM((B, keys_last, 2 * HD), BF16),
            pltpu.VMEM((2, TILE, keys_main), F32),
            pltpu.VMEM((2, TILE, keys_main), BF16),
        ],
        compiler_params=params(ATTENTION_MIB),
        cost_estimate=pl.CostEstimate(flops=1000, bytes_accessed=1000, transcendentals=0),
        name="far_attention" if far else "near_attention",
    )(*args)


def merge_kernel(u_ref, fresh_out, fresh_rows, *refs):
    msgs, out_ref = refs[0:4], refs[4]
    lses = {}
    for k in range(4):
        for s in range(B):
            stack = msgs[k][s, 2 * TOK : MSG_ROWS].astype(F32)
            lses[s, k] = stack[0:4] + stack[4:8] + stack[8:12]
    weights, jobs = [], []
    for s in range(B):
        for k in range(LOCAL_HEADS):
            at = (s * LOCAL_HEADS + k) * 2
            parts = [(None, fresh_rows[at : at + 2])]
            if k < 4:
                parts.append((k, lses[s, k][0:2]))
            else:
                parts += [(n, lses[s, n][2:4]) for n in range(4)]
            top = parts[0][1]
            for _, lse in parts[1:]:
                top = jnp.maximum(top, lse)
            raw = [jnp.exp2(lse - top) for _, lse in parts]
            total = sum(raw[1:], raw[0])
            jobs.append((s, k, [(source, len(weights) + n) for n, (source, _) in enumerate(parts)]))
            weights += [one / total for one in raw]
    filler = jnp.zeros((HD - 2 * len(weights), HD), F32)
    table = jnp.concatenate(weights + [filler], axis=0).T
    for s, k, parts in jobs:
        head = lax.rem(u_ref[0] + k, 4) if k < 4 else 4
        out = [None, None]
        for source, n in parts:
            for half, rows in enumerate((slice(0, HD), slice(HD, TOK))):
                if source is None:
                    value = fresh_out[s, k, rows]
                else:
                    at = 0 if k < 4 else TOK
                    value = msgs[source][s, at + rows.start : at + rows.stop].astype(F32)
                column = table[0 : rows.stop - rows.start, 2 * n + half : 2 * n + half + 1]
                term = value * column
                out[half] = term if out[half] is None else out[half] + term
        cols = pl.ds(pl.multiple_of(head * HD, HD), HD)
        out_ref[s, :, cols] = jnp.concatenate(out, axis=0).astype(BF16)


def merge(u, fresh_out, fresh_rows, msgs):
    return pl.pallas_call(
        merge_kernel,
        out_shape=jax.ShapeDtypeStruct((B, TOK, WIDTH), BF16),
        in_specs=[smem()] + [vmem()] * 6,
        out_specs=vmem(),
        compiler_params=params(VMEM_MIB),
        cost_estimate=pl.CostEstimate(
            flops=10 * ROWS * WIDTH, bytes_accessed=14 * ROWS * WIDTH, transcendentals=0
        ),
        name="merge",
    )(u, fresh_out, fresh_rows, *msgs)


def shards(
    hidden,
    mod_shift,
    mod_scale,
    w_query,
    w_key,
    w_value,
    q_gain,
    k_gain,
    token_place,
    stale_keys,
    stale_values,
):
    patch = lax.axis_index("patch")
    tp = lax.axis_index("tp")
    y = patch // (NX * NZ)
    x = (patch // NZ) % NX
    u = jnp.where(tp % 2 == 0, y, x).astype(jnp.int32).reshape(1)
    own_rows = hidden.reshape(ROWS, CHUNK)
    z_rows = swap_tp(own_rows, 1, 0)
    core_rows = swap_tp(own_rows, 0, 1)

    packed = pack_stale(u, stale_keys, stale_values)
    arrived = exchange_u(packed)
    near = assemble([*arrived, packed[4]])
    cond, cos, sin, mod, own_rows = tables(token_place, own_rows, mod_shift, mod_scale, near)
    near_one, near_three = swap_v(near, 1), swap_v(near, 3)
    far = swap_z_hi(near)

    z_rows, cond = lax.optimization_barrier((z_rows, cond))
    cross_rows = swap_tp(z_rows, 0, 1)
    blocks = jnp.stack([tp, tp ^ 1, tp ^ 2, tp ^ 3]).astype(jnp.int32)
    modded, query = modulate(blocks, [own_rows, core_rows, z_rows, cross_rows], cond, mod, w_query)
    key = jnp.dot(modded, w_key, preferred_element_type=F32)
    near_one, near_three, key = lax.optimization_barrier((near_one, near_three, key))
    near_two = swap_v(near_one, 3)
    fresh_values = jnp.dot(modded, w_value, preferred_element_type=F32).astype(BF16)
    own_sq = sum_squares(query, key)
    squares = [own_sq] + [swap_tp(own_sq, z, c) for z, c in ((1, 1), (1, 0), (0, 1))]
    fresh_values, *squares = lax.optimization_barrier((fresh_values, *squares))
    fresh_keys, *sends = norm_rope(u, query, key, squares, q_gain, k_gain, cos, sin)
    far, fresh_keys = lax.optimization_barrier((far, fresh_keys))
    far_one, far_three = swap_v(far, 1), swap_v(far, 3)
    near_two, sends[1] = lax.optimization_barrier((near_two, sends[1]))
    far_two = swap_z_hi(near_two)
    queries = exchange_u(sends)
    fresh_out, fresh_rows = fresh_attention(u, fresh_keys, fresh_values, sends)

    partial = stale_attention(queries, [near, near_one, near_three, near_two, far])
    outs = stale_attention(
        queries, [far_one, far_three, far_two], near=partial, after=fresh_rows
    )
    returned = exchange_u(outs)
    attended = merge(u, fresh_out, fresh_rows, returned)
    return (
        attended,
        fresh_keys.reshape(B, TOK, WIDTH),
        fresh_values.reshape(B, TOK, WIDTH),
    )


def solution(mesh):
    in_specs = (
        P(None, "patch", "tp"),
        P(),
        P(),
        P(None, "tp"),
        P(None, "tp"),
        P(None, "tp"),
        P("tp"),
        P("tp"),
        P("patch"),
        P(None, "patch", "tp"),
        P(None, "patch", "tp"),
    )
    out_specs = (P(None, "patch", "tp"), P(None, "patch", "tp"), P(None, "patch", "tp"))
    return jax.shard_map(shards, mesh=mesh, in_specs=in_specs, out_specs=out_specs, check_vma=False)
```
